32 devices in a mesh: section: 2 (over x), dp: 16 (over z, y, core).
Axes of the slice: x: 2, y: 2, z: 4, core: 2. Of those that a mesh axis runs over, the one named last changes fastest.
Arguments:
- tokens: bfloat16 [2, 16, 384, 768], P('section', 'dp'), may hold values from -6 to 6
- segments: int32 [2, 16, 384], P(None, 'dp'), may hold values from 0 to 6, as said below
- cotangent: bfloat16 [16, 384, 768], P('dp'), may hold values from -6 to 6
- attn_qk: bfloat16 [2, 768, 1536], P('section', 'dp'), may hold values from -0.21875 to 0.21875
- attn_vo: bfloat16 [2, 768, 1536], P('section', 'dp'), may hold values from -0.625 to 0.625
- cross_qk: bfloat16 [2, 768, 768], P('section', 'dp'), may hold values from -0.21875 to 0.21875
- cross_vo: bfloat16 [2, 768, 768], P('section', 'dp'), may hold values from -0.625 to 0.625
- ffn_in: bfloat16 [2, 768, 3072], P('section', 'dp'), may hold values from -0.21875 to 0.21875
- ffn_out: bfloat16 [2, 3072, 768], P('section', 'dp'), may hold values from -0.109375 to 0.109375
- gains: float32 [5, 768], replicated, may hold values from 0.5 to 1.5
- biases: float32 [16, 768], replicated, may hold values from -1.25 to 1.25
- ffn_bias: float32 [2, 3072], replicated, may hold values from -1.25 to 1.25
Outputs:
- layer_out: bfloat16 [2, 16, 384, 768], P('section', 'dp')
- input_grad: float32 [2, 16, 384, 768], P('section', 'dp')
- grad_attn_qk: float32 [2, 768, 1536], P('section', 'dp')
- grad_attn_vo: float32 [2, 768, 1536], P('section', 'dp')
- grad_cross_qk: float32 [2, 768, 768], P('section', 'dp')
- grad_cross_vo: float32 [2, 768, 768], P('section', 'dp')
- grad_ffn_in: float32 [2, 768, 3072], P('section', 'dp')
- grad_ffn_out: float32 [2, 3072, 768], P('section', 'dp')
- grad_gains: float32 [5, 768], replicated
- grad_biases: float32 [16, 768], replicated
- grad_ffn_bias: float32 [2, 3072], replicated
The draws below stay inside these ranges and needn't reach their ends.
Inputs may be any that keep to these rules, and one draw needn't show every extreme that they name: `segments`: in each row, ids 1 to n (2 <= n <= 6) fill runs of consecutive tokens in increasing order, followed by one or more padding tokens of id 0; the source row and the target row of the same index hold the same ids, with their own lengths; row 0 holds 6 documents.
All inputs are finite; a program needn't handle non-finite values.
Results may differ from the reference program's by a relative error of at most 0.025.
Values may be sent and summed in bfloat16 or wider, within the bound.
A program may use at most 192 MiB of HBM per device.

```python
import math
import jax
import jax.numpy as jnp
from jax import lax

D = 768
HEAD_DIM = 64
FF = 3072
SEQ = 384
MAXDOC = 6
ROWS = 16


def draw_segments(key, part):
    row_index = jnp.arange(ROWS)
    doc_count = jax.random.randint(jax.random.fold_in(key, 11), (ROWS,), 2, MAXDOC + 1)
    doc_count = jnp.where(row_index == 0, MAXDOC, doc_count)
    padding = jax.random.randint(jax.random.fold_in(key, 12), (2, ROWS), 1, SEQ // 8 + 1)
    valid_len = SEQ - padding
    cut_index = jnp.arange(1, MAXDOC)
    cut_base = cut_index[None, None, :] * valid_len[:, :, None] // doc_count[None, :, None]
    cut_reach = valid_len[:, :, None] // (4 * doc_count[None, :, None])
    cut_reach = jnp.broadcast_to(cut_reach, (2, ROWS, MAXDOC - 1))
    jitter = jax.random.randint(jax.random.fold_in(key, 13), (2, ROWS, MAXDOC - 1), -cut_reach, cut_reach + 1)
    cut_place = cut_base + jitter
    cut_live = cut_index[None, None, :] < doc_count[None, :, None]
    position = jnp.arange(SEQ)
    passed_cut = (position[None, None, :, None] >= cut_place[:, :, None, :]) & cut_live[:, :, None, :]
    segment_id = 1 + jnp.sum(passed_cut.astype(jnp.int32), axis=-1)
    return jnp.where(position[None, None, :] < valid_len[:, :, None], segment_id, 0).astype(jnp.int32)


def spiked(drawn, own_key, source, target, shards_of, factor):
    def block_of(axis_at):
        return (jnp.arange(drawn.shape[axis_at]) // (drawn.shape[axis_at] // shards_of)).reshape((-1,) + (1,) * (drawn.ndim - 1 - axis_at))

    near = jax.random.permutation(own_key, shards_of)[block_of(target)]
    other_side = (block_of(target) + shards_of // 2) % shards_of
    return jnp.where((block_of(source) == near) | (block_of(source) == other_side), factor * drawn, drawn)


def steps_of(key, extent, cuts, smallest, largest):
    def one(dim, shards_of):
        steps = jax.random.uniform(jax.random.fold_in(jax.random.fold_in(key, 6), dim), (shards_of,), jnp.float32, smallest / len(cuts), largest / len(cuts))
        return jnp.repeat(jnp.exp(steps), extent[dim] // shards_of).reshape((-1,) + (1,) * (len(extent) - dim - 1))

    level = one(*cuts[0])
    for cut in cuts[1:]:
        level = level * one(*cut)
    return level


def centred(rng, shape, scale, reach, shards=(), held_as=jnp.bfloat16):
    values = scale * jax.random.normal(rng, shape, jnp.float32)
    if shards:
        values = values * steps_of(rng, shape, shards, -0.22, 0.18)
    return jnp.clip(values, -reach, reach).astype(held_as)


def gaussian_with(rng, shape, scale, limit, cuts, heavy, held_as=jnp.bfloat16):
    values = scale * jax.random.normal(rng, shape, jnp.float32)
    if cuts:
        values = values * steps_of(rng, shape, cuts, -0.22, 0.18)
    return jnp.clip(spiked(values, jax.random.fold_in(rng, 3), *heavy), -limit, limit).astype(held_as)


def setup_inputs(seed: int = 0) -> dict:
    arg_keys = jax.random.split(jax.random.key(seed), 13)
    tokens = gaussian_with(arg_keys[0], (2, ROWS, SEQ, D), 1.0, 6.0, ((0, 2), (1, 16)), (1, 3, 16, 2.0))
    segments = draw_segments(jax.random.fold_in(arg_keys[12], 71), 0)
    cotangent = centred(arg_keys[2], (ROWS, SEQ, D), 1.0, 6.0, ((0, 16),))
    attn_qk = centred(arg_keys[3], (2, D, 2 * D), D ** -0.5, 0.21875, ((0, 2), (1, 16)))
    attn_vo = centred(arg_keys[4], (2, D, 2 * D), (D // 10) ** -0.5, 0.625, ((0, 2), (1, 16)))
    cross_qk = centred(arg_keys[5], (2, D, D), D ** -0.5, 0.21875, ((0, 2), (1, 16)))
    cross_vo = centred(arg_keys[6], (2, D, D), (D // 10) ** -0.5, 0.625, ((0, 2), (1, 16)))
    ffn_in = centred(arg_keys[7], (2, D, FF), D ** -0.5, 0.21875, ((0, 2), (1, 16)))
    ffn_out = centred(arg_keys[8], (2, FF, D), FF ** -0.5, 0.109375, ((0, 2), (1, 16)))
    gains = jnp.clip(1.0 + 0.1 * jax.random.normal(arg_keys[9], (5, D), jnp.float32), 0.5, 1.5)
    biases = centred(arg_keys[10], (16, D), 0.2, 1.25, (), jnp.float32)
    ffn_bias = centred(arg_keys[11], (2, FF), 0.2, 1.25, (), jnp.float32)
    return {"tokens": tokens, "segments": segments, "cotangent": cotangent, "attn_qk": attn_qk, "attn_vo": attn_vo, "cross_qk": cross_qk, "cross_vo": cross_vo, "ffn_in": ffn_in, "ffn_out": ffn_out, "gains": gains, "biases": biases, "ffn_bias": ffn_bias}


@jax.custom_vjp
def low(v):
    return lax.optimization_barrier(v.astype(jnp.bfloat16)).astype(jnp.float32)

@jax.custom_vjp
def low_back(v):
    return v

def low_keep(v):
    return (low(v), None)

def low_pass(kept, grad):
    return (grad,)

def back_keep(v):
    return (v, None)

def back_low(kept, grad):
    return (low(grad),)
low.defvjp(low_keep, low_pass)
low_back.defvjp(back_keep, back_low)

def matmul(left, right):
    return jnp.einsum('rld,de->rle', left, right, precision=lax.Precision.HIGHEST)

def round_both(value):
    return low_back(low(value))

def layer_norm(resid, gain, shift):
    center = resid - lax.optimization_barrier(jnp.mean(resid, axis=-1, keepdims=True))
    spread = lax.optimization_barrier(jnp.mean(center * center, axis=-1, keepdims=True))
    return center * lax.rsqrt(spread + 1e-05) * gain + shift

def attend(query, key_rows, value_rows, allowed):
    batch, length, width = query.shape
    head_count = width // HEAD_DIM
    query_heads = query.reshape(batch, length, head_count, HEAD_DIM)
    key_heads = key_rows.reshape(batch, key_rows.shape[1], head_count, HEAD_DIM)
    value_heads = value_rows.reshape(batch, key_rows.shape[1], head_count, HEAD_DIM)
    scores = jnp.einsum('rqhe,rkhe->rhqk', query_heads, key_heads, precision=lax.Precision.HIGHEST) * HEAD_DIM ** (-0.5)
    scores = low_back(jnp.where(allowed[:, None], scores, -1e+30))
    peak = lax.optimization_barrier(jnp.max(scores, axis=-1, keepdims=True))
    exponent = jnp.exp(scores - peak)
    soft = low(exponent / lax.optimization_barrier(jnp.sum(exponent, axis=-1, keepdims=True)))
    mixed = jnp.einsum('rhqk,rkhe->rqhe', soft, value_heads, precision=lax.Precision.HIGHEST)
    return mixed.reshape(batch, length, width)

def self_block(inputs, w_qk, w_vo, section_bias, gain, allowed):
    query = round_both(matmul(inputs, w_qk[:, :D]) + section_bias[0])
    key_rows = round_both(matmul(inputs, w_qk[:, D:]))
    value_rows = round_both(matmul(inputs, w_vo[:, :D]) + section_bias[1])
    mixed = round_both(attend(query, key_rows, value_rows, allowed))
    branch = low_back(matmul(mixed, w_vo[:, D:]) + section_bias[2])
    return layer_norm(inputs + branch, gain, section_bias[3])

def feed_forward(hidden, w_in, w_out, b_in, b_out):
    pre = low_back(matmul(low(hidden), w_in) + b_in)
    act = low(jax.nn.gelu(pre, approximate=False))
    return low_back(matmul(act, w_out) + b_out)

def forward(params, source_rows, target_rows, seg_source, seg_target):
    attn_qk, attn_vo, cross_qk, cross_vo, ffn_in, ffn_out, gains, biases, ffn_bias = params
    position = jnp.arange(SEQ)
    earlier = position[None, :] <= position[:, None]
    same_source = seg_source[:, :, None] == seg_source[:, None, :]
    same_target = (seg_target[:, :, None] == seg_target[:, None, :]) & earlier[None]
    cross_mask = seg_target[:, :, None] == seg_source[:, None, :]
    enc_hidden = self_block(source_rows, attn_qk[0], attn_vo[0], biases[0:6], gains[0], same_source)
    enc_resid = enc_hidden + feed_forward(enc_hidden, ffn_in[0], ffn_out[0], ffn_bias[0], biases[4])
    memory = low(layer_norm(enc_resid, gains[1], biases[5]))
    cross_keys = round_both(matmul(memory, cross_qk[0]))
    cross_values = round_both(matmul(memory, cross_vo[0]) + biases[13])
    dec_hidden = self_block(target_rows, attn_qk[1], attn_vo[1], biases[6:12], gains[2], same_target)
    cross_query = round_both(matmul(low(dec_hidden), cross_qk[1]) + biases[12])
    cross_mixed = round_both(attend(cross_query, cross_keys, cross_values, cross_mask))
    cross_branch = low_back(matmul(cross_mixed, cross_vo[1]) + biases[14])
    middle = layer_norm(dec_hidden + cross_branch, gains[4], biases[15])
    dec_resid = middle + feed_forward(middle, ffn_in[1], ffn_out[1], ffn_bias[1], biases[10])
    result = layer_norm(dec_resid, gains[3], biases[11])
    return (memory, result)

def reference(tokens, segments, cotangent, attn_qk, attn_vo, cross_qk, cross_vo, ffn_in, ffn_out, gains, biases, ffn_bias):
    params = tuple((weight.astype(jnp.float32) for weight in (attn_qk, attn_vo, cross_qk, cross_vo, ffn_in, ffn_out, gains, biases, ffn_bias)))
    group = math.gcd(ROWS, 8)
    blocks = ROWS // group

    def regroup(array):
        return array.reshape((blocks, group) + array.shape[1:])
    batch_items = (regroup(tokens[0].astype(jnp.float32)), regroup(tokens[1].astype(jnp.float32)), regroup(segments[0]), regroup(segments[1]), regroup(cotangent.astype(jnp.float32)))

    def scan_step(summed, batch_item):
        source_rows, target_rows, seg_source, seg_target, cot_rows = batch_item

        def forward_part(weights, source_part, target_part):
            return forward(weights, source_part, target_part, seg_source, seg_target)
        (memory, result), pull = jax.vjp(forward_part, params, source_rows, target_rows)
        grad_weights, grad_source, grad_target = pull((jnp.zeros_like(memory), cot_rows))
        summed = jax.tree.map(jnp.add, summed, grad_weights)
        return (summed, (memory.astype(jnp.bfloat16), result.astype(jnp.bfloat16), grad_source, grad_target))
    start = jax.tree.map(jnp.zeros_like, params)
    summed, outputs = lax.scan(scan_step, start, batch_items)
    merged = [piece.reshape((ROWS,) + piece.shape[2:]) for piece in outputs]
    layer_out = jnp.stack([merged[0], merged[1]])
    input_grad = jnp.stack([merged[2], merged[3]])
    return (layer_out, input_grad, summed[0], summed[1], summed[2], summed[3], summed[4], summed[5], summed[6], summed[7], summed[8])
```

```python
import jax
import jax.numpy as jnp
from jax import lax
from jax.experimental import pallas as pl
from jax.experimental.pallas import tpu as pltpu
from jax.sharding import PartitionSpec as P

HEADS = 12


NORM_EPSILON = 1e-05


def from_behind(x, axis, by):
    devices = lax.axis_size(axis)
    pairs = [(i, i + by) for i in range(devices) if 0 <= i + by < devices]
    return lax.ppermute(x, axis, pairs)


def product(left, right):
    return jnp.einsum("rld,de->rle", left, right, preferred_element_type=jnp.float32)


def back_product(grad, right):
    return jnp.einsum("rle,de->rld", grad, right, preferred_element_type=jnp.float32)


def weight_grad(left, grad):
    return jnp.einsum("rld,rle->de", left, grad, preferred_element_type=jnp.float32)


def column_sum(values):
    return jnp.sum(values.astype(jnp.float32), axis=(0, 1))


def norm_rows(resid, gain, shift):
    center = resid - jnp.mean(resid, axis=-1, keepdims=True)
    spread = jnp.mean(center * center, axis=-1, keepdims=True)
    return center * lax.rsqrt(spread + NORM_EPSILON) * gain + shift


def norm_back(resid, gain, shift, grad):
    unused, pull = jax.vjp(norm_rows, resid, gain, shift)
    return pull(grad)


def split_heads(values, head_count):
    return values.reshape(
        values.shape[0], values.shape[1], head_count, values.shape[2] // head_count
    )


def masked_scores(query_heads, key_heads, allowed):
    scale = query_heads.shape[-1] ** (-0.5)
    scores = (
        jnp.einsum("rqhe,rkhe->rhqk", query_heads, key_heads, preferred_element_type=jnp.float32)
        * scale
    )
    return jnp.where(allowed[:, None], scores, -1e30)


def attend(query, key_rows, value_rows, allowed, head_count):
    query_heads = split_heads(query, head_count)
    scores = masked_scores(query_heads, split_heads(key_rows, head_count), allowed)
    peak = jnp.max(scores, axis=-1, keepdims=True)
    exponent = jnp.exp(scores - peak)
    summed = jnp.sum(exponent, axis=-1, keepdims=True)
    soft = (exponent / summed).astype(jnp.bfloat16)
    mixed = jnp.einsum(
        "rhqk,rkhe->rqhe",
        soft,
        split_heads(value_rows, head_count),
        preferred_element_type=jnp.float32,
    )
    return (mixed.reshape(query.shape), peak + jnp.log(summed))


def attend_back(query, key_rows, value_rows, allowed, log_total, grad_mixed, head_count):
    query_heads = split_heads(query, head_count)
    key_heads = split_heads(key_rows, head_count)
    value_heads = split_heads(value_rows, head_count)
    grad_heads = split_heads(grad_mixed, head_count)
    scale = query_heads.shape[-1] ** (-0.5)
    soft = jnp.exp(masked_scores(query_heads, key_heads, allowed) - log_total)
    grad_values = jnp.einsum(
        "rhqk,rqhe->rkhe", soft.astype(jnp.bfloat16), grad_heads, preferred_element_type=jnp.float32
    )
    grad_soft = jnp.einsum(
        "rqhe,rkhe->rhqk", grad_heads, value_heads, preferred_element_type=jnp.float32
    )
    inner_sum = jnp.sum(soft * grad_soft, axis=-1, keepdims=True)
    grad_scores = (soft * (grad_soft - inner_sum)).astype(jnp.bfloat16)
    grad_query = (
        jnp.einsum("rhqk,rkhe->rqhe", grad_scores, key_heads, preferred_element_type=jnp.float32)
        * scale
    )
    grad_keys = (
        jnp.einsum("rhqk,rqhe->rkhe", grad_scores, query_heads, preferred_element_type=jnp.float32)
        * scale
    )
    return (
        grad_query.reshape(query.shape),
        grad_keys.reshape(key_rows.shape),
        grad_values.reshape(key_rows.shape),
    )


def self_forward(inputs, w_qk, w_vo, section_bias, gain, allowed, head_count):
    model_width = inputs.shape[-1]
    query = (product(inputs, w_qk[:, :model_width]) + section_bias[0]).astype(jnp.bfloat16)
    key_rows = product(inputs, w_qk[:, model_width:]).astype(jnp.bfloat16)
    value_rows = (product(inputs, w_vo[:, :model_width]) + section_bias[1]).astype(jnp.bfloat16)
    mixed, log_total = attend(query, key_rows, value_rows, allowed, head_count)
    mixed = mixed.astype(jnp.bfloat16)
    resid = inputs.astype(jnp.float32) + product(mixed, w_vo[:, model_width:]) + section_bias[2]
    return (
        norm_rows(resid, gain, section_bias[3]),
        (query, key_rows, value_rows, log_total, mixed, resid),
    )


def self_backward(inputs, w_qk, w_vo, section_bias, gain, allowed, head_count, kept, grad_hidden):
    query, key_rows, value_rows, log_total, mixed, resid = kept
    model_width = inputs.shape[-1]
    grad_resid, grad_gain, grad_shift = norm_back(resid, gain, section_bias[3], grad_hidden)
    grad_branch = grad_resid.astype(jnp.bfloat16)
    grad_mixed = back_product(grad_branch, w_vo[:, model_width:]).astype(jnp.bfloat16)
    grad_query, grad_keys, grad_values = attend_back(
        query, key_rows, value_rows, allowed, log_total, grad_mixed, head_count
    )
    grad_query = grad_query.astype(jnp.bfloat16)
    grad_keys = grad_keys.astype(jnp.bfloat16)
    grad_values = grad_values.astype(jnp.bfloat16)
    grad_pair = jnp.concatenate([grad_query, grad_keys], axis=-1)
    grad_inputs = (
        grad_resid
        + back_product(grad_pair, w_qk)
        + back_product(grad_values, w_vo[:, :model_width])
    )
    grad_rows = jnp.stack(
        [column_sum(grad_query), column_sum(grad_values), column_sum(grad_branch), grad_shift]
    )
    return (grad_inputs, (inputs, grad_pair, grad_values, mixed, grad_branch), grad_rows, grad_gain)


def ffn_forward(hidden, w_in, w_out, b_in, b_out):
    hidden_low = hidden.astype(jnp.bfloat16)
    pre_act = product(hidden_low, w_in) + b_in
    activated = jax.nn.gelu(pre_act, approximate=False).astype(jnp.bfloat16)
    return (product(activated, w_out) + b_out, (hidden_low, pre_act, activated))


def gelu_exact(values):
    return jax.nn.gelu(values, approximate=False)


def ffn_backward(w_in, w_out, kept, grad_branch):
    hidden_low, pre_act, activated = kept
    grad_low = grad_branch.astype(jnp.bfloat16)
    grad_act = back_product(grad_low, w_out)
    unused, pull = jax.vjp(gelu_exact, pre_act)
    grad_pre = pull(grad_act)[0].astype(jnp.bfloat16)
    grad_hidden = back_product(grad_pre, w_in)
    return (
        grad_hidden,
        (hidden_low, grad_pre, activated, grad_low),
        column_sum(grad_pre),
        column_sum(grad_low),
    )


def encoder_forward(hidden, w_in, w_out, b_in, section_bias, gain_last, w_ck, w_cv, bias_cv):
    branch, kept = ffn_forward(hidden, w_in, w_out, b_in, section_bias[4])
    resid = hidden + branch
    memory = norm_rows(resid, gain_last, section_bias[5]).astype(jnp.bfloat16)
    key_rows = product(memory, w_ck).astype(jnp.bfloat16)
    value_rows = (product(memory, w_cv) + bias_cv).astype(jnp.bfloat16)
    return (memory, key_rows, value_rows, resid, kept)


def encoder_backward(
    w_in, w_out, section_bias, gain_last, w_ck, w_cv, memory, resid, kept, grad_keys, grad_values
):
    grad_memory = back_product(grad_keys, w_ck) + back_product(grad_values, w_cv)
    grad_last, grad_gain, grad_shift = norm_back(resid, gain_last, section_bias[5], grad_memory)
    grad_ffn, ffn_ops, grad_bin, grad_bout = ffn_backward(w_in, w_out, kept, grad_last)
    zero_line = jnp.zeros_like(grad_gain)
    cross_rows = jnp.stack([zero_line, column_sum(grad_values), zero_line, zero_line])
    operands = (memory, grad_keys, memory, grad_values) + ffn_ops
    return (
        grad_last + grad_ffn,
        operands,
        grad_bin,
        grad_bout,
        grad_gain,
        grad_shift,
        cross_rows,
        zero_line,
    )


def decoder_step(
    hidden,
    w_cq,
    w_co,
    w_in,
    w_out,
    b_in,
    section_bias,
    gain_last,
    gain_cross,
    cross_bias,
    key_rows,
    value_rows,
    allowed,
    cotangent,
    head_count,
):
    hidden_low = hidden.astype(jnp.bfloat16)
    query = (product(hidden_low, w_cq) + cross_bias[0]).astype(jnp.bfloat16)
    mixed, log_total = attend(query, key_rows, value_rows, allowed, head_count)
    mixed = mixed.astype(jnp.bfloat16)
    resid_mid = hidden + product(mixed, w_co) + cross_bias[2]
    middle = norm_rows(resid_mid, gain_cross, cross_bias[3])
    branch, kept = ffn_forward(middle, w_in, w_out, b_in, section_bias[4])
    resid_last = middle + branch
    result = norm_rows(resid_last, gain_last, section_bias[5])
    grad_last, grad_gain, grad_shift = norm_back(
        resid_last, gain_last, section_bias[5], cotangent.astype(jnp.float32)
    )
    grad_ffn, ffn_ops, grad_bin, grad_bout = ffn_backward(w_in, w_out, kept, grad_last)
    grad_mid, grad_gain_cross, grad_shift_cross = norm_back(
        resid_mid, gain_cross, cross_bias[3], grad_last + grad_ffn
    )
    grad_branch = grad_mid.astype(jnp.bfloat16)
    grad_mixed = back_product(grad_branch, w_co).astype(jnp.bfloat16)
    grad_query, grad_keys, grad_values = attend_back(
        query, key_rows, value_rows, allowed, log_total, grad_mixed, head_count
    )
    grad_query = grad_query.astype(jnp.bfloat16)
    grad_hidden = grad_mid + back_product(grad_query, w_cq)
    cross_rows = jnp.stack(
        [
            column_sum(grad_query),
            jnp.zeros_like(grad_gain),
            column_sum(grad_branch),
            grad_shift_cross,
        ]
    )
    operands = (hidden_low, grad_query, mixed, grad_branch) + ffn_ops
    tail_result = (
        grad_hidden,
        operands,
        grad_bin,
        grad_bout,
        grad_gain,
        grad_shift,
        cross_rows,
        grad_gain_cross,
    )
    return (
        result.astype(jnp.bfloat16),
        grad_keys.astype(jnp.bfloat16),
        grad_values.astype(jnp.bfloat16),
        tail_result,
    )


def zero_tail(hidden, w_in):
    model_width = hidden.shape[-1]
    ffn_width = w_in.shape[1]
    flat = jnp.zeros(hidden.shape, jnp.bfloat16)
    wide = jnp.zeros((hidden.shape[0], hidden.shape[1], ffn_width), jnp.bfloat16)
    zero_line = jnp.zeros((model_width,), jnp.float32)
    operands = (flat, flat, flat, flat, flat, wide, wide, flat)
    return (
        jnp.zeros_like(hidden),
        operands,
        jnp.zeros((ffn_width,), jnp.float32),
        zero_line,
        zero_line,
        zero_line,
        jnp.zeros((4, model_width), jnp.float32),
        zero_line,
    )


def tail_whole(operands):
    return (
        weight_grad(operands[0], operands[1]),
        weight_grad(operands[2], operands[3]),
        weight_grad(operands[4], operands[5]),
        weight_grad(operands[6], operands[7]),
    )


def self_whole(operands):
    grad_qk = weight_grad(operands[0], operands[1])
    grad_vo = jnp.concatenate(
        [weight_grad(operands[0], operands[2]), weight_grad(operands[3], operands[4])], axis=1
    )
    return (grad_qk, grad_vo)


def local_any(
    tokens,
    segments,
    cotangent,
    attn_qk,
    attn_vo,
    cross_qk,
    cross_vo,
    ffn_in,
    ffn_out,
    gains,
    biases,
    ffn_bias,
):
    head_count = HEADS
    section_index = lax.axis_index("section")
    is_enc = section_index == 0
    qk_whole, vo_whole = (
        lax.all_gather(attn_qk, "dp", axis=1, tiled=True),
        lax.all_gather(attn_vo, "dp", axis=1, tiled=True),
    )
    w_qk = qk_whole[0]
    w_vo = vo_whole[0]
    cqk_whole, cvo_whole, in_whole, out_whole = (
        lax.all_gather(cross_qk, "dp", axis=1, tiled=True),
        lax.all_gather(cross_vo, "dp", axis=1, tiled=True),
        lax.all_gather(ffn_in, "dp", axis=1, tiled=True),
        lax.all_gather(ffn_out, "dp", axis=1, tiled=True),
    )
    w_cqk = cqk_whole[0]
    w_cvo = cvo_whole[0]
    w_in = in_whole[0]
    w_out = out_whole[0]
    section_bias = lax.dynamic_slice_in_dim(biases, 6 * section_index, 6, 0)
    section_gain = lax.dynamic_slice_in_dim(gains, 2 * section_index, 2, 0)
    bias_in = lax.dynamic_index_in_dim(ffn_bias, section_index, 0, keepdims=False)
    section_seg = lax.dynamic_index_in_dim(segments, section_index, 0, keepdims=False)
    length = tokens.shape[2]
    position = jnp.arange(length)
    earlier = position[None, :] <= position[:, None]
    allowed_self = (section_seg[:, :, None] == section_seg[:, None, :]) & (earlier[None] | is_enc)
    allowed_cross = segments[1][:, :, None] == segments[0][:, None, :]
    source = tokens[0]
    hidden_one, kept_self = self_forward(
        source, w_qk, w_vo, section_bias, section_gain[0], allowed_self, head_count
    )

    def run_encoder():
        return encoder_forward(
            hidden_one,
            w_in,
            w_out,
            bias_in,
            section_bias,
            section_gain[1],
            w_cqk,
            w_cvo,
            biases[13],
        )

    def skip_encoder():
        flat = jnp.zeros(hidden_one.shape, jnp.bfloat16)
        wide_shape = (hidden_one.shape[0], hidden_one.shape[1], w_in.shape[1])
        return (
            flat,
            flat,
            flat,
            jnp.zeros_like(hidden_one),
            (flat, jnp.zeros(wide_shape, jnp.float32), jnp.zeros(wide_shape, jnp.bfloat16)),
        )

    memory, enc_keys, enc_values, enc_resid, enc_kept = lax.cond(is_enc, run_encoder, skip_encoder)
    got_keys, got_values = from_behind((enc_keys, enc_values), "section", 1)

    def run_decoder():
        return decoder_step(
            hidden_one,
            w_cqk,
            w_cvo,
            w_in,
            w_out,
            bias_in,
            section_bias,
            section_gain[1],
            gains[4],
            biases[12:16],
            got_keys,
            got_values,
            allowed_cross,
            cotangent,
            head_count,
        )

    def skip_decoder():
        flat = jnp.zeros(hidden_one.shape, jnp.bfloat16)
        return (flat, flat, flat, zero_tail(hidden_one, w_in))

    decoded, grad_keys, grad_values, dec_tail = lax.cond(is_enc, skip_decoder, run_decoder)
    back_keys, back_values = from_behind((grad_keys, grad_values), "section", -1)

    def run_encoder_back():
        return encoder_backward(
            w_in,
            w_out,
            section_bias,
            section_gain[1],
            w_cqk,
            w_cvo,
            memory,
            enc_resid,
            enc_kept,
            back_keys,
            back_values,
        )

    def keep_decoder():
        return dec_tail

    tail_result = lax.cond(is_enc, run_encoder_back, keep_decoder)
    (
        grad_hidden,
        tail_ops,
        grad_bin,
        grad_bout,
        grad_gain_last,
        grad_shift_last,
        cross_rows,
        grad_gain_cross,
    ) = tail_result
    layer_out = jnp.where(is_enc, memory, decoded)
    model_width = source.shape[-1]
    grad_ca, grad_cb, grad_in, grad_out = tail_whole(tail_ops)
    tail_parts = (
        lax.psum_scatter(grad_ca[None], "dp", scatter_dimension=1, tiled=True),
        lax.psum_scatter(grad_cb[None], "dp", scatter_dimension=1, tiled=True),
        lax.psum_scatter(grad_in[None], "dp", scatter_dimension=1, tiled=True),
        lax.psum_scatter(grad_out[None], "dp", scatter_dimension=1, tiled=True),
    )
    grad_source, self_ops, self_rows, grad_gain_first = self_backward(
        source,
        w_qk,
        w_vo,
        section_bias,
        section_gain[0],
        allowed_self,
        head_count,
        kept_self,
        grad_hidden,
    )
    grad_qk, grad_vo = self_whole(self_ops)
    attn_parts = (
        lax.psum_scatter(grad_qk[None], "dp", scatter_dimension=1, tiled=True),
        lax.psum_scatter(grad_vo[None], "dp", scatter_dimension=1, tiled=True),
    )
    large_parts = tuple(attn_parts) + tuple(tail_parts)
    section_rows = jnp.concatenate([self_rows, jnp.stack([grad_bout, grad_shift_last])], axis=0)
    bias_block = lax.dynamic_update_slice_in_dim(
        jnp.zeros((12, model_width), jnp.float32), section_rows, 6 * section_index, 0
    )
    grad_biases = jnp.concatenate([bias_block, cross_rows], axis=0)
    gain_block = lax.dynamic_update_slice_in_dim(
        jnp.zeros((4, model_width), jnp.float32),
        jnp.stack([grad_gain_first, grad_gain_last]),
        2 * section_index,
        0,
    )
    grad_gains = jnp.concatenate([gain_block, grad_gain_cross[None]], axis=0)
    grad_fbias = lax.dynamic_update_slice_in_dim(
        jnp.zeros_like(ffn_bias), grad_bin[None], section_index, 0
    )
    sum_gains, sum_biases, sum_fbias = lax.psum(
        (grad_gains, grad_biases, grad_fbias), ("section", "dp")
    )
    return (
        layer_out[None],
        grad_source[None],
        large_parts[0],
        large_parts[1],
        large_parts[2],
        large_parts[3],
        large_parts[4],
        large_parts[5],
        sum_gains,
        sum_biases,
        sum_fbias,
    )


MESH = pl.DeviceIdType.MESH
CHIPS = 8
FAR = 3


class Place:
    def __init__(self):
        self.section = lax.axis_index("section")
        shard = lax.axis_index("dp")
        self.core = shard % 2
        self.chip = shard // 2
        across = self.chip % 2
        along = self.chip // 2
        self.pos = along + across * (7 - 2 * along)

    def chip_at(self, step):
        spot = (self.pos + step + CHIPS) % CHIPS
        across = spot // 4
        along = spot + across * (7 - 2 * spot)
        return along * 2 + across

    def ring(self, step):
        return (self.section, self.chip_at(step) * 2 + self.core)

    def sibling(self):
        return (self.section, self.chip * 2 + 1 - self.core)

    def peer(self):
        return (1 - self.section, self.chip * 2 + self.core)


def enter(place):
    barrier = pltpu.get_barrier_semaphore()
    for other in (place.ring(1), place.ring(-1), place.sibling(), place.peer()):
        pl.semaphore_signal(barrier, inc=1, device_id=other, device_id_type=MESH)
    pl.semaphore_wait(barrier, 4)


class Piece:
    def __init__(self, ref, by_rows, low, span, slot):
        self.ref, self.by_rows, self.low, self.span, self.slot = ref, by_rows, low, span, slot

    def at(self, chip, core, half=None):
        low, span = self.low, self.span
        if half is not None:
            span = span // 2
            low = low + half * span
        if self.by_rows:
            return self.ref.at[chip, core, low : low + span, :]
        return self.ref.at[chip, core, :, low : low + span]


class Gather:
    def __init__(self, place, pieces, ring_send, ring_recv, side_send, side_recv):
        self.place, self.pieces = place, pieces
        self.ring_send, self.ring_recv, self.side_send, self.side_recv = ring_send, ring_recv, side_send, side_recv

    def ring_copy(self, p, way, hop):
        sign = 1 - 2 * way
        ref = self.pieces[p].at(self.place.chip_at(-sign * hop), self.place.core, way if hop == FAR else None)
        return pltpu.make_async_remote_copy(
            ref, ref, self.ring_send.at[p, way, hop], self.ring_recv.at[p, way, hop],
            device_id=self.place.ring(sign), device_id_type=MESH,
        )

    def arrival(self, p, way, hop, core):
        sign = 1 - 2 * way
        return self.pieces[p].at(self.place.chip_at(-sign * (hop + 1)), core, way if hop == FAR else None)

    def side_copy(self, p, k, core):
        if k == 0:
            ref = self.pieces[p].at(self.place.chip, core)
        else:
            ref = self.arrival(p, (k - 1) // 4, (k - 1) % 4, core)
        return pltpu.make_async_remote_copy(
            ref, ref, self.side_send.at[p, k], self.side_recv.at[p, k],
            device_id=self.place.sibling(), device_id_type=MESH,
        )

    def start(self, p):
        self.ring_copy(p, 0, 0).start()
        self.ring_copy(p, 1, 0).start()
        self.side_copy(p, 0, self.place.core).start()

    def event(self, p, way, hop):
        ref = self.arrival(p, way, hop, self.place.core)
        pltpu.make_async_remote_copy(
            ref, ref, self.ring_send.at[p, way, hop], self.ring_recv.at[p, way, hop],
            device_id=self.place.ring(1), device_id_type=MESH,
        ).wait_recv()
        if hop < FAR:
            self.ring_copy(p, way, hop + 1).start()
        self.side_copy(p, 1 + 4 * way + hop, self.place.core).start()

    def side_arrivals(self, p):
        for k in range(9):
            self.side_copy(p, k, 1 - self.place.core).wait_recv()

    def finish(self, p):
        for way in range(2):
            for hop in range(4):
                self.ring_copy(p, way, hop).wait_send()
        for k in range(9):
            self.side_copy(p, k, self.place.core).wait_send()


def piece_list(qk, vo, w_in, w_out, cross):
    return [
        Piece(qk, False, 0, 1536, 0),
        Piece(vo, False, 0, 1536, 1),
        Piece(w_in, False, 0, 1536, 2),
        Piece(w_in, False, 1536, 1536, 3),
        Piece(w_out, True, 0, 96, 0),
        Piece(w_out, True, 96, 96, 1),
        Piece(cross, False, 0, 1536, 4),
        Piece(cross, False, 1536, 1536, 5),
    ]


def gather_kernel(qk, vo, cqk, cvo, fin, fout, w_qk, w_vo, w_in, w_out, w_x, local_sem, x_send, x_recv, rs, rr, ss, sr):
    place = Place()
    chip, core = place.chip, place.core
    width = cqk.shape[-1]
    copies = [
        pltpu.make_async_copy(src.at[0], dst.at[chip, core], local_sem.at[i])
        for i, (src, dst) in enumerate([(qk, w_qk), (vo, w_vo), (fin, w_in), (fout, w_out)])
    ]
    for copy in copies:
        copy.start()
    enter(place)
    decoder = place.section == 1
    own_cross = [
        pltpu.make_async_copy(src.at[0], w_x.at[chip, core, :, i * width : (i + 1) * width], local_sem.at[4 + i])
        for i, src in enumerate([cqk, cvo])
    ]
    from_encoder = [
        pltpu.make_async_remote_copy(
            src.at[0], w_x.at[chip, core, :, (2 + i) * width : (3 + i) * width], x_send.at[i], x_recv.at[i],
            device_id=place.peer(), device_id_type=MESH,
        )
        for i, src in enumerate([cqk, cvo])
    ]

    @pl.when(place.section == 0)
    def _():
        for copy in from_encoder:
            copy.start()

    @pl.when(decoder)
    def _():
        for copy in own_cross:
            copy.start()

    for copy in copies:
        copy.wait()
    gather = Gather(place, piece_list(w_qk, w_vo, w_in, w_out, w_x), rs, rr, ss, sr)
    gather.start(0)
    gather.start(1)
    for pair in range(3):
        for hop in range(4):
            for p in (2 * pair, 2 * pair + 1):
                for way in range(2):
                    gather.event(p, way, hop)
                if hop == 2 and p + 2 < 6:
                    gather.start(p + 2)

    @pl.when(decoder)
    def _():
        for copy in own_cross:
            copy.wait()
        for copy in from_encoder:
            copy.wait_recv()
        gather.start(6)
        gather.start(7)
        for hop in range(4):
            for p in (6, 7):
                for way in range(2):
                    gather.event(p, way, hop)
        for p in (6, 7):
            gather.side_arrivals(p)
            gather.finish(p)

    @pl.when(place.section == 0)
    def _():
        for copy in from_encoder:
            copy.wait_send()

    for p in range(6):
        gather.side_arrivals(p)
        gather.finish(p)


def gather_weights(qk, vo, cqk, cvo, fin, fout):
    def whole(shard, columns):
        return jax.ShapeDtypeStruct((CHIPS, 2, shard.shape[1], columns), shard.dtype)

    any_space = pl.BlockSpec(memory_space=pl.ANY)
    return pl.pallas_call(
        gather_kernel,
        out_shape=(
            whole(qk, qk.shape[2]), whole(vo, vo.shape[2]), whole(fin, fin.shape[2]), whole(fout, fout.shape[2]),
            whole(cqk, 4 * cqk.shape[2]),
        ),
        in_specs=[any_space] * 6,
        out_specs=(any_space,) * 5,
        scratch_shapes=[
            pltpu.SemaphoreType.DMA((6,)),
            pltpu.SemaphoreType.DMA((2,)),
            pltpu.SemaphoreType.DMA((2,)),
            pltpu.SemaphoreType.DMA((8, 2, 4)),
            pltpu.SemaphoreType.DMA((8, 2, 4)),
            pltpu.SemaphoreType.DMA((8, 9)),
            pltpu.SemaphoreType.DMA((8, 9)),
        ],
        compiler_params=pltpu.CompilerParams(collective_id=0, has_side_effects=True),
        name="gather_weights",
    )(qk, vo, cqk, cvo, fin, fout)


class Scatter:
    def __init__(self, place, pieces, side_c, side_r, land_c, land_r, ring_send, ring_recv, side_send, side_recv):
        self.place, self.pieces = place, pieces
        self.side_c, self.side_r, self.land_c, self.land_r = side_c, side_r, land_c, land_r
        self.ring_send, self.ring_recv, self.side_send, self.side_recv = ring_send, ring_recv, side_send, side_recv

    def cut(self, p, ref, half):
        piece = self.pieces[p]
        if half is None:
            return ref
        span = piece.span // 2
        if piece.by_rows:
            return ref.at[half * span : (half + 1) * span, :]
        return ref.at[:, half * span : (half + 1) * span]

    def from_side(self, p, chip, half=None):
        piece = self.pieces[p]
        return self.cut(p, (self.side_r if piece.by_rows else self.side_c).at[piece.slot, chip], half)

    def landed(self, p, way, step, half=None):
        piece = self.pieces[p]
        return self.cut(p, (self.land_r if piece.by_rows else self.land_c).at[piece.slot, way, step], half)

    def side_copy(self, p):
        piece = self.pieces[p]
        span = slice(piece.low, piece.low + piece.span)
        other = 1 - self.place.core
        src = piece.ref.at[:, other, span, :] if piece.by_rows else piece.ref.at[:, other, :, span]
        dst = (self.side_r if piece.by_rows else self.side_c).at[piece.slot]
        return pltpu.make_async_remote_copy(
            src, dst, self.side_send.at[p], self.side_recv.at[p],
            device_id=self.place.sibling(), device_id_type=MESH,
        )

    def chip_of(self, way, step):
        sign = 1 - 2 * way
        return self.place.chip_at(sign * (4 - step))

    def ring_copy(self, p, way, step):
        sign = 1 - 2 * way
        half = way if step == 0 else None
        return pltpu.make_async_remote_copy(
            self.pieces[p].at(self.chip_of(way, step), self.place.core, half), self.landed(p, way, step, half),
            self.ring_send.at[p, way, step], self.ring_recv.at[p, way, step],
            device_id=self.place.ring(sign), device_id_type=MESH,
        )

    def start(self, p):
        self.side_copy(p).wait_recv()
        for way in range(2):
            chip = self.chip_of(way, 0)
            own = self.pieces[p].at(chip, self.place.core, way)
            total = own[...].astype(jnp.float32) + self.from_side(p, chip, way)[...].astype(jnp.float32)
            own[...] = total.astype(jnp.bfloat16)
            self.ring_copy(p, way, 0).start()

    def event(self, p, way, step):
        self.ring_copy(p, way, step).wait_recv()
        chip = self.chip_of(way, step + 1)
        for half in range(2):
            own = self.pieces[p].at(chip, self.place.core, half)
            total = own[...].astype(jnp.float32) + self.from_side(p, chip, half)[...].astype(jnp.float32)
            if step > 0 or half == way:
                total = total + self.landed(p, way, step, half)[...].astype(jnp.float32)
            own[...] = total.astype(jnp.bfloat16)
        self.ring_copy(p, way, step + 1).start()

    def last(self, p):
        chip = self.place.chip
        total = self.pieces[p].at(chip, self.place.core)[...].astype(jnp.float32)
        total = total + self.from_side(p, chip)[...].astype(jnp.float32)
        for way in range(2):
            self.ring_copy(p, way, 3).wait_recv()
            total = total + self.landed(p, way, 3)[...].astype(jnp.float32)
        return total

    def finish(self, p):
        self.side_copy(p).wait_send()
        for way in range(2):
            for step in range(4):
                self.ring_copy(p, way, step).wait_send()


def scatter_kernel(
    i_qk, i_vo, i_in, i_out, i_x, o_qk, o_vo, o_cqk, o_cvo, o_in, o_out,
    g_qk, g_vo, g_in, g_out, g_x, side_c, side_r, land_c, land_r, x_total, x_land,
    local_sem, x_send, x_recv, rs, rr, ss, sr,
):
    place = Place()
    decoder = place.section == 1
    copies = [
        pltpu.make_async_copy(src, dst, local_sem.at[i])
        for i, (src, dst) in enumerate([(i_qk, g_qk), (i_vo, g_vo), (i_in, g_in), (i_out, g_out), (i_x, g_x)])
    ]
    for copy in copies:
        copy.start()
    enter(place)
    scatter = Scatter(
        place, piece_list(g_qk, g_vo, g_in, g_out, g_x), side_c, side_r, land_c, land_r, rs, rr, ss, sr
    )
    for copy in copies:
        copy.wait()
    for p in range(6):
        scatter.side_copy(p).start()
    to_encoder = pltpu.make_async_remote_copy(
        x_total, x_land, x_send.at[0], x_recv.at[0], device_id=place.peer(), device_id_type=MESH
    )
    width = o_cqk.shape[-1]

    @pl.when(decoder)
    def _():
        for p in (6, 7):
            scatter.side_copy(p).start()
        for p in (6, 7):
            scatter.start(p)
        for step in range(3):
            for p in (6, 7):
                for way in range(2):
                    scatter.event(p, way, step)
        total = scatter.last(6)
        o_cqk[0] = total[:, :width]
        o_cvo[0] = total[:, width:]
        x_total[...] = scatter.last(7)
        to_encoder.start()

    scatter.start(0)
    scatter.start(1)
    for pair in range(3):
        for step in range(3):
            for p in (2 * pair, 2 * pair + 1):
                for way in range(2):
                    scatter.event(p, way, step)
                if step == 2 and p + 2 < 6:
                    scatter.start(p + 2)
        if pair == 0:
            o_qk[0] = scatter.last(0)
            o_vo[0] = scatter.last(1)
        elif pair == 1:
            o_in[0, :, :1536] = scatter.last(2)
            o_in[0, :, 1536:] = scatter.last(3)
        else:
            o_out[0, :96] = scatter.last(4)
            o_out[0, 96:] = scatter.last(5)

    @pl.when(decoder)
    def _():
        to_encoder.wait_send()
        for p in (6, 7):
            scatter.finish(p)

    @pl.when(place.section == 0)
    def _():
        to_encoder.wait_recv()
        o_cqk[0] = x_land[:, :width]
        o_cvo[0] = x_land[:, width:]

    for p in range(6):
        scatter.finish(p)


def scatter_grads(g_qk, g_vo, g_in, g_out, g_x):
    def mine(shape):
        return jax.ShapeDtypeStruct(shape, jnp.float32)

    any_space = pl.BlockSpec(memory_space=pl.ANY)
    in_vmem = pl.BlockSpec(memory_space=pltpu.VMEM)
    return pl.pallas_call(
        scatter_kernel,
        out_shape=(
            mine((1, 48, 1536)), mine((1, 48, 1536)), mine((1, 48, 768)), mine((1, 48, 768)),
            mine((1, 48, 3072)), mine((1, 192, 768)),
        ),
        in_specs=[any_space] * 5,
        out_specs=(in_vmem,) * 6,
        scratch_shapes=[pltpu.VMEM(g.shape, jnp.bfloat16) for g in (g_qk, g_vo, g_in, g_out, g_x)]
        + [
            pltpu.VMEM((6, CHIPS, 48, 1536), jnp.bfloat16),
            pltpu.VMEM((2, CHIPS, 96, 768), jnp.bfloat16),
            pltpu.VMEM((6, 2, 4, 48, 1536), jnp.bfloat16),
            pltpu.VMEM((2, 2, 4, 96, 768), jnp.bfloat16),
            pltpu.VMEM((48, 1536), jnp.float32),
            pltpu.VMEM((48, 1536), jnp.float32),
            pltpu.SemaphoreType.DMA((5,)),
            pltpu.SemaphoreType.DMA((1,)),
            pltpu.SemaphoreType.DMA((1,)),
            pltpu.SemaphoreType.DMA((8, 2, 4)),
            pltpu.SemaphoreType.DMA((8, 2, 4)),
            pltpu.SemaphoreType.DMA((8,)),
            pltpu.SemaphoreType.DMA((8,)),
        ],
        compiler_params=pltpu.CompilerParams(
            collective_id=1, has_side_effects=True, vmem_limit_bytes=56 * 1024 * 1024
        ),
        name="scatter_grads",
    )(g_qk, g_vo, g_in, g_out, g_x)


def local_ring(
    tokens,
    segments,
    cotangent,
    attn_qk,
    attn_vo,
    cross_qk,
    cross_vo,
    ffn_in,
    ffn_out,
    gains,
    biases,
    ffn_bias,
):
    head_count = HEADS
    section_index = lax.axis_index("section")
    is_enc = section_index == 0
    model_width = tokens.shape[-1]
    w_qk, w_vo, w_in, w_out, w_x = (
        whole.reshape(-1, whole.shape[-1])
        for whole in gather_weights(attn_qk, attn_vo, cross_qk, cross_vo, ffn_in, ffn_out)
    )
    w_cq, w_co, w_ck, w_cv = (w_x[:, i * model_width : (i + 1) * model_width] for i in range(4))
    section_bias = lax.dynamic_slice_in_dim(biases, 6 * section_index, 6, 0)
    section_gain = lax.dynamic_slice_in_dim(gains, 2 * section_index, 2, 0)
    bias_in = lax.dynamic_index_in_dim(ffn_bias, section_index, 0, keepdims=False)
    section_seg = lax.dynamic_index_in_dim(segments, section_index, 0, keepdims=False)
    length = tokens.shape[2]
    position = jnp.arange(length)
    earlier = position[None, :] <= position[:, None]
    allowed_self = (section_seg[:, :, None] == section_seg[:, None, :]) & (earlier[None] | is_enc)
    allowed_cross = segments[1][:, :, None] == segments[0][:, None, :]
    source = tokens[0]
    hidden_one, kept_self = self_forward(
        source, w_qk, w_vo, section_bias, section_gain[0], allowed_self, head_count
    )

    def run_encoder():
        branch, kept = ffn_forward(hidden_one, w_in, w_out, bias_in, section_bias[4])
        resid = hidden_one + branch
        return norm_rows(resid, section_gain[1], section_bias[5]).astype(jnp.bfloat16), resid, kept

    def skip_encoder():
        flat = jnp.zeros(hidden_one.shape, jnp.bfloat16)
        wide_shape = (hidden_one.shape[0], hidden_one.shape[1], w_in.shape[1])
        return (
            flat,
            jnp.zeros_like(hidden_one),
            (flat, jnp.zeros(wide_shape, jnp.float32), jnp.zeros(wide_shape, jnp.bfloat16)),
        )

    memory, enc_resid, enc_kept = lax.cond(is_enc, run_encoder, skip_encoder)
    got_memory = from_behind(memory, "section", 1)

    def run_decoder():
        key_rows = product(got_memory, w_ck).astype(jnp.bfloat16)
        value_rows = (product(got_memory, w_cv) + biases[13]).astype(jnp.bfloat16)
        decoded, grad_keys, grad_values, tail = decoder_step(
            hidden_one,
            w_cq,
            w_co,
            w_in,
            w_out,
            bias_in,
            section_bias,
            section_gain[1],
            gains[4],
            biases[12:16],
            key_rows,
            value_rows,
            allowed_cross,
            cotangent,
            head_count,
        )
        grad_memory = back_product(grad_keys, w_ck) + back_product(grad_values, w_cv)
        grad_hidden, operands, grad_bin, grad_bout, grad_gain, grad_shift, cross_rows, grad_gain_cross = tail
        cross_rows = cross_rows.at[1].set(column_sum(grad_values))
        grad_x = jnp.concatenate(
            [
                weight_grad(operands[0], operands[1]),
                weight_grad(operands[2], operands[3]),
                weight_grad(got_memory, grad_keys),
                weight_grad(got_memory, grad_values),
            ],
            axis=1,
        ).astype(jnp.bfloat16)
        return (
            decoded,
            grad_memory.astype(jnp.bfloat16),
            grad_x,
            (grad_hidden, operands[4:], grad_bin, grad_bout, grad_gain, grad_shift, cross_rows, grad_gain_cross),
        )

    def skip_decoder():
        flat = jnp.zeros(hidden_one.shape, jnp.bfloat16)
        tail = zero_tail(hidden_one, w_in)
        return (flat, flat, jnp.zeros(w_x.shape, jnp.bfloat16), (tail[0], tail[1][4:]) + tail[2:])

    decoded, grad_memory, grad_x, dec_tail = lax.cond(is_enc, skip_decoder, run_decoder)
    back_memory = from_behind(grad_memory, "section", -1).astype(jnp.float32)

    def run_encoder_back():
        grad_last, grad_gain, grad_shift = norm_back(enc_resid, section_gain[1], section_bias[5], back_memory)
        grad_ffn, ffn_ops, grad_bin, grad_bout = ffn_backward(w_in, w_out, enc_kept, grad_last)
        zero_line = jnp.zeros_like(grad_gain)
        return (
            grad_last + grad_ffn,
            ffn_ops,
            grad_bin,
            grad_bout,
            grad_gain,
            grad_shift,
            jnp.zeros((4, model_width), jnp.float32),
            zero_line,
        )

    def keep_decoder():
        return dec_tail

    tail_result = lax.cond(is_enc, run_encoder_back, keep_decoder)
    (
        grad_hidden,
        tail_ops,
        grad_bin,
        grad_bout,
        grad_gain_last,
        grad_shift_last,
        cross_rows,
        grad_gain_cross,
    ) = tail_result
    layer_out = jnp.where(is_enc, memory, decoded)
    grad_in = weight_grad(tail_ops[0], tail_ops[1]).astype(jnp.bfloat16)
    grad_out = weight_grad(tail_ops[2], tail_ops[3]).astype(jnp.bfloat16)
    grad_source, self_ops, self_rows, grad_gain_first = self_backward(
        source,
        w_qk,
        w_vo,
        section_bias,
        section_gain[0],
        allowed_self,
        head_count,
        kept_self,
        grad_hidden,
    )
    grad_qk, grad_vo = self_whole(self_ops)

    def blocks(grad):
        return grad.astype(jnp.bfloat16).reshape(CHIPS, 2, -1, grad.shape[-1])

    large_parts = scatter_grads(blocks(grad_qk), blocks(grad_vo), blocks(grad_in), blocks(grad_out), blocks(grad_x))
    section_rows = jnp.concatenate([self_rows, jnp.stack([grad_bout, grad_shift_last])], axis=0)
    bias_block = lax.dynamic_update_slice_in_dim(
        jnp.zeros((12, model_width), jnp.float32), section_rows, 6 * section_index, 0
    )
    grad_biases = jnp.concatenate([bias_block, cross_rows], axis=0)
    gain_block = lax.dynamic_update_slice_in_dim(
        jnp.zeros((4, model_width), jnp.float32),
        jnp.stack([grad_gain_first, grad_gain_last]),
        2 * section_index,
        0,
    )
    grad_gains = jnp.concatenate([gain_block, grad_gain_cross[None]], axis=0)
    grad_fbias = lax.dynamic_update_slice_in_dim(
        jnp.zeros_like(ffn_bias), grad_bin[None], section_index, 0
    )
    sum_gains, sum_biases, sum_fbias = lax.psum(
        (grad_gains, grad_biases, grad_fbias), ("section", "dp")
    )
    return (layer_out[None], grad_source[None]) + tuple(large_parts) + (sum_gains, sum_biases, sum_fbias)


def solution(mesh):
    any_size = mesh.shape["section"] != 2 or mesh.shape["dp"] != 2 * CHIPS
    placed = (
        P("section", "dp", None, None),
        P(None, "dp", None),
        P("dp", None, None),
        P("section", "dp", None),
        P("section", "dp", None),
        P("section", "dp", None),
        P("section", "dp", None),
        P("section", "dp", None),
        P("section", "dp", None),
        P(),
        P(),
        P(),
    )
    return jax.shard_map(
        local_any if any_size else local_ring,
        mesh=mesh,
        in_specs=placed,
        out_specs=(
            P("section", "dp", None, None),
            P("section", "dp", None, None),
            P("section", "dp", None),
            P("section", "dp", None),
            P("section", "dp", None),
            P("section", "dp", None),
            P("section", "dp", None),
            P("section", "dp", None),
            P(),
            P(),
            P(),
        ),
        check_vma=False,
    )
```

```python
import functools

import jax
import jax.numpy as jnp
from jax import lax
from jax.experimental import pallas as pl
from jax.experimental.pallas import tpu as pltpu
from jax.sharding import PartitionSpec as P

HEADS = 12


NORM_EPSILON = 1e-05


def from_behind(x, axis, by):
    devices = lax.axis_size(axis)
    pairs = [(i, i + by) for i in range(devices) if 0 <= i + by < devices]
    return lax.ppermute(x, axis, pairs)


def product(left, right):
    return jnp.einsum("rld,de->rle", left, right, preferred_element_type=jnp.float32)


def back_product(grad, right):
    return jnp.einsum("rle,de->rld", grad, right, preferred_element_type=jnp.float32)


def weight_grad(left, grad):
    return jnp.einsum("rld,rle->de", left, grad, preferred_element_type=jnp.float32)


def column_sum(values):
    return jnp.sum(values.astype(jnp.float32), axis=(0, 1))


def norm_rows(resid, gain, shift):
    center = resid - jnp.mean(resid, axis=-1, keepdims=True)
    spread = jnp.mean(center * center, axis=-1, keepdims=True)
    return center * lax.rsqrt(spread + NORM_EPSILON) * gain + shift


def norm_back(resid, gain, shift, grad):
    unused, pull = jax.vjp(norm_rows, resid, gain, shift)
    return pull(grad)


def split_heads(values, head_count):
    return values.reshape(
        values.shape[0], values.shape[1], head_count, values.shape[2] // head_count
    )


def masked_scores(query_heads, key_heads, allowed):
    scale = query_heads.shape[-1] ** (-0.5)
    scores = (
        jnp.einsum("rqhe,rkhe->rhqk", query_heads, key_heads, preferred_element_type=jnp.float32)
        * scale
    )
    return jnp.where(allowed[:, None], scores, -1e30)


def attend(query, key_rows, value_rows, allowed, head_count):
    query_heads = split_heads(query, head_count)
    scores = masked_scores(query_heads, split_heads(key_rows, head_count), allowed)
    peak = jnp.max(scores, axis=-1, keepdims=True)
    exponent = jnp.exp(scores - peak)
    summed = jnp.sum(exponent, axis=-1, keepdims=True)
    soft = (exponent / summed).astype(jnp.bfloat16)
    mixed = jnp.einsum(
        "rhqk,rkhe->rqhe",
        soft,
        split_heads(value_rows, head_count),
        preferred_element_type=jnp.float32,
    )
    return (mixed.reshape(query.shape), peak + jnp.log(summed))


def attend_back(query, key_rows, value_rows, allowed, log_total, grad_mixed, head_count):
    query_heads = split_heads(query, head_count)
    key_heads = split_heads(key_rows, head_count)
    value_heads = split_heads(value_rows, head_count)
    grad_heads = split_heads(grad_mixed, head_count)
    scale = query_heads.shape[-1] ** (-0.5)
    soft = jnp.exp(masked_scores(query_heads, key_heads, allowed) - log_total)
    grad_values = jnp.einsum(
        "rhqk,rqhe->rkhe", soft.astype(jnp.bfloat16), grad_heads, preferred_element_type=jnp.float32
    )
    grad_soft = jnp.einsum(
        "rqhe,rkhe->rhqk", grad_heads, value_heads, preferred_element_type=jnp.float32
    )
    inner_sum = jnp.sum(soft * grad_soft, axis=-1, keepdims=True)
    grad_scores = (soft * (grad_soft - inner_sum)).astype(jnp.bfloat16)
    grad_query = (
        jnp.einsum("rhqk,rkhe->rqhe", grad_scores, key_heads, preferred_element_type=jnp.float32)
        * scale
    )
    grad_keys = (
        jnp.einsum("rhqk,rqhe->rkhe", grad_scores, query_heads, preferred_element_type=jnp.float32)
        * scale
    )
    return (
        grad_query.reshape(query.shape),
        grad_keys.reshape(key_rows.shape),
        grad_values.reshape(key_rows.shape),
    )


def self_forward(inputs, w_qk, w_vo, section_bias, gain, allowed, head_count):
    model_width = inputs.shape[-1]
    query = (product(inputs, w_qk[:, :model_width]) + section_bias[0]).astype(jnp.bfloat16)
    key_rows = product(inputs, w_qk[:, model_width:]).astype(jnp.bfloat16)
    value_rows = (product(inputs, w_vo[:, :model_width]) + section_bias[1]).astype(jnp.bfloat16)
    mixed, log_total = attend(query, key_rows, value_rows, allowed, head_count)
    mixed = mixed.astype(jnp.bfloat16)
    resid = inputs.astype(jnp.float32) + product(mixed, w_vo[:, model_width:]) + section_bias[2]
    return (
        norm_rows(resid, gain, section_bias[3]),
        (query, key_rows, value_rows, log_total, mixed, resid),
    )


def self_backward(inputs, w_qk, w_vo, section_bias, gain, allowed, head_count, kept, grad_hidden):
    query, key_rows, value_rows, log_total, mixed, resid = kept
    model_width = inputs.shape[-1]
    grad_resid, grad_gain, grad_shift = norm_back(resid, gain, section_bias[3], grad_hidden)
    grad_branch = grad_resid.astype(jnp.bfloat16)
    grad_mixed = back_product(grad_branch, w_vo[:, model_width:]).astype(jnp.bfloat16)
    grad_query, grad_keys, grad_values = attend_back(
        query, key_rows, value_rows, allowed, log_total, grad_mixed, head_count
    )
    grad_query = grad_query.astype(jnp.bfloat16)
    grad_keys = grad_keys.astype(jnp.bfloat16)
    grad_values = grad_values.astype(jnp.bfloat16)
    grad_pair = jnp.concatenate([grad_query, grad_keys], axis=-1)
    grad_inputs = (
        grad_resid
        + back_product(grad_pair, w_qk)
        + back_product(grad_values, w_vo[:, :model_width])
    )
    grad_rows = jnp.stack(
        [column_sum(grad_query), column_sum(grad_values), column_sum(grad_branch), grad_shift]
    )
    return (grad_inputs, (inputs, grad_pair, grad_values, mixed, grad_branch), grad_rows, grad_gain)


def ffn_forward(hidden, w_in, w_out, b_in, b_out):
    hidden_low = hidden.astype(jnp.bfloat16)
    pre_act = product(hidden_low, w_in) + b_in
    activated = jax.nn.gelu(pre_act, approximate=False).astype(jnp.bfloat16)
    return (product(activated, w_out) + b_out, (hidden_low, pre_act, activated))


def gelu_exact(values):
    return jax.nn.gelu(values, approximate=False)


def ffn_backward(w_in, w_out, kept, grad_branch):
    hidden_low, pre_act, activated = kept
    grad_low = grad_branch.astype(jnp.bfloat16)
    grad_act = back_product(grad_low, w_out)
    unused, pull = jax.vjp(gelu_exact, pre_act)
    grad_pre = pull(grad_act)[0].astype(jnp.bfloat16)
    grad_hidden = back_product(grad_pre, w_in)
    return (
        grad_hidden,
        (hidden_low, grad_pre, activated, grad_low),
        column_sum(grad_pre),
        column_sum(grad_low),
    )


def encoder_forward(hidden, w_in, w_out, b_in, section_bias, gain_last, w_ck, w_cv, bias_cv):
    branch, kept = ffn_forward(hidden, w_in, w_out, b_in, section_bias[4])
    resid = hidden + branch
    memory = norm_rows(resid, gain_last, section_bias[5]).astype(jnp.bfloat16)
    key_rows = product(memory, w_ck).astype(jnp.bfloat16)
    value_rows = (product(memory, w_cv) + bias_cv).astype(jnp.bfloat16)
    return (memory, key_rows, value_rows, resid, kept)


def encoder_backward(
    w_in, w_out, section_bias, gain_last, w_ck, w_cv, memory, resid, kept, grad_keys, grad_values
):
    grad_memory = back_product(grad_keys, w_ck) + back_product(grad_values, w_cv)
    grad_last, grad_gain, grad_shift = norm_back(resid, gain_last, section_bias[5], grad_memory)
    grad_ffn, ffn_ops, grad_bin, grad_bout = ffn_backward(w_in, w_out, kept, grad_last)
    zero_line = jnp.zeros_like(grad_gain)
    cross_rows = jnp.stack([zero_line, column_sum(grad_values), zero_line, zero_line])
    operands = (memory, grad_keys, memory, grad_values) + ffn_ops
    return (
        grad_last + grad_ffn,
        operands,
        grad_bin,
        grad_bout,
        grad_gain,
        grad_shift,
        cross_rows,
        zero_line,
    )


def decoder_step(
    hidden,
    w_cq,
    w_co,
    w_in,
    w_out,
    b_in,
    section_bias,
    gain_last,
    gain_cross,
    cross_bias,
    key_rows,
    value_rows,
    allowed,
    cotangent,
    head_count,
):
    hidden_low = hidden.astype(jnp.bfloat16)
    query = (product(hidden_low, w_cq) + cross_bias[0]).astype(jnp.bfloat16)
    mixed, log_total = attend(query, key_rows, value_rows, allowed, head_count)
    mixed = mixed.astype(jnp.bfloat16)
    resid_mid = hidden + product(mixed, w_co) + cross_bias[2]
    middle = norm_rows(resid_mid, gain_cross, cross_bias[3])
    branch, kept = ffn_forward(middle, w_in, w_out, b_in, section_bias[4])
    resid_last = middle + branch
    result = norm_rows(resid_last, gain_last, section_bias[5])
    grad_last, grad_gain, grad_shift = norm_back(
        resid_last, gain_last, section_bias[5], cotangent.astype(jnp.float32)
    )
    grad_ffn, ffn_ops, grad_bin, grad_bout = ffn_backward(w_in, w_out, kept, grad_last)
    grad_mid, grad_gain_cross, grad_shift_cross = norm_back(
        resid_mid, gain_cross, cross_bias[3], grad_last + grad_ffn
    )
    grad_branch = grad_mid.astype(jnp.bfloat16)
    grad_mixed = back_product(grad_branch, w_co).astype(jnp.bfloat16)
    grad_query, grad_keys, grad_values = attend_back(
        query, key_rows, value_rows, allowed, log_total, grad_mixed, head_count
    )
    grad_query = grad_query.astype(jnp.bfloat16)
    grad_hidden = grad_mid + back_product(grad_query, w_cq)
    cross_rows = jnp.stack(
        [
            column_sum(grad_query),
            jnp.zeros_like(grad_gain),
            column_sum(grad_branch),
            grad_shift_cross,
        ]
    )
    operands = (hidden_low, grad_query, mixed, grad_branch) + ffn_ops
    tail_result = (
        grad_hidden,
        operands,
        grad_bin,
        grad_bout,
        grad_gain,
        grad_shift,
        cross_rows,
        grad_gain_cross,
    )
    return (
        result.astype(jnp.bfloat16),
        grad_keys.astype(jnp.bfloat16),
        grad_values.astype(jnp.bfloat16),
        tail_result,
    )


def zero_tail(hidden, w_in):
    model_width = hidden.shape[-1]
    ffn_width = w_in.shape[1]
    flat = jnp.zeros(hidden.shape, jnp.bfloat16)
    wide = jnp.zeros((hidden.shape[0], hidden.shape[1], ffn_width), jnp.bfloat16)
    zero_line = jnp.zeros((model_width,), jnp.float32)
    operands = (flat, flat, flat, flat, flat, wide, wide, flat)
    return (
        jnp.zeros_like(hidden),
        operands,
        jnp.zeros((ffn_width,), jnp.float32),
        zero_line,
        zero_line,
        zero_line,
        jnp.zeros((4, model_width), jnp.float32),
        zero_line,
    )


def tail_whole(operands):
    return (
        weight_grad(operands[0], operands[1]),
        weight_grad(operands[2], operands[3]),
        weight_grad(operands[4], operands[5]),
        weight_grad(operands[6], operands[7]),
    )


def self_whole(operands):
    grad_qk = weight_grad(operands[0], operands[1])
    grad_vo = jnp.concatenate(
        [weight_grad(operands[0], operands[2]), weight_grad(operands[3], operands[4])], axis=1
    )
    return (grad_qk, grad_vo)


def local_any(
    tokens,
    segments,
    cotangent,
    attn_qk,
    attn_vo,
    cross_qk,
    cross_vo,
    ffn_in,
    ffn_out,
    gains,
    biases,
    ffn_bias,
):
    head_count = HEADS
    section_index = lax.axis_index("section")
    is_enc = section_index == 0
    qk_whole, vo_whole = (
        lax.all_gather(attn_qk, "dp", axis=1, tiled=True),
        lax.all_gather(attn_vo, "dp", axis=1, tiled=True),
    )
    w_qk = qk_whole[0]
    w_vo = vo_whole[0]
    cqk_whole, cvo_whole, in_whole, out_whole = (
        lax.all_gather(cross_qk, "dp", axis=1, tiled=True),
        lax.all_gather(cross_vo, "dp", axis=1, tiled=True),
        lax.all_gather(ffn_in, "dp", axis=1, tiled=True),
        lax.all_gather(ffn_out, "dp", axis=1, tiled=True),
    )
    w_cqk = cqk_whole[0]
    w_cvo = cvo_whole[0]
    w_in = in_whole[0]
    w_out = out_whole[0]
    section_bias = lax.dynamic_slice_in_dim(biases, 6 * section_index, 6, 0)
    section_gain = lax.dynamic_slice_in_dim(gains, 2 * section_index, 2, 0)
    bias_in = lax.dynamic_index_in_dim(ffn_bias, section_index, 0, keepdims=False)
    section_seg = lax.dynamic_index_in_dim(segments, section_index, 0, keepdims=False)
    length = tokens.shape[2]
    position = jnp.arange(length)
    earlier = position[None, :] <= position[:, None]
    allowed_self = (section_seg[:, :, None] == section_seg[:, None, :]) & (earlier[None] | is_enc)
    allowed_cross = segments[1][:, :, None] == segments[0][:, None, :]
    source = tokens[0]
    hidden_one, kept_self = self_forward(
        source, w_qk, w_vo, section_bias, section_gain[0], allowed_self, head_count
    )

    def run_encoder():
        return encoder_forward(
            hidden_one,
            w_in,
            w_out,
            bias_in,
            section_bias,
            section_gain[1],
            w_cqk,
            w_cvo,
            biases[13],
        )

    def skip_encoder():
        flat = jnp.zeros(hidden_one.shape, jnp.bfloat16)
        wide_shape = (hidden_one.shape[0], hidden_one.shape[1], w_in.shape[1])
        return (
            flat,
            flat,
            flat,
            jnp.zeros_like(hidden_one),
            (flat, jnp.zeros(wide_shape, jnp.float32), jnp.zeros(wide_shape, jnp.bfloat16)),
        )

    memory, enc_keys, enc_values, enc_resid, enc_kept = lax.cond(is_enc, run_encoder, skip_encoder)
    got_keys, got_values = from_behind((enc_keys, enc_values), "section", 1)

    def run_decoder():
        return decoder_step(
            hidden_one,
            w_cqk,
            w_cvo,
            w_in,
            w_out,
            bias_in,
            section_bias,
            section_gain[1],
            gains[4],
            biases[12:16],
            got_keys,
            got_values,
            allowed_cross,
            cotangent,
            head_count,
        )

    def skip_decoder():
        flat = jnp.zeros(hidden_one.shape, jnp.bfloat16)
        return (flat, flat, flat, zero_tail(hidden_one, w_in))

    decoded, grad_keys, grad_values, dec_tail = lax.cond(is_enc, skip_decoder, run_decoder)
    back_keys, back_values = from_behind((grad_keys, grad_values), "section", -1)

    def run_encoder_back():
        return encoder_backward(
            w_in,
            w_out,
            section_bias,
            section_gain[1],
            w_cqk,
            w_cvo,
            memory,
            enc_resid,
            enc_kept,
            back_keys,
            back_values,
        )

    def keep_decoder():
        return dec_tail

    tail_result = lax.cond(is_enc, run_encoder_back, keep_decoder)
    (
        grad_hidden,
        tail_ops,
        grad_bin,
        grad_bout,
        grad_gain_last,
        grad_shift_last,
        cross_rows,
        grad_gain_cross,
    ) = tail_result
    layer_out = jnp.where(is_enc, memory, decoded)
    model_width = source.shape[-1]
    grad_ca, grad_cb, grad_in, grad_out = tail_whole(tail_ops)
    tail_parts = (
        lax.psum_scatter(grad_ca[None], "dp", scatter_dimension=1, tiled=True),
        lax.psum_scatter(grad_cb[None], "dp", scatter_dimension=1, tiled=True),
        lax.psum_scatter(grad_in[None], "dp", scatter_dimension=1, tiled=True),
        lax.psum_scatter(grad_out[None], "dp", scatter_dimension=1, tiled=True),
    )
    grad_source, self_ops, self_rows, grad_gain_first = self_backward(
        source,
        w_qk,
        w_vo,
        section_bias,
        section_gain[0],
        allowed_self,
        head_count,
        kept_self,
        grad_hidden,
    )
    grad_qk, grad_vo = self_whole(self_ops)
    attn_parts = (
        lax.psum_scatter(grad_qk[None], "dp", scatter_dimension=1, tiled=True),
        lax.psum_scatter(grad_vo[None], "dp", scatter_dimension=1, tiled=True),
    )
    large_parts = tuple(attn_parts) + tuple(tail_parts)
    section_rows = jnp.concatenate([self_rows, jnp.stack([grad_bout, grad_shift_last])], axis=0)
    bias_block = lax.dynamic_update_slice_in_dim(
        jnp.zeros((12, model_width), jnp.float32), section_rows, 6 * section_index, 0
    )
    grad_biases = jnp.concatenate([bias_block, cross_rows], axis=0)
    gain_block = lax.dynamic_update_slice_in_dim(
        jnp.zeros((4, model_width), jnp.float32),
        jnp.stack([grad_gain_first, grad_gain_last]),
        2 * section_index,
        0,
    )
    grad_gains = jnp.concatenate([gain_block, grad_gain_cross[None]], axis=0)
    grad_fbias = lax.dynamic_update_slice_in_dim(
        jnp.zeros_like(ffn_bias), grad_bin[None], section_index, 0
    )
    sum_gains, sum_biases, sum_fbias = lax.psum(
        (grad_gains, grad_biases, grad_fbias), ("section", "dp")
    )
    return (
        layer_out[None],
        grad_source[None],
        large_parts[0],
        large_parts[1],
        large_parts[2],
        large_parts[3],
        large_parts[4],
        large_parts[5],
        sum_gains,
        sum_biases,
        sum_fbias,
    )


MESH = pl.DeviceIdType.MESH
LOW = jnp.bfloat16
CHIPS = 8
FAR = 3
MASKED = -1e30


class Place:
    def __init__(self):
        self.section = lax.axis_index("section")
        shard = lax.axis_index("dp")
        self.core = shard % 2
        self.chip = shard // 2
        self.across = self.chip % 2
        self.along = self.chip // 2
        self.pos = self.along + self.across * (7 - 2 * self.along)

    def chip_at(self, step):
        spot = (self.pos + step + CHIPS) % CHIPS
        across = spot // 4
        along = spot + across * (7 - 2 * spot)
        return along * 2 + across

    def ring(self, step):
        return (self.section, self.chip_at(step) * 2 + self.core)

    def sibling(self):
        return (self.section, self.chip * 2 + 1 - self.core)

    def peer(self):
        return (1 - self.section, self.chip * 2 + self.core)

    def folds(self):
        near = self.along + 1 - 2 * (self.along % 2)
        far = (self.along + 2) % 4
        return (
            self.sibling(),
            (self.section, (self.along * 2 + 1 - self.across) * 2 + self.core),
            (self.section, (near * 2 + self.across) * 2 + self.core),
            (self.section, (far * 2 + self.across) * 2 + self.core),
            self.peer(),
        )


def enter(place):
    barrier = pltpu.get_barrier_semaphore()
    others = (place.ring(1), place.ring(-1)) + place.folds()
    for other in others:
        pl.semaphore_signal(barrier, inc=1, device_id=other, device_id_type=MESH)
    pl.semaphore_wait(barrier, len(others))


class Piece:
    def __init__(self, ref, by_rows, low, span, slot):
        self.ref, self.by_rows, self.low, self.span, self.slot = ref, by_rows, low, span, slot

    def at(self, chip, core, half=None):
        low, span = self.low, self.span
        if half is not None:
            span = span // 2
            low = low + half * span
        if self.by_rows:
            return self.ref.at[chip, core, low : low + span, :]
        return self.ref.at[chip, core, :, low : low + span]


def piece_list(qk, vo, w_in, w_out, cross):
    return [
        Piece(qk, False, 0, 1536, 0),
        Piece(vo, False, 0, 1536, 1),
        Piece(w_in, False, 0, 1536, 2),
        Piece(w_in, False, 1536, 1536, 3),
        Piece(w_out, True, 0, 96, 0),
        Piece(w_out, True, 96, 96, 1),
        Piece(cross, False, 0, 1536, 4),
        Piece(cross, False, 1536, 1536, 5),
    ]


class Gather:
    def __init__(self, place, pieces, ring_send, ring_recv, side_send, side_recv):
        self.place, self.pieces = place, pieces
        self.ring_send, self.ring_recv, self.side_send, self.side_recv = ring_send, ring_recv, side_send, side_recv

    def ring_copy(self, p, way, hop):
        sign = 1 - 2 * way
        ref = self.pieces[p].at(self.place.chip_at(-sign * hop), self.place.core, way if hop == FAR else None)
        return pltpu.make_async_remote_copy(
            ref, ref, self.ring_send.at[p, way, hop], self.ring_recv.at[p, way, hop],
            device_id=self.place.ring(sign), device_id_type=MESH,
        )

    def arrival(self, p, way, hop, core):
        sign = 1 - 2 * way
        return self.pieces[p].at(self.place.chip_at(-sign * (hop + 1)), core, way if hop == FAR else None)

    def side_copy(self, p, k, core):
        if k == 0:
            ref = self.pieces[p].at(self.place.chip, core)
        else:
            ref = self.arrival(p, (k - 1) // 4, (k - 1) % 4, core)
        return pltpu.make_async_remote_copy(
            ref, ref, self.side_send.at[p, k], self.side_recv.at[p, k],
            device_id=self.place.sibling(), device_id_type=MESH,
        )

    def start(self, p):
        self.ring_copy(p, 0, 0).start()
        self.ring_copy(p, 1, 0).start()
        self.side_copy(p, 0, self.place.core).start()

    def event(self, p, way, hop):
        ref = self.arrival(p, way, hop, self.place.core)
        pltpu.make_async_remote_copy(
            ref, ref, self.ring_send.at[p, way, hop], self.ring_recv.at[p, way, hop],
            device_id=self.place.ring(1), device_id_type=MESH,
        ).wait_recv()
        if hop < FAR:
            self.ring_copy(p, way, hop + 1).start()
        self.side_copy(p, 1 + 4 * way + hop, self.place.core).start()

    def side_arrivals(self, p):
        for k in range(9):
            self.side_copy(p, k, 1 - self.place.core).wait_recv()

    def finish(self, p):
        for way in range(2):
            for hop in range(4):
                self.ring_copy(p, way, hop).wait_send()
        for k in range(9):
            self.side_copy(p, k, self.place.core).wait_send()

    def steps(self, pair, then):
        found = []
        for hop in range(4):
            for i, p in enumerate(pair):
                for way in range(2):
                    found.append(functools.partial(self.event, p, way, hop))
                if hop == 2 and i < len(then):
                    found.append(functools.partial(self.start, then[i]))
        return found


class Scatter:
    def __init__(self, place, pieces, side_c, side_r, land_c, land_r, near_c, near_r, ring_send, ring_recv, side_send, side_recv):
        self.place, self.pieces = place, pieces
        self.side_c, self.side_r, self.land_c, self.land_r = side_c, side_r, land_c, land_r
        self.near_c, self.near_r = near_c, near_r
        self.ring_send, self.ring_recv, self.side_send, self.side_recv = ring_send, ring_recv, side_send, side_recv

    def cut(self, p, ref, half):
        piece = self.pieces[p]
        if half is None:
            return ref
        span = piece.span // 2
        if piece.by_rows:
            return ref.at[half * span : (half + 1) * span, :]
        return ref.at[:, half * span : (half + 1) * span]

    def from_side(self, p, chip, half=None):
        piece = self.pieces[p]
        return self.cut(p, (self.side_r if piece.by_rows else self.side_c).at[piece.slot, chip], half)

    def landed(self, p, way, step, half=None):
        piece = self.pieces[p]
        if step == 0:
            return (self.near_r if piece.by_rows else self.near_c).at[piece.slot, way]
        return self.cut(p, (self.land_r if piece.by_rows else self.land_c).at[piece.slot, way, step - 1], half)

    def side_copy(self, p):
        piece = self.pieces[p]
        span = slice(piece.low, piece.low + piece.span)
        other = 1 - self.place.core
        src = piece.ref.at[:, other, span, :] if piece.by_rows else piece.ref.at[:, other, :, span]
        dst = (self.side_r if piece.by_rows else self.side_c).at[piece.slot]
        return pltpu.make_async_remote_copy(
            src, dst, self.side_send.at[p], self.side_recv.at[p],
            device_id=self.place.sibling(), device_id_type=MESH,
        )

    def chip_of(self, way, step):
        sign = 1 - 2 * way
        return self.place.chip_at(sign * (4 - step))

    def ring_copy(self, p, way, step):
        sign = 1 - 2 * way
        half = way if step == 0 else None
        return pltpu.make_async_remote_copy(
            self.pieces[p].at(self.chip_of(way, step), self.place.core, half), self.landed(p, way, step, half),
            self.ring_send.at[p, way, step], self.ring_recv.at[p, way, step],
            device_id=self.place.ring(sign), device_id_type=MESH,
        )

    def hand_over(self, p):
        self.side_copy(p).start()

    def start(self, p):
        self.side_copy(p).wait_recv()
        for way in range(2):
            chip = self.chip_of(way, 0)
            own = self.pieces[p].at(chip, self.place.core, way)
            total = own[...].astype(jnp.float32) + self.from_side(p, chip, way)[...].astype(jnp.float32)
            own[...] = total.astype(LOW)
            self.ring_copy(p, way, 0).start()

    def event(self, p, way, step):
        self.ring_copy(p, way, step).wait_recv()
        chip = self.chip_of(way, step + 1)
        for half in range(2):
            own = self.pieces[p].at(chip, self.place.core, half)
            total = own[...].astype(jnp.float32) + self.from_side(p, chip, half)[...].astype(jnp.float32)
            if step > 0 or half == way:
                total = total + self.landed(p, way, step, half)[...].astype(jnp.float32)
            own[...] = total.astype(LOW)
        self.ring_copy(p, way, step + 1).start()

    def last(self, p):
        chip = self.place.chip
        total = self.pieces[p].at(chip, self.place.core)[...].astype(jnp.float32)
        total = total + self.from_side(p, chip)[...].astype(jnp.float32)
        for way in range(2):
            self.ring_copy(p, way, 3).wait_recv()
            total = total + self.landed(p, way, 3)[...].astype(jnp.float32)
        return total

    def finish(self, p):
        self.side_copy(p).wait_send()
        for way in range(2):
            for step in range(4):
                self.ring_copy(p, way, step).wait_send()

    def steps(self, pair, then, after):
        found = []
        for step in range(3):
            for i, p in enumerate(pair):
                for way in range(2):
                    found.append(functools.partial(self.event, p, way, step))
                if step == 2 and i < len(then):
                    found.append(functools.partial(self.start, then[i]))
        for p in pair:
            found.append(functools.partial(after, p))
        return found


def serve(queue, count=None):
    for _ in range(len(queue) if count is None else min(count, len(queue))):
        queue.pop(0)()


def nn(left, right):
    return jnp.dot(left, right, preferred_element_type=jnp.float32)


def nt(left, right):
    return lax.dot_general(left, right, (((1,), (1,)), ((), ())), preferred_element_type=jnp.float32)


def tn(left, right):
    return lax.dot_general(left, right, (((0,), (0,)), ((), ())), preferred_element_type=jnp.float32)


def tiles(low, high, body):
    def step(j, carry):
        body(j)
        return carry

    lax.fori_loop(low, high, step, 0)


def span_of(j, width):
    return pl.ds(pl.multiple_of(j * width, width), width)


def columns_of(ref, at):
    block = ref[:, :, :, at]
    return block.reshape(block.shape[0] * block.shape[1] * block.shape[2], block.shape[3])


def head_masks(length, value):
    lane = lax.broadcasted_iota(jnp.int32, (length, 128), 1)
    first = jnp.where(lane < 64, value, 0.0).astype(LOW)
    second = jnp.where(lane < 64, 0.0, value).astype(LOW)
    return first, second


def mask_scores(bias_ref, key_row, query_row, causal):
    length = bias_ref.shape[0]
    keys = jnp.transpose(jnp.broadcast_to(key_row.astype(jnp.float32), (128, length)))
    keys = jnp.concatenate([keys] * (length // 128), axis=1)
    same = keys == jnp.broadcast_to(query_row.astype(jnp.float32), (length, length))
    if causal:
        key_at = lax.broadcasted_iota(jnp.int32, (length, length), 0)
        query_at = lax.broadcasted_iota(jnp.int32, (length, length), 1)
        same = same & (key_at <= query_at)
    bias_ref[...] = jnp.where(same, 0.0, MASKED)


def attend_pairs(q_ref, k_ref, v_ref, bias_ref, o_ref, lse_ref, p_ref, low, high):
    masks = head_masks(q_ref.shape[0], 0.125)

    def pair(i):
        at = span_of(i, 128)
        q2, k2 = q_ref[:, at], k_ref[:, at]
        v_turned = jnp.transpose(v_ref[:, at])
        parts = []
        for h in range(2):
            scores = nt(k2 * masks[h], q2) + bias_ref[...]
            peak = jnp.max(scores, axis=0, keepdims=True)
            exponent = jnp.exp(scores - peak)
            summed = jnp.sum(exponent, axis=0, keepdims=True)
            soft = (exponent * (1.0 / summed)).astype(LOW)
            if p_ref is not None:
                p_ref[2 * i + h] = soft
            if lse_ref is not None:
                lse_ref[2 * i + h] = peak + jnp.log(summed)
            parts.append(nn(v_turned[64 * h : 64 * h + 64], soft))
        o_ref[:, at] = jnp.transpose(jnp.concatenate(parts, axis=0)).astype(LOW)

    tiles(low, high, pair)


def attend_back_pairs(q_ref, k_ref, v_ref, bias_ref, lse_ref, p_ref, do_ref, low, high):
    masks = head_masks(q_ref.shape[0], 0.125)
    ones = head_masks(q_ref.shape[0], 1.0)

    def pair(i):
        at = span_of(i, 128)
        q2, k2, v2, do2 = q_ref[:, at], k_ref[:, at], v_ref[:, at], do_ref[:, at]
        k_turned = jnp.transpose(k2)
        parts = []
        dk = dv = None
        for h in range(2):
            if p_ref is not None:
                low_soft = p_ref[2 * i + h]
                soft = low_soft.astype(jnp.float32)
            else:
                soft = jnp.exp(nt(k2 * masks[h], q2) + bias_ref[...] - lse_ref[2 * i + h])
                low_soft = soft.astype(LOW)
            dv_h = nn(low_soft, do2 * ones[h])
            d_soft = nt(v2 * ones[h], do2)
            inner = jnp.sum(soft * d_soft, axis=0, keepdims=True)
            d_scores = (soft * (d_soft - inner)).astype(LOW)
            dk_h = nn(d_scores, q2 * masks[h])
            parts.append(nn(k_turned[64 * h : 64 * h + 64], d_scores))
            dk = dk_h if dk is None else dk + dk_h
            dv = dv_h if dv is None else dv + dv_h
        q_ref[:, at] = (jnp.transpose(jnp.concatenate(parts, axis=0)) * 0.125).astype(LOW)
        k_ref[:, at] = dk.astype(LOW)
        v_ref[:, at] = dv.astype(LOW)

    tiles(low, high, pair)


def gelu_parts(u):
    size = jnp.abs(u)
    bell = jnp.exp(-0.5 * u * u)
    t = 1.0 / (1.0 + 0.2316419 * size)
    tail = t * (0.127414796 + t * (-0.142248368 + t * (0.710706870 + t * (-0.726576013 + t * 0.530702714)))) * bell
    upper = jnp.where(u < 0, tail, 1.0 - tail)
    return u * upper, upper + u * bell * 0.3989422804014327


def norm_pass(norm_ref, rstd_ref, gain, shift, hidden_ref, low_ref):
    def rows(j):
        at = span_of(j, 64)
        resid = norm_ref[at, :]
        center = resid - jnp.mean(resid, axis=-1, keepdims=True)
        rstd = lax.rsqrt(jnp.mean(center * center, axis=-1, keepdims=True) + NORM_EPSILON)
        normal = center * rstd
        norm_ref[at, :] = normal
        rstd_ref[at, :] = rstd
        result = normal * gain + shift
        if hidden_ref is not None:
            hidden_ref[at, :] = result
        low_ref[at, :] = result.astype(LOW)

    tiles(0, norm_ref.shape[0] // 64, rows)


def norm_undo(norm_ref, rstd_ref, gain, source_ref, grad_ref, low_ref):
    width = norm_ref.shape[1]

    def rows(j, carry):
        d_gain, d_shift, d_low = carry
        at = span_of(j, 64)
        dy = source_ref[at, :].astype(jnp.float32)
        normal = norm_ref[at, :]
        scaled = dy * gain
        mean = jnp.mean(scaled, axis=-1, keepdims=True)
        along = jnp.mean(scaled * normal, axis=-1, keepdims=True)
        d_resid = rstd_ref[at, :] * (scaled - mean - normal * along)
        grad_ref[at, :] = d_resid
        low = d_resid.astype(LOW)
        low_ref[at, :] = low
        return (
            d_gain + jnp.sum(dy * normal, axis=0, keepdims=True),
            d_shift + jnp.sum(dy, axis=0, keepdims=True),
            d_low + jnp.sum(low.astype(jnp.float32), axis=0, keepdims=True),
        )

    zero = jnp.zeros((1, width), jnp.float32)
    return lax.fori_loop(0, norm_ref.shape[0] // 64, rows, (zero, zero, zero))


def column_total(ref):
    return jnp.sum(ref[...].astype(jnp.float32), axis=0, keepdims=True)


def layer_kernel(
    tokens, segments, gains, biases, ffn_bias, cotangent, s_qk, s_vo, s_cqk, s_cvo, s_in, s_out,
    out_layer, out_input, out_qk, out_vo, out_cqk, out_cvo, out_in, out_out, out_small,
    w_qk, w_vo, w_in, w_out, w_x,
    side_c, side_r, land_c, land_r, near_c, near_r, x_land, small, small_land,
    sec_bias, sec_gain, sec_fbias, b1_rows,
    q, k, v, o, h_low, norm_a, h, act, slope, norm_f, d_ffn, score_bias, x_send, x_recv,
    qc, kc, vc, p_c, oc, h2_low, norm_c, d_branch, d_mixed, grad, lse, rstd_a, rstd_f, rstd_c,
    load_sem, peer_send, peer_recv, rs, rr, ss, sr, rs2, rr2, ss2, sr2, fold_send, fold_recv, out_sem,
):
    place = Place()
    chip, core = place.chip, place.core
    width = tokens.shape[-1]
    encoder, decoder = place.section == 0, place.section == 1
    x = tokens.at[0, 0]
    loads = [
        pltpu.make_async_copy(src.at[0], dst.at[chip, core], load_sem.at[i])
        for i, (src, dst) in enumerate([(s_qk, w_qk), (s_vo, w_vo), (s_in, w_in), (s_out, w_out)])
    ]
    for copy in loads:
        copy.start()
    enter(place)
    own_cross = [
        pltpu.make_async_copy(src.at[0], w_x.at[chip, core, :, i * width : (i + 1) * width], load_sem.at[4 + i])
        for i, src in enumerate([s_cqk, s_cvo])
    ]
    from_encoder = [
        pltpu.make_async_remote_copy(
            src.at[0], w_x.at[chip, core, :, (2 + i) * width : (3 + i) * width], peer_send.at[i], peer_recv.at[i],
            device_id=place.peer(), device_id_type=MESH,
        )
        for i, src in enumerate([s_cqk, s_cvo])
    ]
    pieces = piece_list(w_qk, w_vo, w_in, w_out, w_x)
    gather = Gather(place, pieces, rs, rr, ss, sr)
    scatter = Scatter(place, pieces, side_c, side_r, land_c, land_r, near_c, near_r, rs2, rr2, ss2, sr2)
    for copy in loads:
        copy.wait()
    gather.start(0)
    gather.start(1)
    cot_load = pltpu.make_async_copy(cotangent, d_mixed, load_sem.at[6])

    @pl.when(encoder)
    def _():
        for copy in from_encoder:
            copy.start()
        sec_bias[0:6] = biases[0:6]
        sec_gain[0:1] = gains[0:1]
        sec_fbias[...] = ffn_bias[0:1]
        mask_scores(score_bias, segments[0], segments[0], False)

    @pl.when(decoder)
    def _():
        for copy in own_cross:
            copy.start()
        cot_load.start()
        sec_bias[0:6] = biases[6:12]
        sec_gain[0:1] = gains[2:3]
        sec_fbias[...] = ffn_bias[1:2]
        mask_scores(score_bias, segments[1], segments[1], True)

    small[...] = jnp.zeros_like(small)
    shared = gather.steps((0, 1), (2, 3))
    serve(shared)
    gather.side_arrivals(0)
    gather.side_arrivals(1)
    shared = gather.steps((2, 3), (4, 5))

    def project(j):
        at = span_of(j, 256)
        past = pl.ds(pl.multiple_of(width + j * 256, 256), 256)
        q[:, at] = (nn(x[...], columns_of(w_qk, at)) + sec_bias[0:1, at]).astype(LOW)
        k[:, at] = nn(x[...], columns_of(w_qk, past)).astype(LOW)
        v[:, at] = (nn(x[...], columns_of(w_vo, at)) + sec_bias[1:2, at]).astype(LOW)

    tiles(0, 3, project)
    serve(shared, 4)
    attend_pairs(q, k, v, score_bias, o, lse, None, 0, 3)
    serve(shared, 2)
    attend_pairs(q, k, v, score_bias, o, lse, None, 3, 6)
    serve(shared, 2)

    def self_out(j):
        at = span_of(j, 256)
        past = pl.ds(pl.multiple_of(width + j * 256, 256), 256)
        norm_a[:, at] = x[:, at].astype(jnp.float32) + nn(o[...], columns_of(w_vo, past)) + sec_bias[2:3, at]

    tiles(0, 3, self_out)
    norm_pass(norm_a, rstd_a, sec_gain[0:1], sec_bias[3:4], h, h_low)

    def ffn_up(low_ref, low, high):
        def tile(j):
            at = span_of(j, 256)
            u = nn(low_ref[...], columns_of(w_in, at)) + sec_fbias[:, at]
            value, rise = gelu_parts(u)
            act[:, at] = value.astype(LOW)
            slope[:, at] = rise.astype(LOW)

        tiles(low, high, tile)

    def ffn_down():
        def tile(j):
            at = span_of(j, 256)
            norm_f[:, at] = h[:, at] + nn(act[...], columns_of(w_out, at)) + sec_bias[4:5, at]

        tiles(0, 3, tile)

    def ffn_slope():
        def tile(j):
            at = span_of(j, width)
            block = w_out[pl.ds(2 * j, 2)].reshape(width, width)
            d_pre = (nt(d_ffn[...], block) * slope[:, at].astype(jnp.float32)).astype(LOW)
            slope[:, at] = d_pre
            b1_rows[j] = jnp.sum(d_pre.astype(jnp.float32), axis=0, keepdims=True)

        tiles(0, 4, tile)

    def ffn_hidden():
        def tile(j):
            at = span_of(j, width)
            grad[...] += nt(slope[:, at], columns_of(w_in, at))

        tiles(0, 4, tile)

    def grad_w_out():
        def tile(c):
            block = tn(act[:, span_of(c, 384)], d_ffn[...])
            w_out[c] = block.astype(LOW).reshape(2, 192, width)

        tiles(0, CHIPS, tile)

    def store(ref, at, value):
        ref[:, :, :, at] = value.astype(LOW).reshape(CHIPS, 2, 48, value.shape[1])

    def grad_w_in(low_ref):
        def tile(j):
            at = span_of(j, width)
            store(w_in, at, tn(low_ref[...], slope[:, at]))

        tiles(0, 4, tile)

    def set_small(row, value):
        small[row : row + 1, :] = value

    def set_b1(section):
        for j in range(4):
            set_small(21 + 4 * section + j, b1_rows[j])

    def self_back_a(section):
        gain, shift, branch = norm_undo(norm_a, rstd_a, sec_gain[0:1], grad, grad, d_branch)
        set_small(2 * section, gain)
        set_small(5 + 6 * section + 3, shift)
        set_small(5 + 6 * section + 2, branch)
        d_mixed[...] = nt(d_branch[...], columns_of(w_vo, slice(width, 2 * width))).astype(LOW)

    def self_back_b(section):
        set_small(5 + 6 * section, column_total(q))
        set_small(5 + 6 * section + 1, column_total(v))
        grad[...] += nt(q[...], columns_of(w_qk, slice(0, width)))
        grad[...] += nt(k[...], columns_of(w_qk, slice(width, 2 * width)))
        grad[...] += nt(v[...], columns_of(w_vo, slice(0, width)))
        pltpu.make_async_copy(grad, out_input.at[0, 0], out_sem.at[1]).start()

    def self_back_qk():
        store(w_qk, slice(0, width), tn(x[...], q[...]))
        store(w_qk, slice(width, 2 * width), tn(x[...], k[...]))

    def self_back_vo():
        store(w_vo, slice(0, width), tn(x[...], v[...]))
        store(w_vo, slice(width, 2 * width), tn(o[...], d_branch[...]))

    def result_at(p):
        holder = norm_f if p < 4 else norm_c
        return holder.at[96 * (p % 4) : 96 * (p % 4) + 96, :]

    def out_copies(p, half):
        source = result_at(p)
        if p in (4, 5):
            return pltpu.make_async_copy(
                source.at[48 * half : 48 * half + 48],
                out_out.at[0, 96 * (p - 4) + 48 * half : 96 * (p - 4) + 48 * half + 48, :],
                out_sem.at[2 + 2 * p + half],
            )
        target, first = {0: (out_qk, 0), 1: (out_vo, 0), 2: (out_in, 0), 3: (out_in, 1536)}[p] if p < 4 else (
            (out_cqk, out_cvo)[half], -width * half
        )
        low = first + width * half
        if p == 7:
            source = x_land
        return pltpu.make_async_copy(
            source.at[48 * half : 48 * half + 48], target.at[0, :, low : low + width], out_sem.at[2 + 2 * min(p, 6) + half]
        )

    def finish_piece(p):
        total = scatter.last(p)
        target = result_at(p)
        if p in (4, 5):
            target[...] = total
        else:
            target[0:48] = total[:, :width]
            target[48:96] = total[:, width:]
        if p == 7:
            to_encoder.start()
        else:
            out_copies(p, 0).start()
            out_copies(p, 1).start()

    to_encoder = pltpu.make_async_remote_copy(
        result_at(7), x_land, peer_send.at[3], peer_recv.at[3], device_id=place.peer(), device_id_type=MESH
    )
    cross_copy = pltpu.make_async_remote_copy(
        x_send, x_recv, peer_send.at[2], peer_recv.at[2], device_id=place.peer(), device_id_type=MESH
    )
    layer_copy = pltpu.make_async_copy(x_send, out_layer.at[0, 0], out_sem.at[0])

    def fold(i):
        return pltpu.make_async_remote_copy(
            small, small_land.at[i], fold_send.at[i], fold_recv.at[i], device_id=place.folds()[i], device_id_type=MESH
        )

    def fold_start(i):
        fold(i).start()

    def fold_end(i):
        fold(i).wait()
        small[...] = small[...] + small_land[i]
        if i < 4:
            fold(i + 1).start()

    @pl.when(encoder)
    def _():
        queue = list(shared) + gather.steps((4, 5), ())
        serve(queue, len(shared))
        gather.side_arrivals(2)
        gather.side_arrivals(3)
        for part in range(4):
            ffn_up(h_low, 3 * part, 3 * part + 3)
            serve(queue, 4 if part < 3 else None)
        gather.side_arrivals(4)
        gather.side_arrivals(5)
        ffn_down()
        norm_pass(norm_f, rstd_f, gains[1:2], biases[5:6], None, x_send)
        cross_copy.start()
        layer_copy.start()
        for copy in from_encoder:
            copy.wait_send()
        for p in range(6):
            gather.finish(p)
        layer_copy.wait()
        cross_copy.wait()

        gain, shift, branch = norm_undo(norm_f, rstd_f, gains[1:2], x_recv, grad, d_ffn)
        set_small(1, gain)
        set_small(5 + 5, shift)
        set_small(5 + 4, branch)
        ffn_slope()
        grad_w_out()
        scatter.hand_over(4)
        scatter.hand_over(5)
        ffn_hidden()
        scatter.start(4)
        scatter.start(5)
        grad_w_in(h_low)
        scatter.hand_over(2)
        scatter.hand_over(3)
        set_b1(0)
        queue = scatter.steps((4, 5), (2, 3), finish_piece)
        serve(queue, 2)
        self_back_a(0)
        serve(queue, 2)
        attend_back_pairs(q, k, v, score_bias, lse, None, d_mixed, 0, 3)
        serve(queue, 4)
        attend_back_pairs(q, k, v, score_bias, lse, None, d_mixed, 3, 6)
        serve(queue, 4)
        self_back_b(0)
        fold_start(0)
        serve(queue)
        queue = scatter.steps((2, 3), (0, 1), finish_piece)
        self_back_qk()
        scatter.hand_over(0)
        self_back_vo()
        scatter.hand_over(1)
        fold_end(0)
        serve(queue, 4)
        fold_end(1)
        serve(queue, 4)
        fold_end(2)
        serve(queue)
        fold_end(3)
        serve(scatter.steps((0, 1), (), finish_piece))
        to_encoder.wait_recv()
        out_copies(7, 0).start()
        out_copies(7, 1).start()

    @pl.when(decoder)
    def _():
        for copy in own_cross:
            copy.wait()
        for copy in from_encoder:
            copy.wait_recv()
        queue = list(shared) + gather.steps((4, 5), (6, 7)) + gather.steps((6, 7), ())
        serve(queue)
        for p in range(2, 8):
            gather.side_arrivals(p)
        mask_scores(score_bias, segments[0], segments[1], False)

        def cross_query(j):
            at = span_of(j, 256)
            qc[:, at] = (nn(h_low[...], columns_of(w_x, at)) + biases[12:13, at]).astype(LOW)

        tiles(0, 3, cross_query)
        cross_copy.wait_recv()

        def cross_keys(j):
            at = span_of(j, 256)
            key_at = pl.ds(pl.multiple_of(2 * width + j * 256, 256), 256)
            value_at = pl.ds(pl.multiple_of(3 * width + j * 256, 256), 256)
            kc[:, at] = nn(x_recv[...], columns_of(w_x, key_at)).astype(LOW)
            vc[:, at] = (nn(x_recv[...], columns_of(w_x, value_at)) + biases[13:14, at]).astype(LOW)

        tiles(0, 3, cross_keys)
        attend_pairs(qc, kc, vc, score_bias, oc, None, p_c, 0, 6)

        def cross_out(j):
            at = span_of(j, 256)
            past = pl.ds(pl.multiple_of(width + j * 256, 256), 256)
            norm_c[:, at] = h[:, at] + nn(oc[...], columns_of(w_x, past)) + biases[14:15, at]

        tiles(0, 3, cross_out)
        norm_pass(norm_c, rstd_c, gains[4:5], biases[15:16], h, h2_low)
        ffn_up(h2_low, 0, 12)
        ffn_down()
        norm_pass(norm_f, rstd_f, gains[3:4], biases[11:12], None, x_send)
        layer_copy.start()
        cot_load.wait()
        gain, shift, branch = norm_undo(norm_f, rstd_f, gains[3:4], d_mixed, grad, d_ffn)
        set_small(3, gain)
        set_small(5 + 11, shift)
        set_small(5 + 10, branch)
        ffn_slope()
        ffn_hidden()
        gain, shift, branch = norm_undo(norm_c, rstd_c, gains[4:5], grad, grad, d_branch)
        set_small(4, gain)
        set_small(5 + 15, shift)
        set_small(5 + 14, branch)
        d_mixed[...] = nt(d_branch[...], columns_of(w_x, slice(width, 2 * width))).astype(LOW)
        attend_back_pairs(qc, kc, vc, None, None, p_c, d_mixed, 0, 6)
        layer_copy.wait()
        x_send[...] = (
            nt(kc[...], columns_of(w_x, slice(2 * width, 3 * width)))
            + nt(vc[...], columns_of(w_x, slice(3 * width, 4 * width)))
        ).astype(LOW)
        cross_copy.start()
        for p in range(8):
            gather.finish(p)
        grad_w_out()
        scatter.hand_over(4)
        scatter.hand_over(5)
        grad_w_in(h2_low)
        scatter.hand_over(2)
        scatter.hand_over(3)
        scatter.start(4)
        scatter.start(5)
        grad[...] += nt(qc[...], columns_of(w_x, slice(0, width)))
        store(w_x, slice(2 * width, 3 * width), tn(x_recv[...], kc[...]))
        store(w_x, slice(3 * width, 4 * width), tn(x_recv[...], vc[...]))
        scatter.hand_over(7)
        queue = scatter.steps((4, 5), (7, 6), finish_piece)
        serve(queue, 4)
        store(w_x, slice(0, width), tn(h_low[...], qc[...]))
        store(w_x, slice(width, 2 * width), tn(oc[...], d_branch[...]))
        scatter.hand_over(6)
        serve(queue, 4)
        set_b1(1)
        set_small(5 + 12, column_total(qc))
        set_small(5 + 13, column_total(vc))
        mask_scores(score_bias, segments[1], segments[1], True)
        self_back_a(1)
        serve(queue)
        queue = scatter.steps((7, 6), (2, 3), finish_piece)
        attend_back_pairs(q, k, v, score_bias, lse, None, d_mixed, 0, 3)
        serve(queue, 4)
        attend_back_pairs(q, k, v, score_bias, lse, None, d_mixed, 3, 6)
        serve(queue, 4)
        self_back_b(1)
        fold_start(0)
        serve(queue)
        queue = scatter.steps((2, 3), (0, 1), finish_piece)
        self_back_qk()
        scatter.hand_over(0)
        self_back_vo()
        scatter.hand_over(1)
        fold_end(0)
        serve(queue, 4)
        fold_end(1)
        serve(queue, 4)
        fold_end(2)
        serve(queue)
        fold_end(3)
        serve(scatter.steps((0, 1), (), finish_piece))
        cross_copy.wait_send()
        to_encoder.wait_send()
        for p in (6, 7):
            scatter.finish(p)

    fold_end(4)
    out_small[...] = small[...]
    for p in range(6):
        scatter.finish(p)
    for p in range(7):
        for half in range(2):
            out_copies(p, half).wait()
    pltpu.make_async_copy(grad, out_input.at[0, 0], out_sem.at[1]).wait()


def layer_call(tokens, segments, cotangent, attn_qk, attn_vo, cross_qk, cross_vo, ffn_in, ffn_out, gains, biases, ffn_bias):
    length, width = tokens.shape[2:]
    hidden = ffn_in.shape[2]

    def result(like, kind):
        return jax.ShapeDtypeStruct(like.shape, kind)

    def low(*shape):
        return pltpu.VMEM(shape, LOW)

    def full(*shape):
        return pltpu.VMEM(shape, jnp.float32)

    any_space = pl.BlockSpec(memory_space=pl.ANY)
    in_vmem = pl.BlockSpec(memory_space=pltpu.VMEM)
    flat, wide, exact = low(length, width), low(length, hidden), full(length, width)
    dma = pltpu.SemaphoreType.DMA
    scratch = [
        low(CHIPS, 2, 48, 2 * width), low(CHIPS, 2, 48, 2 * width), low(CHIPS, 2, 48, hidden),
        low(CHIPS, 2, 192, width), low(CHIPS, 2, 48, 4 * width),
        low(6, CHIPS, 48, 2 * width), low(2, CHIPS, 96, width),
        low(6, 2, 3, 48, 2 * width), low(2, 2, 3, 96, width),
        low(6, 2, 48, width), low(2, 2, 48, width),
        full(96, width), full(32, width), full(5, 32, width),
        full(8, width), full(1, width), full(1, hidden), full(4, 1, width),
        flat, flat, flat, flat, flat, exact, exact, wide, wide, exact, flat, full(length, length), flat, flat,
        flat, flat, flat, low(HEADS, length, length), flat, flat, exact, flat, flat, exact,
        full(HEADS, 1, length), full(length, 1), full(length, 1), full(length, 1),
        dma((7,)), dma((4,)), dma((4,)),
        dma((8, 2, 4)), dma((8, 2, 4)), dma((8, 9)), dma((8, 9)),
        dma((8, 2, 4)), dma((8, 2, 4)), dma((8,)), dma((8,)),
        dma((5,)), dma((5,)), dma((16,)),
    ]
    return pl.pallas_call(
        layer_kernel,
        out_shape=(
            result(tokens, LOW), result(tokens, jnp.float32),
            result(attn_qk, jnp.float32), result(attn_vo, jnp.float32),
            result(cross_qk, jnp.float32), result(cross_vo, jnp.float32),
            result(ffn_in, jnp.float32), result(ffn_out, jnp.float32),
            jax.ShapeDtypeStruct((32, width), jnp.float32),
        ),
        in_specs=[in_vmem] * 5 + [any_space] * 7,
        out_specs=(any_space,) * 8 + (in_vmem,),
        scratch_shapes=scratch,
        compiler_params=pltpu.CompilerParams(
            collective_id=0, has_side_effects=True, vmem_limit_bytes=63 * 1024 * 1024
        ),
        name="layer_pair",
    )(
        tokens, segments, gains, biases, ffn_bias, cotangent[0],
        attn_qk, attn_vo, cross_qk, cross_vo, ffn_in, ffn_out,
    )


def local_ring(
    tokens, segments, cotangent, attn_qk, attn_vo, cross_qk, cross_vo, ffn_in, ffn_out, gains, biases, ffn_bias
):
    results = layer_call(
        tokens, segments, cotangent, attn_qk, attn_vo, cross_qk, cross_vo, ffn_in, ffn_out, gains, biases, ffn_bias
    )
    small = results[8]
    return results[:8] + (small[0:5], small[5:21], small[21:29].reshape(ffn_bias.shape))


def solution(mesh):
    any_size = mesh.shape["section"] != 2 or mesh.shape["dp"] != 2 * CHIPS
    placed = (
        P("section", "dp", None, None),
        P(None, "dp", None),
        P("dp", None, None),
        P("section", "dp", None),
        P("section", "dp", None),
        P("section", "dp", None),
        P("section", "dp", None),
        P("section", "dp", None),
        P("section", "dp", None),
        P(),
        P(),
        P(),
    )
    return jax.shard_map(
        local_any if any_size else local_ring,
        mesh=mesh,
        in_specs=placed,
        out_specs=(
            P("section", "dp", None, None),
            P("section", "dp", None, None),
            P("section", "dp", None),
            P("section", "dp", None),
            P("section", "dp", None),
            P("section", "dp", None),
            P("section", "dp", None),
            P("section", "dp", None),
            P(),
            P(),
            P(),
        ),
        check_vma=False,
    )
```

```python
import functools

import jax
import jax.numpy as jnp
from jax import lax
from jax.experimental import pallas as pl
from jax.experimental.pallas import tpu as pltpu
from jax.sharding import PartitionSpec as P

HEADS = 12


NORM_EPSILON = 1e-05


def from_behind(x, axis, by):
    devices = lax.axis_size(axis)
    pairs = [(i, i + by) for i in range(devices) if 0 <= i + by < devices]
    return lax.ppermute(x, axis, pairs)


def product(left, right):
    return jnp.einsum("rld,de->rle", left, right, preferred_element_type=jnp.float32)


def back_product(grad, right):
    return jnp.einsum("rle,de->rld", grad, right, preferred_element_type=jnp.float32)


def weight_grad(left, grad):
    return jnp.einsum("rld,rle->de", left, grad, preferred_element_type=jnp.float32)


def column_sum(values):
    return jnp.sum(values.astype(jnp.float32), axis=(0, 1))


def norm_rows(resid, gain, shift):
    center = resid - jnp.mean(resid, axis=-1, keepdims=True)
    spread = jnp.mean(center * center, axis=-1, keepdims=True)
    return center * lax.rsqrt(spread + NORM_EPSILON) * gain + shift


def norm_back(resid, gain, shift, grad):
    unused, pull = jax.vjp(norm_rows, resid, gain, shift)
    return pull(grad)


def split_heads(values, head_count):
    return values.reshape(
        values.shape[0], values.shape[1], head_count, values.shape[2] // head_count
    )


def masked_scores(query_heads, key_heads, allowed):
    scale = query_heads.shape[-1] ** (-0.5)
    scores = (
        jnp.einsum("rqhe,rkhe->rhqk", query_heads, key_heads, preferred_element_type=jnp.float32)
        * scale
    )
    return jnp.where(allowed[:, None], scores, -1e30)


def attend(query, key_rows, value_rows, allowed, head_count):
    query_heads = split_heads(query, head_count)
    scores = masked_scores(query_heads, split_heads(key_rows, head_count), allowed)
    peak = jnp.max(scores, axis=-1, keepdims=True)
    exponent = jnp.exp(scores - peak)
    summed = jnp.sum(exponent, axis=-1, keepdims=True)
    soft = (exponent / summed).astype(jnp.bfloat16)
    mixed = jnp.einsum(
        "rhqk,rkhe->rqhe",
        soft,
        split_heads(value_rows, head_count),
        preferred_element_type=jnp.float32,
    )
    return (mixed.reshape(query.shape), peak + jnp.log(summed))


def attend_back(query, key_rows, value_rows, allowed, log_total, grad_mixed, head_count):
    query_heads = split_heads(query, head_count)
    key_heads = split_heads(key_rows, head_count)
    value_heads = split_heads(value_rows, head_count)
    grad_heads = split_heads(grad_mixed, head_count)
    scale = query_heads.shape[-1] ** (-0.5)
    soft = jnp.exp(masked_scores(query_heads, key_heads, allowed) - log_total)
    grad_values = jnp.einsum(
        "rhqk,rqhe->rkhe", soft.astype(jnp.bfloat16), grad_heads, preferred_element_type=jnp.float32
    )
    grad_soft = jnp.einsum(
        "rqhe,rkhe->rhqk", grad_heads, value_heads, preferred_element_type=jnp.float32
    )
    inner_sum = jnp.sum(soft * grad_soft, axis=-1, keepdims=True)
    grad_scores = (soft * (grad_soft - inner_sum)).astype(jnp.bfloat16)
    grad_query = (
        jnp.einsum("rhqk,rkhe->rqhe", grad_scores, key_heads, preferred_element_type=jnp.float32)
        * scale
    )
    grad_keys = (
        jnp.einsum("rhqk,rqhe->rkhe", grad_scores, query_heads, preferred_element_type=jnp.float32)
        * scale
    )
    return (
        grad_query.reshape(query.shape),
        grad_keys.reshape(key_rows.shape),
        grad_values.reshape(key_rows.shape),
    )


def self_forward(inputs, w_qk, w_vo, section_bias, gain, allowed, head_count):
    model_width = inputs.shape[-1]
    query = (product(inputs, w_qk[:, :model_width]) + section_bias[0]).astype(jnp.bfloat16)
    key_rows = product(inputs, w_qk[:, model_width:]).astype(jnp.bfloat16)
    value_rows = (product(inputs, w_vo[:, :model_width]) + section_bias[1]).astype(jnp.bfloat16)
    mixed, log_total = attend(query, key_rows, value_rows, allowed, head_count)
    mixed = mixed.astype(jnp.bfloat16)
    resid = inputs.astype(jnp.float32) + product(mixed, w_vo[:, model_width:]) + section_bias[2]
    return (
        norm_rows(resid, gain, section_bias[3]),
        (query, key_rows, value_rows, log_total, mixed, resid),
    )


def self_backward(inputs, w_qk, w_vo, section_bias, gain, allowed, head_count, kept, grad_hidden):
    query, key_rows, value_rows, log_total, mixed, resid = kept
    model_width = inputs.shape[-1]
    grad_resid, grad_gain, grad_shift = norm_back(resid, gain, section_bias[3], grad_hidden)
    grad_branch = grad_resid.astype(jnp.bfloat16)
    grad_mixed = back_product(grad_branch, w_vo[:, model_width:]).astype(jnp.bfloat16)
    grad_query, grad_keys, grad_values = attend_back(
        query, key_rows, value_rows, allowed, log_total, grad_mixed, head_count
    )
    grad_query = grad_query.astype(jnp.bfloat16)
    grad_keys = grad_keys.astype(jnp.bfloat16)
    grad_values = grad_values.astype(jnp.bfloat16)
    grad_pair = jnp.concatenate([grad_query, grad_keys], axis=-1)
    grad_inputs = (
        grad_resid
        + back_product(grad_pair, w_qk)
        + back_product(grad_values, w_vo[:, :model_width])
    )
    grad_rows = jnp.stack(
        [column_sum(grad_query), column_sum(grad_values), column_sum(grad_branch), grad_shift]
    )
    return (grad_inputs, (inputs, grad_pair, grad_values, mixed, grad_branch), grad_rows, grad_gain)


def ffn_forward(hidden, w_in, w_out, b_in, b_out):
    hidden_low = hidden.astype(jnp.bfloat16)
    pre_act = product(hidden_low, w_in) + b_in
    activated = jax.nn.gelu(pre_act, approximate=False).astype(jnp.bfloat16)
    return (product(activated, w_out) + b_out, (hidden_low, pre_act, activated))


def gelu_exact(values):
    return jax.nn.gelu(values, approximate=False)


def ffn_backward(w_in, w_out, kept, grad_branch):
    hidden_low, pre_act, activated = kept
    grad_low = grad_branch.astype(jnp.bfloat16)
    grad_act = back_product(grad_low, w_out)
    unused, pull = jax.vjp(gelu_exact, pre_act)
    grad_pre = pull(grad_act)[0].astype(jnp.bfloat16)
    grad_hidden = back_product(grad_pre, w_in)
    return (
        grad_hidden,
        (hidden_low, grad_pre, activated, grad_low),
        column_sum(grad_pre),
        column_sum(grad_low),
    )


def encoder_forward(hidden, w_in, w_out, b_in, section_bias, gain_last, w_ck, w_cv, bias_cv):
    branch, kept = ffn_forward(hidden, w_in, w_out, b_in, section_bias[4])
    resid = hidden + branch
    memory = norm_rows(resid, gain_last, section_bias[5]).astype(jnp.bfloat16)
    key_rows = product(memory, w_ck).astype(jnp.bfloat16)
    value_rows = (product(memory, w_cv) + bias_cv).astype(jnp.bfloat16)
    return (memory, key_rows, value_rows, resid, kept)


def encoder_backward(
    w_in, w_out, section_bias, gain_last, w_ck, w_cv, memory, resid, kept, grad_keys, grad_values
):
    grad_memory = back_product(grad_keys, w_ck) + back_product(grad_values, w_cv)
    grad_last, grad_gain, grad_shift = norm_back(resid, gain_last, section_bias[5], grad_memory)
    grad_ffn, ffn_ops, grad_bin, grad_bout = ffn_backward(w_in, w_out, kept, grad_last)
    zero_line = jnp.zeros_like(grad_gain)
    cross_rows = jnp.stack([zero_line, column_sum(grad_values), zero_line, zero_line])
    operands = (memory, grad_keys, memory, grad_values) + ffn_ops
    return (
        grad_last + grad_ffn,
        operands,
        grad_bin,
        grad_bout,
        grad_gain,
        grad_shift,
        cross_rows,
        zero_line,
    )


def decoder_step(
    hidden,
    w_cq,
    w_co,
    w_in,
    w_out,
    b_in,
    section_bias,
    gain_last,
    gain_cross,
    cross_bias,
    key_rows,
    value_rows,
    allowed,
    cotangent,
    head_count,
):
    hidden_low = hidden.astype(jnp.bfloat16)
    query = (product(hidden_low, w_cq) + cross_bias[0]).astype(jnp.bfloat16)
    mixed, log_total = attend(query, key_rows, value_rows, allowed, head_count)
    mixed = mixed.astype(jnp.bfloat16)
    resid_mid = hidden + product(mixed, w_co) + cross_bias[2]
    middle = norm_rows(resid_mid, gain_cross, cross_bias[3])
    branch, kept = ffn_forward(middle, w_in, w_out, b_in, section_bias[4])
    resid_last = middle + branch
    result = norm_rows(resid_last, gain_last, section_bias[5])
    grad_last, grad_gain, grad_shift = norm_back(
        resid_last, gain_last, section_bias[5], cotangent.astype(jnp.float32)
    )
    grad_ffn, ffn_ops, grad_bin, grad_bout = ffn_backward(w_in, w_out, kept, grad_last)
    grad_mid, grad_gain_cross, grad_shift_cross = norm_back(
        resid_mid, gain_cross, cross_bias[3], grad_last + grad_ffn
    )
    grad_branch = grad_mid.astype(jnp.bfloat16)
    grad_mixed = back_product(grad_branch, w_co).astype(jnp.bfloat16)
    grad_query, grad_keys, grad_values = attend_back(
        query, key_rows, value_rows, allowed, log_total, grad_mixed, head_count
    )
    grad_query = grad_query.astype(jnp.bfloat16)
    grad_hidden = grad_mid + back_product(grad_query, w_cq)
    cross_rows = jnp.stack(
        [
            column_sum(grad_query),
            jnp.zeros_like(grad_gain),
            column_sum(grad_branch),
            grad_shift_cross,
        ]
    )
    operands = (hidden_low, grad_query, mixed, grad_branch) + ffn_ops
    tail_result = (
        grad_hidden,
        operands,
        grad_bin,
        grad_bout,
        grad_gain,
        grad_shift,
        cross_rows,
        grad_gain_cross,
    )
    return (
        result.astype(jnp.bfloat16),
        grad_keys.astype(jnp.bfloat16),
        grad_values.astype(jnp.bfloat16),
        tail_result,
    )


def zero_tail(hidden, w_in):
    model_width = hidden.shape[-1]
    ffn_width = w_in.shape[1]
    flat = jnp.zeros(hidden.shape, jnp.bfloat16)
    wide = jnp.zeros((hidden.shape[0], hidden.shape[1], ffn_width), jnp.bfloat16)
    zero_line = jnp.zeros((model_width,), jnp.float32)
    operands = (flat, flat, flat, flat, flat, wide, wide, flat)
    return (
        jnp.zeros_like(hidden),
        operands,
        jnp.zeros((ffn_width,), jnp.float32),
        zero_line,
        zero_line,
        zero_line,
        jnp.zeros((4, model_width), jnp.float32),
        zero_line,
    )


def tail_whole(operands):
    return (
        weight_grad(operands[0], operands[1]),
        weight_grad(operands[2], operands[3]),
        weight_grad(operands[4], operands[5]),
        weight_grad(operands[6], operands[7]),
    )


def self_whole(operands):
    grad_qk = weight_grad(operands[0], operands[1])
    grad_vo = jnp.concatenate(
        [weight_grad(operands[0], operands[2]), weight_grad(operands[3], operands[4])], axis=1
    )
    return (grad_qk, grad_vo)


def local_any(
    tokens,
    segments,
    cotangent,
    attn_qk,
    attn_vo,
    cross_qk,
    cross_vo,
    ffn_in,
    ffn_out,
    gains,
    biases,
    ffn_bias,
):
    head_count = HEADS
    section_index = lax.axis_index("section")
    is_enc = section_index == 0
    qk_whole, vo_whole = (
        lax.all_gather(attn_qk, "dp", axis=1, tiled=True),
        lax.all_gather(attn_vo, "dp", axis=1, tiled=True),
    )
    w_qk = qk_whole[0]
    w_vo = vo_whole[0]
    cqk_whole, cvo_whole, in_whole, out_whole = (
        lax.all_gather(cross_qk, "dp", axis=1, tiled=True),
        lax.all_gather(cross_vo, "dp", axis=1, tiled=True),
        lax.all_gather(ffn_in, "dp", axis=1, tiled=True),
        lax.all_gather(ffn_out, "dp", axis=1, tiled=True),
    )
    w_cqk = cqk_whole[0]
    w_cvo = cvo_whole[0]
    w_in = in_whole[0]
    w_out = out_whole[0]
    section_bias = lax.dynamic_slice_in_dim(biases, 6 * section_index, 6, 0)
    section_gain = lax.dynamic_slice_in_dim(gains, 2 * section_index, 2, 0)
    bias_in = lax.dynamic_index_in_dim(ffn_bias, section_index, 0, keepdims=False)
    section_seg = lax.dynamic_index_in_dim(segments, section_index, 0, keepdims=False)
    length = tokens.shape[2]
    position = jnp.arange(length)
    earlier = position[None, :] <= position[:, None]
    allowed_self = (section_seg[:, :, None] == section_seg[:, None, :]) & (earlier[None] | is_enc)
    allowed_cross = segments[1][:, :, None] == segments[0][:, None, :]
    source = tokens[0]
    hidden_one, kept_self = self_forward(
        source, w_qk, w_vo, section_bias, section_gain[0], allowed_self, head_count
    )

    def run_encoder():
        return encoder_forward(
            hidden_one,
            w_in,
            w_out,
            bias_in,
            section_bias,
            section_gain[1],
            w_cqk,
            w_cvo,
            biases[13],
        )

    def skip_encoder():
        flat = jnp.zeros(hidden_one.shape, jnp.bfloat16)
        wide_shape = (hidden_one.shape[0], hidden_one.shape[1], w_in.shape[1])
        return (
            flat,
            flat,
            flat,
            jnp.zeros_like(hidden_one),
            (flat, jnp.zeros(wide_shape, jnp.float32), jnp.zeros(wide_shape, jnp.bfloat16)),
        )

    memory, enc_keys, enc_values, enc_resid, enc_kept = lax.cond(is_enc, run_encoder, skip_encoder)
    got_keys, got_values = from_behind((enc_keys, enc_values), "section", 1)

    def run_decoder():
        return decoder_step(
            hidden_one,
            w_cqk,
            w_cvo,
            w_in,
            w_out,
            bias_in,
            section_bias,
            section_gain[1],
            gains[4],
            biases[12:16],
            got_keys,
            got_values,
            allowed_cross,
            cotangent,
            head_count,
        )

    def skip_decoder():
        flat = jnp.zeros(hidden_one.shape, jnp.bfloat16)
        return (flat, flat, flat, zero_tail(hidden_one, w_in))

    decoded, grad_keys, grad_values, dec_tail = lax.cond(is_enc, skip_decoder, run_decoder)
    back_keys, back_values = from_behind((grad_keys, grad_values), "section", -1)

    def run_encoder_back():
        return encoder_backward(
            w_in,
            w_out,
            section_bias,
            section_gain[1],
            w_cqk,
            w_cvo,
            memory,
            enc_resid,
            enc_kept,
            back_keys,
            back_values,
        )

    def keep_decoder():
        return dec_tail

    tail_result = lax.cond(is_enc, run_encoder_back, keep_decoder)
    (
        grad_hidden,
        tail_ops,
        grad_bin,
        grad_bout,
        grad_gain_last,
        grad_shift_last,
        cross_rows,
        grad_gain_cross,
    ) = tail_result
    layer_out = jnp.where(is_enc, memory, decoded)
    model_width = source.shape[-1]
    grad_ca, grad_cb, grad_in, grad_out = tail_whole(tail_ops)
    tail_parts = (
        lax.psum_scatter(grad_ca[None], "dp", scatter_dimension=1, tiled=True),
        lax.psum_scatter(grad_cb[None], "dp", scatter_dimension=1, tiled=True),
        lax.psum_scatter(grad_in[None], "dp", scatter_dimension=1, tiled=True),
        lax.psum_scatter(grad_out[None], "dp", scatter_dimension=1, tiled=True),
    )
    grad_source, self_ops, self_rows, grad_gain_first = self_backward(
        source,
        w_qk,
        w_vo,
        section_bias,
        section_gain[0],
        allowed_self,
        head_count,
        kept_self,
        grad_hidden,
    )
    grad_qk, grad_vo = self_whole(self_ops)
    attn_parts = (
        lax.psum_scatter(grad_qk[None], "dp", scatter_dimension=1, tiled=True),
        lax.psum_scatter(grad_vo[None], "dp", scatter_dimension=1, tiled=True),
    )
    large_parts = tuple(attn_parts) + tuple(tail_parts)
    section_rows = jnp.concatenate([self_rows, jnp.stack([grad_bout, grad_shift_last])], axis=0)
    bias_block = lax.dynamic_update_slice_in_dim(
        jnp.zeros((12, model_width), jnp.float32), section_rows, 6 * section_index, 0
    )
    grad_biases = jnp.concatenate([bias_block, cross_rows], axis=0)
    gain_block = lax.dynamic_update_slice_in_dim(
        jnp.zeros((4, model_width), jnp.float32),
        jnp.stack([grad_gain_first, grad_gain_last]),
        2 * section_index,
        0,
    )
    grad_gains = jnp.concatenate([gain_block, grad_gain_cross[None]], axis=0)
    grad_fbias = lax.dynamic_update_slice_in_dim(
        jnp.zeros_like(ffn_bias), grad_bin[None], section_index, 0
    )
    sum_gains, sum_biases, sum_fbias = lax.psum(
        (grad_gains, grad_biases, grad_fbias), ("section", "dp")
    )
    return (
        layer_out[None],
        grad_source[None],
        large_parts[0],
        large_parts[1],
        large_parts[2],
        large_parts[3],
        large_parts[4],
        large_parts[5],
        sum_gains,
        sum_biases,
        sum_fbias,
    )


MESH = pl.DeviceIdType.MESH
LOW = jnp.bfloat16
CHIPS = 8
FAR = 3
MASKED = -1e30


class Place:
    def __init__(self):
        self.section = lax.axis_index("section")
        shard = lax.axis_index("dp")
        self.core = shard % 2
        self.chip = shard // 2
        self.across = self.chip % 2
        self.along = self.chip // 2
        self.pos = self.along + self.across * (7 - 2 * self.along)

    def chip_at(self, step):
        spot = (self.pos + step + CHIPS) % CHIPS
        across = spot // 4
        along = spot + across * (7 - 2 * spot)
        return along * 2 + across

    def ring(self, step):
        return (self.section, self.chip_at(step) * 2 + self.core)

    def sibling(self):
        return (self.section, self.chip * 2 + 1 - self.core)

    def peer(self):
        return (1 - self.section, self.chip * 2 + self.core)

    def folds(self):
        near = self.along + 1 - 2 * (self.along % 2)
        far = (self.along + 2) % 4
        return (
            self.sibling(),
            (self.section, (self.along * 2 + 1 - self.across) * 2 + self.core),
            (self.section, (near * 2 + self.across) * 2 + self.core),
            (self.section, (far * 2 + self.across) * 2 + self.core),
            self.peer(),
        )


def enter(place):
    barrier = pltpu.get_barrier_semaphore()
    others = (place.ring(1), place.ring(-1)) + place.folds()
    for other in others:
        pl.semaphore_signal(barrier, inc=1, device_id=other, device_id_type=MESH)
    pl.semaphore_wait(barrier, len(others))


class Piece:
    def __init__(self, ref, by_rows, low, span, slot):
        self.ref, self.by_rows, self.low, self.span, self.slot = ref, by_rows, low, span, slot

    def at(self, chip, core, half=None):
        low, span = self.low, self.span
        if half is not None:
            span = span // 2
            low = low + half * span
        if self.by_rows:
            return self.ref.at[chip, core, low : low + span, :]
        return self.ref.at[chip, core, :, low : low + span]


def piece_list(qk, vo, w_in, w_out, cross):
    return [
        Piece(qk, False, 0, 1536, 0),
        Piece(vo, False, 0, 1536, 1),
        Piece(w_in, False, 0, 1536, 2),
        Piece(w_in, False, 1536, 1536, 3),
        Piece(w_out, True, 0, 96, 0),
        Piece(w_out, True, 96, 96, 1),
        Piece(cross, True, 0, 96, 2),
        Piece(cross, True, 96, 96, 3),
    ]


class Gather:
    def __init__(self, place, pieces, ring_send, ring_recv, side_send, side_recv):
        self.place, self.pieces = place, pieces
        self.ring_send, self.ring_recv, self.side_send, self.side_recv = ring_send, ring_recv, side_send, side_recv

    def ring_copy(self, p, way, hop):
        sign = 1 - 2 * way
        ref = self.pieces[p].at(self.place.chip_at(-sign * hop), self.place.core, way if hop == FAR else None)
        return pltpu.make_async_remote_copy(
            ref, ref, self.ring_send.at[p, way, hop], self.ring_recv.at[p, way, hop],
            device_id=self.place.ring(sign), device_id_type=MESH,
        )

    def arrival(self, p, way, hop, core):
        sign = 1 - 2 * way
        return self.pieces[p].at(self.place.chip_at(-sign * (hop + 1)), core, way if hop == FAR else None)

    def side_copy(self, p, k, core):
        if k == 0:
            ref = self.pieces[p].at(self.place.chip, core)
        else:
            ref = self.arrival(p, (k - 1) // 4, (k - 1) % 4, core)
        return pltpu.make_async_remote_copy(
            ref, ref, self.side_send.at[p, k], self.side_recv.at[p, k],
            device_id=self.place.sibling(), device_id_type=MESH,
        )

    def start(self, p):
        self.ring_copy(p, 0, 0).start()
        self.ring_copy(p, 1, 0).start()
        self.side_copy(p, 0, self.place.core).start()

    def event(self, p, way, hop):
        ref = self.arrival(p, way, hop, self.place.core)
        pltpu.make_async_remote_copy(
            ref, ref, self.ring_send.at[p, way, hop], self.ring_recv.at[p, way, hop],
            device_id=self.place.ring(1), device_id_type=MESH,
        ).wait_recv()
        if hop < FAR:
            self.ring_copy(p, way, hop + 1).start()
        self.side_copy(p, 1 + 4 * way + hop, self.place.core).start()

    def side_arrivals(self, p):
        for k in range(9):
            self.side_copy(p, k, 1 - self.place.core).wait_recv()

    def finish(self, p):
        for way in range(2):
            for hop in range(4):
                self.ring_copy(p, way, hop).wait_send()
        for k in range(9):
            self.side_copy(p, k, self.place.core).wait_send()


class Scatter:
    def __init__(self, place, pieces, side_c, side_r, land_c, land_r, near_c, near_r, ring_send, ring_recv, side_send, side_recv):
        self.place, self.pieces = place, pieces
        self.side_c, self.side_r, self.land_c, self.land_r = side_c, side_r, land_c, land_r
        self.near_c, self.near_r = near_c, near_r
        self.ring_send, self.ring_recv, self.side_send, self.side_recv = ring_send, ring_recv, side_send, side_recv

    def cut(self, p, ref, half):
        piece = self.pieces[p]
        if half is None:
            return ref
        span = piece.span // 2
        if piece.by_rows:
            return ref.at[half * span : (half + 1) * span, :]
        return ref.at[:, half * span : (half + 1) * span]

    def from_side(self, p, chip, half=None):
        piece = self.pieces[p]
        return self.cut(p, (self.side_r if piece.by_rows else self.side_c).at[piece.slot, chip], half)

    def landed(self, p, way, step, half=None):
        piece = self.pieces[p]
        if step == 0:
            return (self.near_r if piece.by_rows else self.near_c).at[piece.slot, way]
        return self.cut(p, (self.land_r if piece.by_rows else self.land_c).at[piece.slot, way, step - 1], half)

    def side_copy(self, p):
        piece = self.pieces[p]
        span = slice(piece.low, piece.low + piece.span)
        other = 1 - self.place.core
        src = piece.ref.at[:, other, span, :] if piece.by_rows else piece.ref.at[:, other, :, span]
        dst = (self.side_r if piece.by_rows else self.side_c).at[piece.slot]
        return pltpu.make_async_remote_copy(
            src, dst, self.side_send.at[p], self.side_recv.at[p],
            device_id=self.place.sibling(), device_id_type=MESH,
        )

    def chip_of(self, way, step):
        sign = 1 - 2 * way
        return self.place.chip_at(sign * (4 - step))

    def ring_copy(self, p, way, step):
        sign = 1 - 2 * way
        half = way if step == 0 else None
        return pltpu.make_async_remote_copy(
            self.pieces[p].at(self.chip_of(way, step), self.place.core, half), self.landed(p, way, step, half),
            self.ring_send.at[p, way, step], self.ring_recv.at[p, way, step],
            device_id=self.place.ring(sign), device_id_type=MESH,
        )

    def hand_over(self, p):
        self.side_copy(p).start()

    def start(self, p):
        self.side_copy(p).wait_recv()
        for way in range(2):
            chip = self.chip_of(way, 0)
            own = self.pieces[p].at(chip, self.place.core, way)
            total = own[...].astype(jnp.float32) + self.from_side(p, chip, way)[...].astype(jnp.float32)
            own[...] = total.astype(LOW)
            self.ring_copy(p, way, 0).start()

    def event(self, p, way, step):
        self.ring_copy(p, way, step).wait_recv()
        chip = self.chip_of(way, step + 1)
        for half in range(2):
            own = self.pieces[p].at(chip, self.place.core, half)
            total = own[...].astype(jnp.float32) + self.from_side(p, chip, half)[...].astype(jnp.float32)
            if step > 0 or half == way:
                total = total + self.landed(p, way, step, half)[...].astype(jnp.float32)
            own[...] = total.astype(LOW)
        self.ring_copy(p, way, step + 1).start()

    def last(self, p):
        chip = self.place.chip
        total = self.pieces[p].at(chip, self.place.core)[...].astype(jnp.float32)
        total = total + self.from_side(p, chip)[...].astype(jnp.float32)
        for way in range(2):
            self.ring_copy(p, way, 3).wait_recv()
            total = total + self.landed(p, way, 3)[...].astype(jnp.float32)
        return total

    def finish(self, p):
        self.side_copy(p).wait_send()
        for way in range(2):
            for step in range(4):
                self.ring_copy(p, way, step).wait_send()


def plan(text, ring, after=None):
    found = []
    for word in text.split():
        if word[0] == "+":
            found.append([functools.partial(ring.start, int(word[1:]))])
        elif word[0] == "=":
            found.append([functools.partial(after, int(word[1:]))])
        else:
            p, step = (int(part) for part in word.split("."))
            found.append([functools.partial(ring.event, p, way, step) for way in range(2)])
    return found


def serve(queue, count=None):
    for _ in range(len(queue) if count is None else min(count, len(queue))):
        for step in queue.pop(0):
            step()


def nn(left, right):
    return jnp.dot(left, right, preferred_element_type=jnp.float32)


def nt(left, right):
    return lax.dot_general(left, right, (((1,), (1,)), ((), ())), preferred_element_type=jnp.float32)


def tn(left, right):
    return lax.dot_general(left, right, (((0,), (0,)), ((), ())), preferred_element_type=jnp.float32)


def tiles(low, high, body):
    def step(j, carry):
        body(j)
        return carry

    lax.fori_loop(low, high, step, 0, unroll=min(6, high - low))


def span_of(j, width):
    return pl.ds(pl.multiple_of(j * width, width), width)


def columns_of(ref, at, rows=slice(None)):
    block = ref[:, :, rows, at]
    return block.reshape(block.shape[0] * block.shape[1] * block.shape[2], block.shape[3])


def head_masks(length, value):
    lane = lax.broadcasted_iota(jnp.int32, (length, 128), 1)
    first = jnp.where(lane < 64, value, 0.0).astype(LOW)
    second = jnp.where(lane < 64, 0.0, value).astype(LOW)
    return first, second


def mask_scores(bias_ref, key_row, query_row, causal):
    length = bias_ref.shape[0]
    keys = jnp.transpose(jnp.broadcast_to(key_row.astype(jnp.float32), (128, length)))
    keys = jnp.concatenate([keys] * (length // 128), axis=1)
    same = keys == jnp.broadcast_to(query_row.astype(jnp.float32), (length, length))
    if causal:
        key_at = lax.broadcasted_iota(jnp.int32, (length, length), 0)
        query_at = lax.broadcasted_iota(jnp.int32, (length, length), 1)
        same = same & (key_at <= query_at)
    bias_ref[...] = jnp.where(same, 0.0, MASKED)


def attend_pairs(q_ref, k_ref, v_ref, bias_ref, o_ref, lse_ref, p_ref, low, high):
    masks = head_masks(q_ref.shape[0], 0.125)

    def pair(i):
        at = span_of(i, 128)
        q2, k2 = q_ref[:, at], k_ref[:, at]
        v_turned = jnp.transpose(v_ref[:, at])
        parts = []
        for h in range(2):
            scores = nt(k2 * masks[h], q2) + bias_ref[...]
            peak = jnp.max(scores, axis=0, keepdims=True)
            exponent = jnp.exp(scores - peak)
            summed = jnp.sum(exponent, axis=0, keepdims=True)
            soft = (exponent * (1.0 / summed)).astype(LOW)
            if p_ref is not None:
                p_ref[2 * i + h] = soft
            if lse_ref is not None:
                lse_ref[2 * i + h] = peak + jnp.log(summed)
            parts.append(nn(v_turned[64 * h : 64 * h + 64], soft))
        o_ref[:, at] = jnp.transpose(jnp.concatenate(parts, axis=0)).astype(LOW)

    tiles(low, high, pair)


def attend_back_pairs(q_ref, k_ref, v_ref, bias_ref, lse_ref, p_ref, do_ref, low, high):
    masks = head_masks(q_ref.shape[0], 0.125)
    ones = head_masks(q_ref.shape[0], 1.0)

    def pair(i):
        at = span_of(i, 128)
        q2, k2, v2, do2 = q_ref[:, at], k_ref[:, at], v_ref[:, at], do_ref[:, at]
        k_turned = jnp.transpose(k2)
        parts = []
        dk = dv = None
        for h in range(2):
            if p_ref is not None:
                low_soft = p_ref[2 * i + h]
                soft = low_soft.astype(jnp.float32)
            else:
                soft = jnp.exp(nt(k2 * masks[h], q2) + bias_ref[...] - lse_ref[2 * i + h])
                low_soft = soft.astype(LOW)
            dv_h = nn(low_soft, do2 * ones[h])
            d_soft = nt(v2 * ones[h], do2)
            inner = jnp.sum(soft * d_soft, axis=0, keepdims=True)
            d_scores = (soft * (d_soft - inner)).astype(LOW)
            dk_h = nn(d_scores, q2 * masks[h])
            parts.append(nn(k_turned[64 * h : 64 * h + 64], d_scores))
            dk = dk_h if dk is None else dk + dk_h
            dv = dv_h if dv is None else dv + dv_h
        q_ref[:, at] = (jnp.transpose(jnp.concatenate(parts, axis=0)) * 0.125).astype(LOW)
        k_ref[:, at] = dk.astype(LOW)
        v_ref[:, at] = dv.astype(LOW)

    tiles(low, high, pair)


def attend_back_keys(q_ref, k_ref, v_ref, o_ref, p_ref, do_ref, dq_ref, low, span, first):
    masks = head_masks(q_ref.shape[0], 0.125)
    ones = head_masks(q_ref.shape[0], 1.0)
    short = head_masks(span, 1.0)
    rows = slice(low, low + span)

    def pair(i):
        at = span_of(i, 128)
        q2, k2, v2, do2 = q_ref[:, at], k_ref[rows, at], v_ref[rows, at], do_ref[:, at]
        k_turned = jnp.transpose(k2)
        inner = jnp.transpose(do2.astype(jnp.float32) * o_ref[:, at].astype(jnp.float32))
        parts = []
        dk = dv = None
        for h in range(2):
            low_soft = p_ref[2 * i + h, rows, :]
            soft = low_soft.astype(jnp.float32)
            dv_h = nn(low_soft, do2 * ones[h])
            d_soft = nt(v2 * short[h], do2)
            total = jnp.sum(inner[64 * h : 64 * h + 64], axis=0, keepdims=True)
            d_scores = (soft * (d_soft - total)).astype(LOW)
            dk_h = nn(d_scores, q2 * masks[h])
            parts.append(nn(k_turned[64 * h : 64 * h + 64], d_scores))
            dk = dk_h if dk is None else dk + dk_h
            dv = dv_h if dv is None else dv + dv_h
        dq = jnp.transpose(jnp.concatenate(parts, axis=0)) * 0.125
        dq_ref[:, at] = dq if first else dq_ref[:, at] + dq
        k_ref[rows, at] = dk.astype(LOW)
        v_ref[rows, at] = dv.astype(LOW)

    tiles(0, q_ref.shape[1] // 128, pair)


def gelu_parts(u):
    size = jnp.abs(u)
    bell = jnp.exp(-0.5 * u * u)
    t = 1.0 / (1.0 + 0.2316419 * size)
    tail = t * (0.127414796 + t * (-0.142248368 + t * (0.710706870 + t * (-0.726576013 + t * 0.530702714)))) * bell
    upper = jnp.where(u < 0, tail, 1.0 - tail)
    return u * upper, upper + u * bell * 0.3989422804014327


def norm_pass(norm_ref, rstd_ref, gain, shift, hidden_ref, low_ref, first=0, last=6):
    def rows(j):
        at = span_of(j, 64)
        resid = norm_ref[at, :]
        center = resid - jnp.mean(resid, axis=-1, keepdims=True)
        rstd = lax.rsqrt(jnp.mean(center * center, axis=-1, keepdims=True) + NORM_EPSILON)
        normal = center * rstd
        norm_ref[at, :] = normal
        rstd_ref[0][at, rstd_ref[1]] = rstd
        result = normal * gain + shift
        if hidden_ref is not None:
            hidden_ref[at, :] = result
        low_ref[at, :] = result.astype(LOW)

    tiles(first, last, rows)


def norm_undo(norm_ref, rstd_ref, gain, source_ref, grad_ref, low_ref, first=0, last=6, carry=None):
    width = norm_ref.shape[1]

    def rows(j, carry):
        d_gain, d_shift, d_low = carry
        at = span_of(j, 64)
        dy = source_ref[at, :].astype(jnp.float32)
        normal = norm_ref[at, :]
        scaled = dy * gain
        mean = jnp.mean(scaled, axis=-1, keepdims=True)
        along = jnp.mean(scaled * normal, axis=-1, keepdims=True)
        d_resid = rstd_ref[0][at, rstd_ref[1]] * (scaled - mean - normal * along)
        grad_ref[at, :] = d_resid
        low = d_resid.astype(LOW)
        low_ref[at, :] = low
        return (
            d_gain + jnp.sum(dy * normal, axis=0, keepdims=True),
            d_shift + jnp.sum(dy, axis=0, keepdims=True),
            d_low + jnp.sum(low.astype(jnp.float32), axis=0, keepdims=True),
        )

    zero = jnp.zeros((1, width), jnp.float32)
    return lax.fori_loop(first, last, rows, (zero, zero, zero) if carry is None else carry)


def column_total(ref):
    return jnp.sum(ref[...].astype(jnp.float32), axis=0, keepdims=True)


def layer_kernel(
    tokens, segments, gains, biases, ffn_bias, cotangent, s_qk, s_vo, s_cqk, s_cvo, s_in, s_out,
    out_layer, out_input, out_qk, out_vo, out_cqk, out_cvo, out_in, out_out, out_small,
    w_qk, w_vo, w_in, w_out, w_x,
    side_c, side_r, land_c, land_r, near_c, near_r, small, small_land,
    sec_bias, sec_gain, sec_fbias, b1_rows,
    q, k, v, o, h_low, norm_a, h, act, slope, norm_f, d_ffn, score_bias, x_send, x_recv,
    qc, kc, vc, p_c, oc, h2_low, norm_c, d_branch, d_mixed, grad, lse, rstd,
    load_sem, peer_send, peer_recv, rs, rr, ss, sr, rs2, rr2, ss2, sr2, fold_send, fold_recv, out_sem,
):
    place = Place()
    chip, core = place.chip, place.core
    width = tokens.shape[-1]
    encoder, decoder = place.section == 0, place.section == 1
    x = tokens.at[0, 0]
    rstd_a, rstd_f, rstd_c = ((rstd, slice(i, i + 1)) for i in range(3))
    loads = [
        pltpu.make_async_copy(src.at[0], dst.at[chip, core], load_sem.at[i])
        for i, (src, dst) in enumerate([(s_qk, w_qk), (s_vo, w_vo), (s_in, w_in), (s_out, w_out)])
    ]
    for copy in loads:
        copy.start()
    enter(place)
    own_cross = [
        pltpu.make_async_copy(src.at[0], w_x.at[chip, core, 48 * i : 48 * i + 48, :], load_sem.at[4 + i])
        for i, src in enumerate([s_cqk, s_cvo])
    ]
    from_encoder = [
        pltpu.make_async_remote_copy(
            src.at[0], w_x.at[chip, core, 96 + 48 * i : 144 + 48 * i, :], peer_send.at[i], peer_recv.at[i],
            device_id=place.peer(), device_id_type=MESH,
        )
        for i, src in enumerate([s_cqk, s_cvo])
    ]
    pieces = piece_list(w_qk, w_vo, w_in, w_out, w_x)
    gather = Gather(place, pieces, rs, rr, ss, sr)
    for copy in loads:
        copy.wait()
    gather.start(0)
    gather.start(1)
    cot_load = pltpu.make_async_copy(cotangent, d_mixed, load_sem.at[6])

    @pl.when(encoder)
    def _():
        for copy in from_encoder:
            copy.start()
        sec_bias[0:6] = biases[0:6]
        sec_gain[0:1] = gains[0:1]
        sec_fbias[...] = ffn_bias[0:1]
        mask_scores(score_bias, segments[0], segments[0], False)

    @pl.when(decoder)
    def _():
        for copy in own_cross:
            copy.start()
        cot_load.start()
        sec_bias[0:6] = biases[6:12]
        sec_gain[0:1] = gains[2:3]
        sec_fbias[...] = ffn_bias[1:2]
        mask_scores(score_bias, segments[1], segments[1], True)

    small[...] = jnp.zeros_like(small)
    serve(plan("0.0 1.0 0.1 1.1", gather))

    def next_pieces(first, second):
        serve(plan(f"0.2 +{first} 1.2 +{second} 0.3 1.3", gather))

    @pl.when(encoder)
    def _():
        next_pieces(2, 3)

    @pl.when(decoder)
    def _():
        for copy in own_cross:
            copy.wait()
        for copy in from_encoder:
            copy.wait_recv()
        next_pieces(6, 7)

    gather.side_arrivals(0)
    gather.side_arrivals(1)

    def early(count):
        @pl.when(encoder)
        def _():
            serve(first_steps, count)

        @pl.when(decoder)
        def _():
            serve(other_steps, count)

    first_steps = plan("2.0 +4 3.0 +5 2.1 3.1 4.0 5.0", gather)
    other_steps = plan("6.0 +2 7.0 +3 6.1 7.1 2.0 3.0", gather)

    def project(j):
        at = span_of(j, 256)
        past = pl.ds(pl.multiple_of(width + j * 256, 256), 256)
        q[:, at] = (nn(x[...], columns_of(w_qk, at)) + sec_bias[0:1, at]).astype(LOW)
        k[:, at] = nn(x[...], columns_of(w_qk, past)).astype(LOW)
        v[:, at] = (nn(x[...], columns_of(w_vo, at)) + sec_bias[1:2, at]).astype(LOW)

    tiles(0, 3, project)
    early(2)
    attend_pairs(q, k, v, score_bias, o, lse, None, 0, 2)
    early(2)
    attend_pairs(q, k, v, score_bias, o, lse, None, 2, 4)
    early(2)
    attend_pairs(q, k, v, score_bias, o, lse, None, 4, 6)
    early(1)

    def self_out(j):
        at = span_of(j, 256)
        past = pl.ds(pl.multiple_of(width + j * 256, 256), 256)
        norm_a[:, at] = x[:, at].astype(jnp.float32) + nn(o[...], columns_of(w_vo, past)) + sec_bias[2:3, at]

    tiles(0, 3, self_out)
    norm_pass(norm_a, rstd_a, sec_gain[0:1], sec_bias[3:4], h, h_low)
    early(None)

    def ffn_up(low_ref, low, high):
        def tile(j):
            at = span_of(j, 256)
            u = nn(low_ref[...], columns_of(w_in, at)) + sec_fbias[:, at]
            value, rise = gelu_parts(u)
            act[:, at] = value.astype(LOW)
            slope[:, at] = rise.astype(LOW)

        tiles(low, high, tile)

    def ffn_down(rows=slice(None)):
        def tile(j):
            at = span_of(j, 256)
            norm_f[rows, at] = h[rows, at] + nn(act[rows, :], columns_of(w_out, at)) + sec_bias[4:5, at]

        tiles(0, 3, tile)

    def ffn_slope():
        def tile(j):
            at = span_of(j, width)
            block = w_out[pl.ds(2 * j, 2)].reshape(width, width)
            d_pre = (nt(d_ffn[...], block) * slope[:, at].astype(jnp.float32)).astype(LOW)
            slope[:, at] = d_pre
            b1_rows[j] = jnp.sum(d_pre.astype(jnp.float32), axis=0, keepdims=True)

        tiles(0, 4, tile)

    def ffn_hidden():
        def tile(j):
            at = span_of(j, width)
            grad[...] += nt(slope[:, at], columns_of(w_in, at))

        tiles(0, 4, tile)

    def grad_w_out(ref):
        def tile(c):
            block = tn(act[:, span_of(c, 384)], d_ffn[...])
            ref[c] = block.astype(LOW).reshape(2, 192, width)

        tiles(0, CHIPS, tile)

    def store(ref, at, value, rows=slice(None)):
        ref[:, :, rows, at] = value.astype(LOW).reshape(CHIPS, 2, 48, value.shape[1])

    def cross_weight(i, at=slice(None)):
        return columns_of(w_x, at, slice(48 * i, 48 * i + 48))

    def store_cross(i, value):
        store(w_x, slice(None), value, slice(48 * i, 48 * i + 48))

    def grad_w_in(low_ref):
        def tile(j):
            at = span_of(j, width)
            store(w_in, at, tn(low_ref[...], slope[:, at]))

        tiles(0, 4, tile)

    def set_small(row, value):
        small[row : row + 1, :] = value

    def set_b1(section):
        for j in range(4):
            set_small(24 + 4 * section + j, b1_rows[j])

    def self_back_a(section):
        gain, shift, branch = norm_undo(norm_a, rstd_a, sec_gain[0:1], grad, grad, d_branch)
        set_small(2 * section, gain)
        set_small(8 + 6 * section + 3, shift)
        set_small(8 + 6 * section + 2, branch)
        d_mixed[...] = nt(d_branch[...], columns_of(w_vo, slice(width, 2 * width))).astype(LOW)

    def self_back_b(section):
        set_small(8 + 6 * section, column_total(q))
        set_small(8 + 6 * section + 1, column_total(v))
        grad[...] += nt(q[...], columns_of(w_qk, slice(0, width)))
        grad[...] += nt(k[...], columns_of(w_qk, slice(width, 2 * width)))
        grad[...] += nt(v[...], columns_of(w_vo, slice(0, width)))
        pltpu.make_async_copy(grad, out_input.at[0, 0], out_sem.at[1]).start()

    def self_back_qk():
        store(w_qk, slice(0, width), tn(x[...], q[...]))
        store(w_qk, slice(width, 2 * width), tn(x[...], k[...]))

    def self_back_vo():
        store(w_vo, slice(0, width), tn(x[...], v[...]))
        store(w_vo, slice(width, 2 * width), tn(o[...], d_branch[...]))

    def result_at(p):
        holder = norm_f if p < 4 else norm_c
        return holder.at[96 * (p % 4) : 96 * (p % 4) + 96, :]

    def out_copies(p, half):
        source = result_at(p)
        low = width * half
        target = (
            out_qk.at[0, :, low : low + width],
            out_vo.at[0, :, low : low + width],
            out_in.at[0, :, low : low + width],
            out_in.at[0, :, 2 * width + low : 3 * width + low],
            out_out.at[0, 48 * half : 48 * half + 48, :],
            out_out.at[0, 96 + 48 * half : 144 + 48 * half, :],
            (out_cqk, out_cvo)[half].at[0],
            (out_cqk, out_cvo)[half].at[0],
        )[p]
        return pltpu.make_async_copy(
            source.at[48 * half : 48 * half + 48], target, out_sem.at[2 + 2 * min(p, 6) + half]
        )

    def finish_piece(scatter, p):
        total = scatter.last(p)
        target = result_at(p)
        if p >= 4:
            target[...] = total
        else:
            target[0:48] = total[:, :width]
            target[48:96] = total[:, width:]
        if p == 7:
            to_encoder.start()
        else:
            out_copies(p, 0).start()
            out_copies(p, 1).start()

    to_encoder = pltpu.make_async_remote_copy(
        result_at(7), result_at(7), peer_send.at[2], peer_recv.at[2], device_id=place.peer(), device_id_type=MESH
    )
    cross_copies = [
        pltpu.make_async_remote_copy(
            x_send.at[128 * c : 128 * c + 128], x_recv.at[128 * c : 128 * c + 128], peer_send.at[3 + c], peer_recv.at[3 + c],
            device_id=place.peer(), device_id_type=MESH,
        )
        for c in range(3)
    ]
    layer_copy = pltpu.make_async_copy(x_send, out_layer.at[0, 0], out_sem.at[0])

    def fold(i):
        return pltpu.make_async_remote_copy(
            small, small_land.at[i], fold_send.at[i], fold_recv.at[i], device_id=place.folds()[i], device_id_type=MESH
        )

    def fold_start(i):
        fold(i).start()

    def fold_end(i):
        fold(i).wait()
        small[...] = small[...] + small_land[i]
        if i < 4:
            fold(i + 1).start()

    @pl.when(encoder)
    def _():
        serve(plan("2.2 3.2 4.1 5.1 2.3 3.3", gather))
        gather.side_arrivals(2)
        gather.side_arrivals(3)
        queue = plan("4.2 5.2 4.3 5.3", gather)
        for part in range(4):
            ffn_up(h_low, 3 * part, 3 * part + 3)
            serve(queue, 1)
        gather.side_arrivals(4)
        gather.side_arrivals(5)
        for c in range(3):
            ffn_down(slice(128 * c, 128 * c + 128))
            norm_pass(norm_f, rstd_f, gains[1:2], biases[5:6], None, x_send, 2 * c, 2 * c + 2)
            cross_copies[c].start()
        layer_copy.start()
        for copy in from_encoder:
            copy.wait_send()
        for p in range(6):
            gather.finish(p)
        layer_copy.wait()
        found = None
        for c in range(3):
            cross_copies[c].wait()
            found = norm_undo(norm_f, rstd_f, gains[1:2], x_recv, grad, d_ffn, 2 * c, 2 * c + 2, found)
        gain, shift, branch = found
        set_small(1, gain)
        set_small(8 + 5, shift)
        set_small(8 + 4, branch)
        scatter = Scatter(
            place, piece_list(w_qk, w_vo, w_in, w_x, None),
            side_c, side_r, land_c, land_r, near_c, near_r, rs2, rr2, ss2, sr2,
        )
        after = functools.partial(finish_piece, scatter)
        grad_w_out(w_x)
        scatter.hand_over(4)
        scatter.hand_over(5)
        ffn_slope()
        scatter.start(4)
        scatter.start(5)
        ffn_hidden()
        queue = plan("4.0 5.0 +2 +3 4.1 5.1 2.0 3.0 4.2 5.2 2.1 3.1 =4 =5", scatter, after)
        serve(queue, 1)
        grad_w_in(h_low)
        scatter.hand_over(2)
        scatter.hand_over(3)
        serve(queue, 1)
        set_b1(0)
        self_back_a(0)
        serve(queue, 3)
        for part in range(3):
            attend_back_pairs(q, k, v, score_bias, lse, None, d_mixed, 2 * part, 2 * part + 2)
            serve(queue, 1)
        self_back_b(0)
        fold_start(0)
        serve(queue, 2)
        self_back_qk()
        scatter.hand_over(0)
        serve(queue, 1)
        self_back_vo()
        scatter.hand_over(1)
        fold_end(0)
        serve(queue, 1)
        scatter.start(0)
        serve(queue, 1)
        scatter.start(1)
        fold_end(1)
        serve(queue)
        queue = plan("2.2 3.2 0.0 1.0 0.1 1.1 =2 =3 0.2 1.2 =0 =1", scatter, after)
        serve(queue, 2)
        fold_end(2)
        serve(queue, 2)
        fold_end(3)
        serve(queue)
        to_encoder.wait_recv()
        out_copies(7, 0).start()
        out_copies(7, 1).start()
        for p in range(6):
            scatter.finish(p)

    @pl.when(decoder)
    def _():
        queue = plan("6.2 +4 7.2 +5 2.1 3.1 6.3 7.3 2.2 3.2 4.0 5.0 4.1 5.1 2.3 3.3 4.2 5.2 4.3 5.3", gather)
        serve(queue, 8)
        gather.side_arrivals(6)
        gather.side_arrivals(7)
        mask_scores(score_bias, segments[0], segments[1], False)

        def cross_query(j):
            at = span_of(j, 256)
            qc[:, at] = (nn(h_low[...], cross_weight(0, at)) + biases[12:13, at]).astype(LOW)

        tiles(0, 3, cross_query)
        serve(queue, 8)
        for c in range(3):
            rows = slice(128 * c, 128 * c + 128)
            cross_copies[c].wait_recv()

            def cross_keys(j):
                at = span_of(j, 256)
                kc[rows, at] = nn(x_recv[rows, :], cross_weight(2, at)).astype(LOW)
                vc[rows, at] = (nn(x_recv[rows, :], cross_weight(3, at)) + biases[13:14, at]).astype(LOW)

            tiles(0, 3, cross_keys)
        attend_pairs(qc, kc, vc, score_bias, oc, None, p_c, 0, 3)
        serve(queue, 2)
        attend_pairs(qc, kc, vc, score_bias, oc, None, p_c, 3, 6)
        serve(queue)
        gather.side_arrivals(2)
        gather.side_arrivals(3)

        def cross_out(j):
            at = span_of(j, 256)
            norm_c[:, at] = h[:, at] + nn(oc[...], cross_weight(1, at)) + biases[14:15, at]

        tiles(0, 3, cross_out)
        norm_pass(norm_c, rstd_c, gains[4:5], biases[15:16], h, h2_low)
        ffn_up(h2_low, 0, 12)
        gather.side_arrivals(4)
        gather.side_arrivals(5)
        ffn_down()
        norm_pass(norm_f, rstd_f, gains[3:4], biases[11:12], None, x_send)
        layer_copy.start()
        cot_load.wait()
        gain, shift, branch = norm_undo(norm_f, rstd_f, gains[3:4], d_mixed, grad, d_ffn)
        set_small(3, gain)
        set_small(8 + 11, shift)
        set_small(8 + 10, branch)
        for p in range(8):
            gather.finish(p)
        scatter = Scatter(
            place, pieces, side_c, side_r, land_c, land_r, near_c, near_r, rs2, rr2, ss2, sr2,
        )
        after = functools.partial(finish_piece, scatter)
        ffn_slope()
        grad_w_out(w_out)
        scatter.hand_over(4)
        scatter.hand_over(5)
        ffn_hidden()
        gain, shift, branch = norm_undo(norm_c, rstd_c, gains[4:5], grad, grad, d_branch)
        set_small(4, gain)
        set_small(8 + 15, shift)
        set_small(8 + 14, branch)
        scatter.start(4)
        scatter.start(5)
        d_mixed[...] = nt(d_branch[...], cross_weight(1)).astype(LOW)
        layer_copy.wait()
        queue = plan("4.0 5.0 4.1 5.1 +2 +3 4.2 5.2 2.0 3.0 =4 =5 +7 2.1 3.1 +6 7.0 2.2 3.2", scatter, after)
        for c in range(3):
            rows = slice(128 * c, 128 * c + 128)
            attend_back_keys(qc, kc, vc, oc, p_c, d_mixed, norm_f, 128 * c, 128, c == 0)
            x_send[rows, :] = (nt(kc[rows, :], cross_weight(2)) + nt(vc[rows, :], cross_weight(3))).astype(LOW)
            cross_copies[c].start()
            serve(queue, 2 if c == 1 else 0)
        qc[...] = norm_f[...].astype(LOW)
        grad_w_in(h2_low)
        scatter.hand_over(2)
        scatter.hand_over(3)
        serve(queue, 2)
        store_cross(2, tn(x_recv[...], kc[...]))
        store_cross(3, tn(x_recv[...], vc[...]))
        scatter.hand_over(7)
        serve(queue, 4)
        grad[...] += nt(qc[...], cross_weight(0))
        store_cross(0, tn(h_low[...], qc[...]))
        store_cross(1, tn(oc[...], d_branch[...]))
        scatter.hand_over(6)
        set_b1(1)
        set_small(8 + 12, column_total(qc))
        set_small(8 + 13, column_total(vc))
        serve(queue, 1)
        mask_scores(score_bias, segments[1], segments[1], True)
        self_back_a(1)
        serve(queue, 3)
        for part in range(3):
            attend_back_pairs(q, k, v, score_bias, lse, None, d_mixed, 2 * part, 2 * part + 2)
            serve(queue, 1)
        self_back_b(1)
        fold_start(0)
        serve(queue, 2)
        self_back_qk()
        scatter.hand_over(0)
        serve(queue, 1)
        self_back_vo()
        scatter.hand_over(1)
        fold_end(0)
        serve(queue)
        scatter.start(0)
        queue = plan("6.0 +1 7.1 6.1 =2 =3 0.0 1.0 7.2 6.2 0.1 1.1 =7 =6 0.2 1.2 =0 =1", scatter, after)
        serve(queue, 3)
        fold_end(1)
        serve(queue, 3)
        fold_end(2)
        serve(queue, 3)
        fold_end(3)
        serve(queue)
        for copy in cross_copies:
            copy.wait_send()
        to_encoder.wait_send()
        for p in range(8):
            scatter.finish(p)

    fold_end(4)
    out_small[...] = small[...]
    for p in range(7):
        for half in range(2):
            out_copies(p, half).wait()
    pltpu.make_async_copy(grad, out_input.at[0, 0], out_sem.at[1]).wait()


def layer_call(tokens, segments, cotangent, attn_qk, attn_vo, cross_qk, cross_vo, ffn_in, ffn_out, gains, biases, ffn_bias):
    length, width = tokens.shape[2:]
    hidden = ffn_in.shape[2]

    def result(like, kind):
        return jax.ShapeDtypeStruct(like.shape, kind)

    def low(*shape):
        return pltpu.VMEM(shape, LOW)

    def full(*shape):
        return pltpu.VMEM(shape, jnp.float32)

    any_space = pl.BlockSpec(memory_space=pl.ANY)
    in_vmem = pl.BlockSpec(memory_space=pltpu.VMEM)
    flat, wide, exact = low(length, width), low(length, hidden), full(length, width)
    dma = pltpu.SemaphoreType.DMA
    scratch = [
        low(CHIPS, 2, 48, 2 * width), low(CHIPS, 2, 48, 2 * width), low(CHIPS, 2, 48, hidden),
        low(CHIPS, 2, 192, width), low(CHIPS, 2, 192, width),
        low(4, CHIPS, 48, 2 * width), low(4, CHIPS, 96, width),
        low(4, 2, 3, 48, 2 * width), low(4, 2, 3, 96, width),
        low(4, 2, 48, width), low(4, 2, 48, width),
        full(32, width), full(5, 32, width),
        full(8, width), full(1, width), full(1, hidden), full(4, 1, width),
        flat, flat, flat, flat, flat, exact, exact, wide, wide, exact, flat, full(length, length), flat, flat,
        flat, flat, flat, low(HEADS, length, length), flat, flat, exact, flat, flat, exact,
        full(HEADS, 1, length), full(length, 128),
        dma((7,)), dma((6,)), dma((6,)),
        dma((8, 2, 4)), dma((8, 2, 4)), dma((8, 9)), dma((8, 9)),
        dma((8, 2, 4)), dma((8, 2, 4)), dma((8,)), dma((8,)),
        dma((5,)), dma((5,)), dma((16,)),
    ]
    return pl.pallas_call(
        layer_kernel,
        out_shape=(
            result(tokens, LOW), result(tokens, jnp.float32),
            result(attn_qk, jnp.float32), result(attn_vo, jnp.float32),
            result(cross_qk, jnp.float32), result(cross_vo, jnp.float32),
            result(ffn_in, jnp.float32), result(ffn_out, jnp.float32),
            jax.ShapeDtypeStruct((32, width), jnp.float32),
        ),
        in_specs=[in_vmem] * 5 + [any_space] * 7,
        out_specs=(any_space,) * 8 + (in_vmem,),
        scratch_shapes=scratch,
        compiler_params=pltpu.CompilerParams(
            collective_id=0, has_side_effects=True, vmem_limit_bytes=63 * 1024 * 1024
        ),
        name="layer_pair",
    )(
        tokens, segments, gains, biases, ffn_bias, cotangent[0],
        attn_qk, attn_vo, cross_qk, cross_vo, ffn_in, ffn_out,
    )


def hand_out_kernel(*refs):
    sources, small, rest = refs[:8], refs[8], refs[9:]
    targets, (gains, biases, ffn_bias), held, (take, give) = rest[:8], rest[8:11], rest[11:19], rest[19:]
    inward = [pltpu.make_async_copy(a, b, take.at[i]) for i, (a, b) in enumerate(zip(sources, held))]
    outward = [pltpu.make_async_copy(a, b, give.at[i]) for i, (a, b) in enumerate(zip(held, targets))]
    for copy in inward:
        copy.start()
    gains[...] = small[0:5]
    biases[...] = small[8:24]
    width = gains.shape[1]
    for row in range(8):
        ffn_bias[row // 4 : row // 4 + 1, width * (row % 4) : width * (row % 4 + 1)] = small[24 + row : 25 + row]
    for first, second in zip(inward, outward):
        first.wait()
        second.start()
    for copy in outward:
        copy.wait()


def hand_out(results, gains, biases, ffn_bias):
    any_space = pl.BlockSpec(memory_space=pl.ANY)
    in_vmem = pl.BlockSpec(memory_space=pltpu.VMEM)
    return pl.pallas_call(
        hand_out_kernel,
        out_shape=tuple(jax.ShapeDtypeStruct(r.shape, r.dtype) for r in tuple(results[:8]) + (gains, biases, ffn_bias)),
        in_specs=[any_space] * 8 + [in_vmem],
        out_specs=(any_space,) * 8 + (in_vmem,) * 3,
        scratch_shapes=[pltpu.VMEM(r.shape, r.dtype) for r in results[:8]] + [pltpu.SemaphoreType.DMA((8,))] * 2,
        compiler_params=pltpu.CompilerParams(vmem_limit_bytes=32 * 1024 * 1024),
        name="hand_out",
    )(*results)


def local_ring(
    tokens, segments, cotangent, attn_qk, attn_vo, cross_qk, cross_vo, ffn_in, ffn_out, gains, biases, ffn_bias
):
    results = layer_call(
        tokens, segments, cotangent, attn_qk, attn_vo, cross_qk, cross_vo, ffn_in, ffn_out, gains, biases, ffn_bias
    )
    return hand_out(results, gains, biases, ffn_bias)


def solution(mesh):
    any_size = mesh.shape["section"] != 2 or mesh.shape["dp"] != 2 * CHIPS
    placed = (
        P("section", "dp", None, None),
        P(None, "dp", None),
        P("dp", None, None),
        P("section", "dp", None),
        P("section", "dp", None),
        P("section", "dp", None),
        P("section", "dp", None),
        P("section", "dp", None),
        P("section", "dp", None),
        P(),
        P(),
        P(),
    )
    return jax.shard_map(
        local_any if any_size else local_ring,
        mesh=mesh,
        in_specs=placed,
        out_specs=(
            P("section", "dp", None, None),
            P("section", "dp", None, None),
            P("section", "dp", None),
            P("section", "dp", None),
            P("section", "dp", None),
            P("section", "dp", None),
            P("section", "dp", None),
            P("section", "dp", None),
            P(),
            P(),
            P(),
        ),
        check_vma=False,
    )
```

```python
import functools

import jax
import jax.numpy as jnp
from jax import lax
from jax.experimental import pallas as pl
from jax.experimental.pallas import tpu as pltpu
from jax.sharding import PartitionSpec as P

HEADS = 12


NORM_EPSILON = 1e-05


def from_behind(x, axis, by):
    devices = lax.axis_size(axis)
    pairs = [(i, i + by) for i in range(devices) if 0 <= i + by < devices]
    return lax.ppermute(x, axis, pairs)


def product(left, right):
    return jnp.einsum("rld,de->rle", left, right, preferred_element_type=jnp.float32)


def back_product(grad, right):
    return jnp.einsum("rle,de->rld", grad, right, preferred_element_type=jnp.float32)


def weight_grad(left, grad):
    return jnp.einsum("rld,rle->de", left, grad, preferred_element_type=jnp.float32)


def column_sum(values):
    return jnp.sum(values.astype(jnp.float32), axis=(0, 1))


def norm_rows(resid, gain, shift):
    center = resid - jnp.mean(resid, axis=-1, keepdims=True)
    spread = jnp.mean(center * center, axis=-1, keepdims=True)
    return center * lax.rsqrt(spread + NORM_EPSILON) * gain + shift


def norm_back(resid, gain, shift, grad):
    unused, pull = jax.vjp(norm_rows, resid, gain, shift)
    return pull(grad)


def split_heads(values, head_count):
    return values.reshape(
        values.shape[0], values.shape[1], head_count, values.shape[2] // head_count
    )


def masked_scores(query_heads, key_heads, allowed):
    scale = query_heads.shape[-1] ** (-0.5)
    scores = (
        jnp.einsum("rqhe,rkhe->rhqk", query_heads, key_heads, preferred_element_type=jnp.float32)
        * scale
    )
    return jnp.where(allowed[:, None], scores, -1e30)


def attend(query, key_rows, value_rows, allowed, head_count):
    query_heads = split_heads(query, head_count)
    scores = masked_scores(query_heads, split_heads(key_rows, head_count), allowed)
    peak = jnp.max(scores, axis=-1, keepdims=True)
    exponent = jnp.exp(scores - peak)
    summed = jnp.sum(exponent, axis=-1, keepdims=True)
    soft = (exponent / summed).astype(jnp.bfloat16)
    mixed = jnp.einsum(
        "rhqk,rkhe->rqhe",
        soft,
        split_heads(value_rows, head_count),
        preferred_element_type=jnp.float32,
    )
    return (mixed.reshape(query.shape), peak + jnp.log(summed))


def attend_back(query, key_rows, value_rows, allowed, log_total, grad_mixed, head_count):
    query_heads = split_heads(query, head_count)
    key_heads = split_heads(key_rows, head_count)
    value_heads = split_heads(value_rows, head_count)
    grad_heads = split_heads(grad_mixed, head_count)
    scale = query_heads.shape[-1] ** (-0.5)
    soft = jnp.exp(masked_scores(query_heads, key_heads, allowed) - log_total)
    grad_values = jnp.einsum(
        "rhqk,rqhe->rkhe", soft.astype(jnp.bfloat16), grad_heads, preferred_element_type=jnp.float32
    )
    grad_soft = jnp.einsum(
        "rqhe,rkhe->rhqk", grad_heads, value_heads, preferred_element_type=jnp.float32
    )
    inner_sum = jnp.sum(soft * grad_soft, axis=-1, keepdims=True)
    grad_scores = (soft * (grad_soft - inner_sum)).astype(jnp.bfloat16)
    grad_query = (
        jnp.einsum("rhqk,rkhe->rqhe", grad_scores, key_heads, preferred_element_type=jnp.float32)
        * scale
    )
    grad_keys = (
        jnp.einsum("rhqk,rqhe->rkhe", grad_scores, query_heads, preferred_element_type=jnp.float32)
        * scale
    )
    return (
        grad_query.reshape(query.shape),
        grad_keys.reshape(key_rows.shape),
        grad_values.reshape(key_rows.shape),
    )


def self_forward(inputs, w_qk, w_vo, section_bias, gain, allowed, head_count):
    model_width = inputs.shape[-1]
    query = (product(inputs, w_qk[:, :model_width]) + section_bias[0]).astype(jnp.bfloat16)
    key_rows = product(inputs, w_qk[:, model_width:]).astype(jnp.bfloat16)
    value_rows = (product(inputs, w_vo[:, :model_width]) + section_bias[1]).astype(jnp.bfloat16)
    mixed, log_total = attend(query, key_rows, value_rows, allowed, head_count)
    mixed = mixed.astype(jnp.bfloat16)
    resid = inputs.astype(jnp.float32) + product(mixed, w_vo[:, model_width:]) + section_bias[2]
    return (
        norm_rows(resid, gain, section_bias[3]),
        (query, key_rows, value_rows, log_total, mixed, resid),
    )


def self_backward(inputs, w_qk, w_vo, section_bias, gain, allowed, head_count, kept, grad_hidden):
    query, key_rows, value_rows, log_total, mixed, resid = kept
    model_width = inputs.shape[-1]
    grad_resid, grad_gain, grad_shift = norm_back(resid, gain, section_bias[3], grad_hidden)
    grad_branch = grad_resid.astype(jnp.bfloat16)
    grad_mixed = back_product(grad_branch, w_vo[:, model_width:]).astype(jnp.bfloat16)
    grad_query, grad_keys, grad_values = attend_back(
        query, key_rows, value_rows, allowed, log_total, grad_mixed, head_count
    )
    grad_query = grad_query.astype(jnp.bfloat16)
    grad_keys = grad_keys.astype(jnp.bfloat16)
    grad_values = grad_values.astype(jnp.bfloat16)
    grad_pair = jnp.concatenate([grad_query, grad_keys], axis=-1)
    grad_inputs = (
        grad_resid
        + back_product(grad_pair, w_qk)
        + back_product(grad_values, w_vo[:, :model_width])
    )
    grad_rows = jnp.stack(
        [column_sum(grad_query), column_sum(grad_values), column_sum(grad_branch), grad_shift]
    )
    return (grad_inputs, (inputs, grad_pair, grad_values, mixed, grad_branch), grad_rows, grad_gain)


def ffn_forward(hidden, w_in, w_out, b_in, b_out):
    hidden_low = hidden.astype(jnp.bfloat16)
    pre_act = product(hidden_low, w_in) + b_in
    activated = jax.nn.gelu(pre_act, approximate=False).astype(jnp.bfloat16)
    return (product(activated, w_out) + b_out, (hidden_low, pre_act, activated))


def gelu_exact(values):
    return jax.nn.gelu(values, approximate=False)


def ffn_backward(w_in, w_out, kept, grad_branch):
    hidden_low, pre_act, activated = kept
    grad_low = grad_branch.astype(jnp.bfloat16)
    grad_act = back_product(grad_low, w_out)
    unused, pull = jax.vjp(gelu_exact, pre_act)
    grad_pre = pull(grad_act)[0].astype(jnp.bfloat16)
    grad_hidden = back_product(grad_pre, w_in)
    return (
        grad_hidden,
        (hidden_low, grad_pre, activated, grad_low),
        column_sum(grad_pre),
        column_sum(grad_low),
    )


def encoder_forward(hidden, w_in, w_out, b_in, section_bias, gain_last, w_ck, w_cv, bias_cv):
    branch, kept = ffn_forward(hidden, w_in, w_out, b_in, section_bias[4])
    resid = hidden + branch
    memory = norm_rows(resid, gain_last, section_bias[5]).astype(jnp.bfloat16)
    key_rows = product(memory, w_ck).astype(jnp.bfloat16)
    value_rows = (product(memory, w_cv) + bias_cv).astype(jnp.bfloat16)
    return (memory, key_rows, value_rows, resid, kept)


def encoder_backward(
    w_in, w_out, section_bias, gain_last, w_ck, w_cv, memory, resid, kept, grad_keys, grad_values
):
    grad_memory = back_product(grad_keys, w_ck) + back_product(grad_values, w_cv)
    grad_last, grad_gain, grad_shift = norm_back(resid, gain_last, section_bias[5], grad_memory)
    grad_ffn, ffn_ops, grad_bin, grad_bout = ffn_backward(w_in, w_out, kept, grad_last)
    zero_line = jnp.zeros_like(grad_gain)
    cross_rows = jnp.stack([zero_line, column_sum(grad_values), zero_line, zero_line])
    operands = (memory, grad_keys, memory, grad_values) + ffn_ops
    return (
        grad_last + grad_ffn,
        operands,
        grad_bin,
        grad_bout,
        grad_gain,
        grad_shift,
        cross_rows,
        zero_line,
    )


def decoder_step(
    hidden,
    w_cq,
    w_co,
    w_in,
    w_out,
    b_in,
    section_bias,
    gain_last,
    gain_cross,
    cross_bias,
    key_rows,
    value_rows,
    allowed,
    cotangent,
    head_count,
):
    hidden_low = hidden.astype(jnp.bfloat16)
    query = (product(hidden_low, w_cq) + cross_bias[0]).astype(jnp.bfloat16)
    mixed, log_total = attend(query, key_rows, value_rows, allowed, head_count)
    mixed = mixed.astype(jnp.bfloat16)
    resid_mid = hidden + product(mixed, w_co) + cross_bias[2]
    middle = norm_rows(resid_mid, gain_cross, cross_bias[3])
    branch, kept = ffn_forward(middle, w_in, w_out, b_in, section_bias[4])
    resid_last = middle + branch
    result = norm_rows(resid_last, gain_last, section_bias[5])
    grad_last, grad_gain, grad_shift = norm_back(
        resid_last, gain_last, section_bias[5], cotangent.astype(jnp.float32)
    )
    grad_ffn, ffn_ops, grad_bin, grad_bout = ffn_backward(w_in, w_out, kept, grad_last)
    grad_mid, grad_gain_cross, grad_shift_cross = norm_back(
        resid_mid, gain_cross, cross_bias[3], grad_last + grad_ffn
    )
    grad_branch = grad_mid.astype(jnp.bfloat16)
    grad_mixed = back_product(grad_branch, w_co).astype(jnp.bfloat16)
    grad_query, grad_keys, grad_values = attend_back(
        query, key_rows, value_rows, allowed, log_total, grad_mixed, head_count
    )
    grad_query = grad_query.astype(jnp.bfloat16)
    grad_hidden = grad_mid + back_product(grad_query, w_cq)
    cross_rows = jnp.stack(
        [
            column_sum(grad_query),
            jnp.zeros_like(grad_gain),
            column_sum(grad_branch),
            grad_shift_cross,
        ]
    )
    operands = (hidden_low, grad_query, mixed, grad_branch) + ffn_ops
    tail_result = (
        grad_hidden,
        operands,
        grad_bin,
        grad_bout,
        grad_gain,
        grad_shift,
        cross_rows,
        grad_gain_cross,
    )
    return (
        result.astype(jnp.bfloat16),
        grad_keys.astype(jnp.bfloat16),
        grad_values.astype(jnp.bfloat16),
        tail_result,
    )


def zero_tail(hidden, w_in):
    model_width = hidden.shape[-1]
    ffn_width = w_in.shape[1]
    flat = jnp.zeros(hidden.shape, jnp.bfloat16)
    wide = jnp.zeros((hidden.shape[0], hidden.shape[1], ffn_width), jnp.bfloat16)
    zero_line = jnp.zeros((model_width,), jnp.float32)
    operands = (flat, flat, flat, flat, flat, wide, wide, flat)
    return (
        jnp.zeros_like(hidden),
        operands,
        jnp.zeros((ffn_width,), jnp.float32),
        zero_line,
        zero_line,
        zero_line,
        jnp.zeros((4, model_width), jnp.float32),
        zero_line,
    )


def tail_whole(operands):
    return (
        weight_grad(operands[0], operands[1]),
        weight_grad(operands[2], operands[3]),
        weight_grad(operands[4], operands[5]),
        weight_grad(operands[6], operands[7]),
    )


def self_whole(operands):
    grad_qk = weight_grad(operands[0], operands[1])
    grad_vo = jnp.concatenate(
        [weight_grad(operands[0], operands[2]), weight_grad(operands[3], operands[4])], axis=1
    )
    return (grad_qk, grad_vo)


def local_any(
    tokens,
    segments,
    cotangent,
    attn_qk,
    attn_vo,
    cross_qk,
    cross_vo,
    ffn_in,
    ffn_out,
    gains,
    biases,
    ffn_bias,
):
    head_count = HEADS
    section_index = lax.axis_index("section")
    is_enc = section_index == 0
    qk_whole, vo_whole = (
        lax.all_gather(attn_qk, "dp", axis=1, tiled=True),
        lax.all_gather(attn_vo, "dp", axis=1, tiled=True),
    )
    w_qk = qk_whole[0]
    w_vo = vo_whole[0]
    cqk_whole, cvo_whole, in_whole, out_whole = (
        lax.all_gather(cross_qk, "dp", axis=1, tiled=True),
        lax.all_gather(cross_vo, "dp", axis=1, tiled=True),
        lax.all_gather(ffn_in, "dp", axis=1, tiled=True),
        lax.all_gather(ffn_out, "dp", axis=1, tiled=True),
    )
    w_cqk = cqk_whole[0]
    w_cvo = cvo_whole[0]
    w_in = in_whole[0]
    w_out = out_whole[0]
    section_bias = lax.dynamic_slice_in_dim(biases, 6 * section_index, 6, 0)
    section_gain = lax.dynamic_slice_in_dim(gains, 2 * section_index, 2, 0)
    bias_in = lax.dynamic_index_in_dim(ffn_bias, section_index, 0, keepdims=False)
    section_seg = lax.dynamic_index_in_dim(segments, section_index, 0, keepdims=False)
    length = tokens.shape[2]
    position = jnp.arange(length)
    earlier = position[None, :] <= position[:, None]
    allowed_self = (section_seg[:, :, None] == section_seg[:, None, :]) & (earlier[None] | is_enc)
    allowed_cross = segments[1][:, :, None] == segments[0][:, None, :]
    source = tokens[0]
    hidden_one, kept_self = self_forward(
        source, w_qk, w_vo, section_bias, section_gain[0], allowed_self, head_count
    )

    def run_encoder():
        return encoder_forward(
            hidden_one,
            w_in,
            w_out,
            bias_in,
            section_bias,
            section_gain[1],
            w_cqk,
            w_cvo,
            biases[13],
        )

    def skip_encoder():
        flat = jnp.zeros(hidden_one.shape, jnp.bfloat16)
        wide_shape = (hidden_one.shape[0], hidden_one.shape[1], w_in.shape[1])
        return (
            flat,
            flat,
            flat,
            jnp.zeros_like(hidden_one),
            (flat, jnp.zeros(wide_shape, jnp.float32), jnp.zeros(wide_shape, jnp.bfloat16)),
        )

    memory, enc_keys, enc_values, enc_resid, enc_kept = lax.cond(is_enc, run_encoder, skip_encoder)
    got_keys, got_values = from_behind((enc_keys, enc_values), "section", 1)

    def run_decoder():
        return decoder_step(
            hidden_one,
            w_cqk,
            w_cvo,
            w_in,
            w_out,
            bias_in,
            section_bias,
            section_gain[1],
            gains[4],
            biases[12:16],
            got_keys,
            got_values,
            allowed_cross,
            cotangent,
            head_count,
        )

    def skip_decoder():
        flat = jnp.zeros(hidden_one.shape, jnp.bfloat16)
        return (flat, flat, flat, zero_tail(hidden_one, w_in))

    decoded, grad_keys, grad_values, dec_tail = lax.cond(is_enc, skip_decoder, run_decoder)
    back_keys, back_values = from_behind((grad_keys, grad_values), "section", -1)

    def run_encoder_back():
        return encoder_backward(
            w_in,
            w_out,
            section_bias,
            section_gain[1],
            w_cqk,
            w_cvo,
            memory,
            enc_resid,
            enc_kept,
            back_keys,
            back_values,
        )

    def keep_decoder():
        return dec_tail

    tail_result = lax.cond(is_enc, run_encoder_back, keep_decoder)
    (
        grad_hidden,
        tail_ops,
        grad_bin,
        grad_bout,
        grad_gain_last,
        grad_shift_last,
        cross_rows,
        grad_gain_cross,
    ) = tail_result
    layer_out = jnp.where(is_enc, memory, decoded)
    model_width = source.shape[-1]
    grad_ca, grad_cb, grad_in, grad_out = tail_whole(tail_ops)
    tail_parts = (
        lax.psum_scatter(grad_ca[None], "dp", scatter_dimension=1, tiled=True),
        lax.psum_scatter(grad_cb[None], "dp", scatter_dimension=1, tiled=True),
        lax.psum_scatter(grad_in[None], "dp", scatter_dimension=1, tiled=True),
        lax.psum_scatter(grad_out[None], "dp", scatter_dimension=1, tiled=True),
    )
    grad_source, self_ops, self_rows, grad_gain_first = self_backward(
        source,
        w_qk,
        w_vo,
        section_bias,
        section_gain[0],
        allowed_self,
        head_count,
        kept_self,
        grad_hidden,
    )
    grad_qk, grad_vo = self_whole(self_ops)
    attn_parts = (
        lax.psum_scatter(grad_qk[None], "dp", scatter_dimension=1, tiled=True),
        lax.psum_scatter(grad_vo[None], "dp", scatter_dimension=1, tiled=True),
    )
    large_parts = tuple(attn_parts) + tuple(tail_parts)
    section_rows = jnp.concatenate([self_rows, jnp.stack([grad_bout, grad_shift_last])], axis=0)
    bias_block = lax.dynamic_update_slice_in_dim(
        jnp.zeros((12, model_width), jnp.float32), section_rows, 6 * section_index, 0
    )
    grad_biases = jnp.concatenate([bias_block, cross_rows], axis=0)
    gain_block = lax.dynamic_update_slice_in_dim(
        jnp.zeros((4, model_width), jnp.float32),
        jnp.stack([grad_gain_first, grad_gain_last]),
        2 * section_index,
        0,
    )
    grad_gains = jnp.concatenate([gain_block, grad_gain_cross[None]], axis=0)
    grad_fbias = lax.dynamic_update_slice_in_dim(
        jnp.zeros_like(ffn_bias), grad_bin[None], section_index, 0
    )
    sum_gains, sum_biases, sum_fbias = lax.psum(
        (grad_gains, grad_biases, grad_fbias), ("section", "dp")
    )
    return (
        layer_out[None],
        grad_source[None],
        large_parts[0],
        large_parts[1],
        large_parts[2],
        large_parts[3],
        large_parts[4],
        large_parts[5],
        sum_gains,
        sum_biases,
        sum_fbias,
    )


MESH = pl.DeviceIdType.MESH
LOW = jnp.bfloat16
CHIPS = 8
FAR = 3
MASKED = -1e30


class Place:
    def __init__(self):
        self.section = lax.axis_index("section")
        shard = lax.axis_index("dp")
        self.core = shard % 2
        self.chip = shard // 2
        self.across = self.chip % 2
        self.along = self.chip // 2
        self.pos = self.along + self.across * (7 - 2 * self.along)

    def chip_at(self, step):
        spot = (self.pos + step + CHIPS) % CHIPS
        across = spot // 4
        along = spot + across * (7 - 2 * spot)
        return along * 2 + across

    def ring(self, step):
        return (self.section, self.chip_at(step) * 2 + self.core)

    def sibling(self):
        return (self.section, self.chip * 2 + 1 - self.core)

    def peer(self):
        return (1 - self.section, self.chip * 2 + self.core)

    def folds(self):
        near = self.along + 1 - 2 * (self.along % 2)
        far = (self.along + 2) % 4
        return (
            self.sibling(),
            (self.section, (self.along * 2 + 1 - self.across) * 2 + self.core),
            (self.section, (near * 2 + self.across) * 2 + self.core),
            (self.section, (far * 2 + self.across) * 2 + self.core),
            self.peer(),
        )


def enter(place):
    barrier = pltpu.get_barrier_semaphore()
    others = (place.ring(1), place.ring(-1)) + place.folds()
    for other in others:
        pl.semaphore_signal(barrier, inc=1, device_id=other, device_id_type=MESH)
    pl.semaphore_wait(barrier, len(others))


class Piece:
    def __init__(self, ref, by_rows, low, span, slot):
        self.ref, self.by_rows, self.low, self.span, self.slot = ref, by_rows, low, span, slot

    def at(self, chip, core, half=None):
        low, span = self.low, self.span
        if half is not None:
            span = span // 2
            low = low + half * span
        if self.by_rows:
            return self.ref.at[chip, core, low : low + span, :]
        return self.ref.at[chip, core, :, low : low + span]


def piece_list(qk, vo, w_in, w_out, cross):
    return [
        Piece(qk, False, 0, 1536, 0),
        Piece(vo, False, 0, 1536, 1),
        Piece(w_in, False, 0, 1536, 2),
        Piece(w_in, False, 1536, 1536, 3),
        Piece(w_out, True, 0, 96, 0),
        Piece(w_out, True, 96, 96, 1),
        Piece(cross, True, 0, 96, 2),
        Piece(cross, True, 96, 96, 3),
    ]


class Gather:
    def __init__(self, place, pieces, ring_send, ring_recv, side_send, side_recv):
        self.place, self.pieces = place, pieces
        self.ring_send, self.ring_recv, self.side_send, self.side_recv = ring_send, ring_recv, side_send, side_recv

    def ring_copy(self, p, way, hop):
        sign = 1 - 2 * way
        ref = self.pieces[p].at(self.place.chip_at(-sign * hop), self.place.core, way if hop == FAR else None)
        return pltpu.make_async_remote_copy(
            ref, ref, self.ring_send.at[p, way, hop], self.ring_recv.at[p, way, hop],
            device_id=self.place.ring(sign), device_id_type=MESH,
        )

    def arrival(self, p, way, hop, core):
        sign = 1 - 2 * way
        return self.pieces[p].at(self.place.chip_at(-sign * (hop + 1)), core, way if hop == FAR else None)

    def side_copy(self, p, k, core):
        if k == 0:
            ref = self.pieces[p].at(self.place.chip, core)
        else:
            ref = self.arrival(p, (k - 1) // 4, (k - 1) % 4, core)
        return pltpu.make_async_remote_copy(
            ref, ref, self.side_send.at[p, k], self.side_recv.at[p, k],
            device_id=self.place.sibling(), device_id_type=MESH,
        )

    def start(self, p):
        self.ring_copy(p, 0, 0).start()
        self.ring_copy(p, 1, 0).start()
        self.side_copy(p, 0, self.place.core).start()

    def event(self, p, way, hop):
        ref = self.arrival(p, way, hop, self.place.core)
        pltpu.make_async_remote_copy(
            ref, ref, self.ring_send.at[p, way, hop], self.ring_recv.at[p, way, hop],
            device_id=self.place.ring(1), device_id_type=MESH,
        ).wait_recv()
        if hop < FAR:
            self.ring_copy(p, way, hop + 1).start()
        self.side_copy(p, 1 + 4 * way + hop, self.place.core).start()

    def side_arrivals(self, p):
        for k in range(9):
            self.side_copy(p, k, 1 - self.place.core).wait_recv()

    def finish(self, p):
        for way in range(2):
            for hop in range(4):
                self.ring_copy(p, way, hop).wait_send()
        for k in range(9):
            self.side_copy(p, k, self.place.core).wait_send()


class Scatter:
    def __init__(self, place, pieces, side_c, side_r, land_c, land_r, near_c, near_r, ring_send, ring_recv, side_send, side_recv):
        self.place, self.pieces = place, pieces
        self.side_c, self.side_r, self.land_c, self.land_r = side_c, side_r, land_c, land_r
        self.near_c, self.near_r = near_c, near_r
        self.ring_send, self.ring_recv, self.side_send, self.side_recv = ring_send, ring_recv, side_send, side_recv

    def cut(self, p, ref, half):
        piece = self.pieces[p]
        if half is None:
            return ref
        span = piece.span // 2
        if piece.by_rows:
            return ref.at[half * span : (half + 1) * span, :]
        return ref.at[:, half * span : (half + 1) * span]

    def from_side(self, p, chip, half=None):
        piece = self.pieces[p]
        return self.cut(p, (self.side_r if piece.by_rows else self.side_c).at[piece.slot, chip], half)

    def landed(self, p, way, step, half=None):
        piece = self.pieces[p]
        if step == 0:
            return (self.near_r if piece.by_rows else self.near_c).at[piece.slot, way]
        return self.cut(p, (self.land_r if piece.by_rows else self.land_c).at[piece.slot, way, step - 1], half)

    def side_copy(self, p):
        piece = self.pieces[p]
        span = slice(piece.low, piece.low + piece.span)
        other = 1 - self.place.core
        src = piece.ref.at[:, other, span, :] if piece.by_rows else piece.ref.at[:, other, :, span]
        dst = (self.side_r if piece.by_rows else self.side_c).at[piece.slot]
        return pltpu.make_async_remote_copy(
            src, dst, self.side_send.at[p], self.side_recv.at[p],
            device_id=self.place.sibling(), device_id_type=MESH,
        )

    def chip_of(self, way, step):
        sign = 1 - 2 * way
        return self.place.chip_at(sign * (4 - step))

    def ring_copy(self, p, way, step):
        sign = 1 - 2 * way
        half = way if step == 0 else None
        return pltpu.make_async_remote_copy(
            self.pieces[p].at(self.chip_of(way, step), self.place.core, half), self.landed(p, way, step, half),
            self.ring_send.at[p, way, step], self.ring_recv.at[p, way, step],
            device_id=self.place.ring(sign), device_id_type=MESH,
        )

    def hand_over(self, p):
        self.side_copy(p).start()

    def start(self, p):
        self.side_copy(p).wait_recv()
        for way in range(2):
            chip = self.chip_of(way, 0)
            own = self.pieces[p].at(chip, self.place.core, way)
            total = own[...].astype(jnp.float32) + self.from_side(p, chip, way)[...].astype(jnp.float32)
            own[...] = total.astype(LOW)
            self.ring_copy(p, way, 0).start()

    def event(self, p, way, step):
        self.ring_copy(p, way, step).wait_recv()
        chip = self.chip_of(way, step + 1)
        for half in range(2):
            own = self.pieces[p].at(chip, self.place.core, half)
            total = own[...].astype(jnp.float32) + self.from_side(p, chip, half)[...].astype(jnp.float32)
            if step > 0 or half == way:
                total = total + self.landed(p, way, step, half)[...].astype(jnp.float32)
            own[...] = total.astype(LOW)
        self.ring_copy(p, way, step + 1).start()

    def last(self, p):
        chip = self.place.chip
        total = self.pieces[p].at(chip, self.place.core)[...].astype(jnp.float32)
        total = total + self.from_side(p, chip)[...].astype(jnp.float32)
        for way in range(2):
            self.ring_copy(p, way, 3).wait_recv()
            total = total + self.landed(p, way, 3)[...].astype(jnp.float32)
        return total

    def finish(self, p):
        self.side_copy(p).wait_send()
        for way in range(2):
            for step in range(4):
                self.ring_copy(p, way, step).wait_send()


def plan(ring, after, *words):
    found = []
    for word in words:
        if word[0] == "+":
            found.append([functools.partial(ring.start, int(word[1:]))])
        elif word[0] in "=f":
            found.append([functools.partial(after, word)])
        else:
            p, step = (int(part) for part in word.split("."))
            found.append([functools.partial(ring.event, p, way, step) for way in range(2)])
    return found


def serve(queue, count=None):
    for _ in range(len(queue) if count is None else min(count, len(queue))):
        for step in queue.pop(0):
            step()


def nn(left, right):
    return jnp.dot(left, right, preferred_element_type=jnp.float32)


def nt(left, right):
    return lax.dot_general(left, right, (((1,), (1,)), ((), ())), preferred_element_type=jnp.float32)


def tn(left, right):
    return lax.dot_general(left, right, (((0,), (0,)), ((), ())), preferred_element_type=jnp.float32)


def tiles(low, high, body):
    def step(j, carry):
        body(j)
        return carry

    lax.fori_loop(low, high, step, 0, unroll=min(6, high - low))


def span_of(j, width):
    return pl.ds(pl.multiple_of(j * width, width), width)


def columns_of(ref, at, rows=slice(None)):
    block = ref[:, :, rows, at]
    return block.reshape(block.shape[0] * block.shape[1] * block.shape[2], block.shape[3])


def head_masks(length, value):
    lane = lax.broadcasted_iota(jnp.int32, (length, 128), 1)
    first = jnp.where(lane < 64, value, 0.0).astype(LOW)
    second = jnp.where(lane < 64, 0.0, value).astype(LOW)
    return first, second


def mask_scores(bias_ref, key_row, query_row, causal):
    length = bias_ref.shape[0]
    keys = jnp.transpose(jnp.broadcast_to(key_row.astype(jnp.float32), (128, length)))
    keys = jnp.concatenate([keys] * (length // 128), axis=1)
    same = keys == jnp.broadcast_to(query_row.astype(jnp.float32), (length, length))
    if causal:
        key_at = lax.broadcasted_iota(jnp.int32, (length, length), 0)
        query_at = lax.broadcasted_iota(jnp.int32, (length, length), 1)
        same = same & (key_at <= query_at)
    bias_ref[...] = jnp.where(same, 0.0, MASKED)


def attend_pairs(q_ref, k_ref, v_ref, bias_ref, o_ref, lse_ref, p_ref, low, high):
    masks = head_masks(q_ref.shape[0], 0.125)

    def pair(i):
        at = span_of(i, 128)
        q2, k2 = q_ref[:, at], k_ref[:, at]
        v_turned = jnp.transpose(v_ref[:, at])
        parts = []
        for h in range(2):
            scores = nt(k2 * masks[h], q2) + bias_ref[...]
            peak = jnp.max(scores, axis=0, keepdims=True)
            exponent = jnp.exp(scores - peak)
            summed = jnp.sum(exponent, axis=0, keepdims=True)
            soft = (exponent * (1.0 / summed)).astype(LOW)
            if p_ref is not None:
                p_ref[2 * i + h] = soft
            if lse_ref is not None:
                lse_ref[2 * i + h] = peak + jnp.log(summed)
            parts.append(nn(v_turned[64 * h : 64 * h + 64], soft))
        o_ref[:, at] = jnp.transpose(jnp.concatenate(parts, axis=0)).astype(LOW)

    tiles(low, high, pair)


def attend_back_pairs(q_ref, k_ref, v_ref, bias_ref, lse_ref, p_ref, do_ref, low, high):
    masks = head_masks(q_ref.shape[0], 0.125)
    ones = head_masks(q_ref.shape[0], 1.0)

    def pair(i):
        at = span_of(i, 128)
        q2, k2, v2, do2 = q_ref[:, at], k_ref[:, at], v_ref[:, at], do_ref[:, at]
        k_turned = jnp.transpose(k2)
        parts = []
        dk = dv = None
        for h in range(2):
            if p_ref is not None:
                low_soft = p_ref[2 * i + h]
                soft = low_soft.astype(jnp.float32)
            else:
                soft = jnp.exp(nt(k2 * masks[h], q2) + bias_ref[...] - lse_ref[2 * i + h])
                low_soft = soft.astype(LOW)
            dv_h = nn(low_soft, do2 * ones[h])
            d_soft = nt(v2 * ones[h], do2)
            inner = jnp.sum(soft * d_soft, axis=0, keepdims=True)
            d_scores = (soft * (d_soft - inner)).astype(LOW)
            dk_h = nn(d_scores, q2 * masks[h])
            parts.append(nn(k_turned[64 * h : 64 * h + 64], d_scores))
            dk = dk_h if dk is None else dk + dk_h
            dv = dv_h if dv is None else dv + dv_h
        q_ref[:, at] = (jnp.transpose(jnp.concatenate(parts, axis=0)) * 0.125).astype(LOW)
        k_ref[:, at] = dk.astype(LOW)
        v_ref[:, at] = dv.astype(LOW)

    tiles(low, high, pair)


def attend_back_keys(q_ref, k_ref, v_ref, o_ref, p_ref, do_ref, dq_ref, low, span, first):
    masks = head_masks(q_ref.shape[0], 0.125)
    ones = head_masks(q_ref.shape[0], 1.0)
    short = head_masks(span, 1.0)
    rows = slice(low, low + span)

    def pair(i):
        at = span_of(i, 128)
        q2, k2, v2, do2 = q_ref[:, at], k_ref[rows, at], v_ref[rows, at], do_ref[:, at]
        k_turned = jnp.transpose(k2)
        inner = jnp.transpose(do2.astype(jnp.float32) * o_ref[:, at].astype(jnp.float32))
        parts = []
        dk = dv = None
        for h in range(2):
            low_soft = p_ref[2 * i + h, rows, :]
            soft = low_soft.astype(jnp.float32)
            dv_h = nn(low_soft, do2 * ones[h])
            d_soft = nt(v2 * short[h], do2)
            total = jnp.sum(inner[64 * h : 64 * h + 64], axis=0, keepdims=True)
            d_scores = (soft * (d_soft - total)).astype(LOW)
            dk_h = nn(d_scores, q2 * masks[h])
            parts.append(nn(k_turned[64 * h : 64 * h + 64], d_scores))
            dk = dk_h if dk is None else dk + dk_h
            dv = dv_h if dv is None else dv + dv_h
        dq = jnp.transpose(jnp.concatenate(parts, axis=0)) * 0.125
        dq_ref[:, at] = dq if first else dq_ref[:, at] + dq
        k_ref[rows, at] = dk.astype(LOW)
        v_ref[rows, at] = dv.astype(LOW)

    tiles(0, q_ref.shape[1] // 128, pair)


def gelu_parts(u):
    size = jnp.abs(u)
    bell = jnp.exp(-0.5 * u * u)
    t = 1.0 / (1.0 + 0.2316419 * size)
    tail = t * (0.127414796 + t * (-0.142248368 + t * (0.710706870 + t * (-0.726576013 + t * 0.530702714)))) * bell
    upper = jnp.where(u < 0, tail, 1.0 - tail)
    return u * upper, upper + u * bell * 0.3989422804014327


def norm_pass(norm_ref, rstd_ref, gain, shift, hidden_ref, low_ref, first=0, last=6):
    def rows(j):
        at = span_of(j, 64)
        resid = norm_ref[at, :]
        center = resid - jnp.mean(resid, axis=-1, keepdims=True)
        rstd = lax.rsqrt(jnp.mean(center * center, axis=-1, keepdims=True) + NORM_EPSILON)
        normal = center * rstd
        norm_ref[at, :] = normal
        rstd_ref[0][at, rstd_ref[1]] = rstd
        result = normal * gain + shift
        if hidden_ref is not None:
            hidden_ref[at, :] = result
        low_ref[at, :] = result.astype(LOW)

    tiles(first, last, rows)


def norm_undo(norm_ref, rstd_ref, gain, source_ref, grad_ref, low_ref, first=0, last=6, carry=None):
    width = norm_ref.shape[1]

    def rows(j, carry):
        d_gain, d_shift, d_low = carry
        at = span_of(j, 64)
        dy = source_ref[at, :].astype(jnp.float32)
        normal = norm_ref[at, :]
        scaled = dy * gain
        mean = jnp.mean(scaled, axis=-1, keepdims=True)
        along = jnp.mean(scaled * normal, axis=-1, keepdims=True)
        d_resid = rstd_ref[0][at, rstd_ref[1]] * (scaled - mean - normal * along)
        grad_ref[at, :] = d_resid
        low = d_resid.astype(LOW)
        low_ref[at, :] = low
        return (
            d_gain + jnp.sum(dy * normal, axis=0, keepdims=True),
            d_shift + jnp.sum(dy, axis=0, keepdims=True),
            d_low + jnp.sum(low.astype(jnp.float32), axis=0, keepdims=True),
        )

    zero = jnp.zeros((1, width), jnp.float32)
    return lax.fori_loop(first, last, rows, (zero, zero, zero) if carry is None else carry)


def column_total(ref):
    return jnp.sum(ref[...].astype(jnp.float32), axis=0, keepdims=True)


def layer_kernel(
    tokens, segments, gains, biases, ffn_bias, cotangent, s_qk, s_vo, s_cqk, s_cvo, s_in, s_out,
    out_layer, out_input, out_qk, out_vo, out_cqk, out_cvo, out_in, out_out, out_small,
    w_qk, w_vo, w_in, w_out, w_x,
    side_c, side_r, land_c, land_r, near_c, near_r, small, small_land,
    sec_bias, sec_gain, sec_fbias, b1_rows,
    q, k, v, o, h_low, norm_a, h, act, slope, norm_f, d_ffn, score_bias, x_send, x_recv,
    qc, kc, vc, p_c, oc, h2_low, norm_c, d_branch, d_mixed, grad, lse, rstd,
    load_sem, peer_send, peer_recv, rs, rr, ss, sr, rs2, rr2, ss2, sr2, fold_send, fold_recv, out_sem,
):
    place = Place()
    chip, core = place.chip, place.core
    width = tokens.shape[-1]
    encoder, decoder = place.section == 0, place.section == 1
    x = tokens.at[0, 0]
    rstd_a, rstd_f, rstd_c = ((rstd, slice(i, i + 1)) for i in range(3))
    loads = [
        pltpu.make_async_copy(src.at[0], dst.at[chip, core], load_sem.at[i])
        for i, (src, dst) in enumerate([(s_qk, w_qk), (s_vo, w_vo), (s_in, w_in), (s_out, w_out)])
    ]
    for copy in loads:
        copy.start()
    enter(place)
    own_cross = [
        pltpu.make_async_copy(src.at[0], w_x.at[chip, core, 48 * i : 48 * i + 48, :], load_sem.at[4 + i])
        for i, src in enumerate([s_cqk, s_cvo])
    ]
    from_encoder = [
        pltpu.make_async_remote_copy(
            src.at[0], w_x.at[chip, core, 96 + 48 * i : 144 + 48 * i, :], peer_send.at[i], peer_recv.at[i],
            device_id=place.peer(), device_id_type=MESH,
        )
        for i, src in enumerate([s_cqk, s_cvo])
    ]
    pieces = piece_list(w_qk, w_vo, w_in, w_out, w_x)
    gather = Gather(place, pieces, rs, rr, ss, sr)
    for copy in loads:
        copy.wait()
    gather.start(0)
    gather.start(1)
    cot_load = pltpu.make_async_copy(cotangent, d_mixed, load_sem.at[6])

    @pl.when(encoder)
    def _():
        for copy in from_encoder:
            copy.start()
        sec_bias[0:6] = biases[0:6]
        sec_gain[0:1] = gains[0:1]
        sec_fbias[...] = ffn_bias[0:1]
        mask_scores(score_bias, segments[0], segments[0], False)

    @pl.when(decoder)
    def _():
        for copy in own_cross:
            copy.start()
        cot_load.start()
        sec_bias[0:6] = biases[6:12]
        sec_gain[0:1] = gains[2:3]
        sec_fbias[...] = ffn_bias[1:2]
        mask_scores(score_bias, segments[1], segments[1], True)

    small[...] = jnp.zeros_like(small)
    serve(plan(gather, None, "0.0", "1.0", "0.1", "1.1"))

    def next_pieces(first, second):
        serve(plan(gather, None, "0.2", f"+{first}", "1.2", f"+{second}", "0.3", "1.3"))

    @pl.when(encoder)
    def _():
        next_pieces(2, 3)

    @pl.when(decoder)
    def _():
        for copy in own_cross:
            copy.wait()
        for copy in from_encoder:
            copy.wait_recv()
        next_pieces(6, 7)

    gather.side_arrivals(0)
    gather.side_arrivals(1)

    def early(count):
        @pl.when(encoder)
        def _():
            serve(first_steps, count)

        @pl.when(decoder)
        def _():
            serve(other_steps, count)

    first_steps = plan(gather, None, "2.0", "+4", "3.0", "+5", "2.1", "3.1", "4.0", "5.0")
    other_steps = plan(gather, None, "6.0", "+2", "7.0", "+3", "6.1", "7.1", "2.0", "3.0")

    def project(j):
        at = span_of(j, 256)
        past = pl.ds(pl.multiple_of(width + j * 256, 256), 256)
        q[:, at] = (nn(x[...], columns_of(w_qk, at)) + sec_bias[0:1, at]).astype(LOW)
        k[:, at] = nn(x[...], columns_of(w_qk, past)).astype(LOW)
        v[:, at] = (nn(x[...], columns_of(w_vo, at)) + sec_bias[1:2, at]).astype(LOW)

    tiles(0, 3, project)
    early(2)
    attend_pairs(q, k, v, score_bias, o, lse, None, 0, 2)
    early(2)
    attend_pairs(q, k, v, score_bias, o, lse, None, 2, 4)
    early(2)
    attend_pairs(q, k, v, score_bias, o, lse, None, 4, 6)
    early(1)

    def self_out(j):
        at = span_of(j, 256)
        past = pl.ds(pl.multiple_of(width + j * 256, 256), 256)
        norm_a[:, at] = x[:, at].astype(jnp.float32) + nn(o[...], columns_of(w_vo, past)) + sec_bias[2:3, at]

    tiles(0, 3, self_out)
    norm_pass(norm_a, rstd_a, sec_gain[0:1], sec_bias[3:4], h, h_low)
    early(None)

    def ffn_up(low_ref, low, high):
        def tile(j):
            at = span_of(j, 256)
            u = nn(low_ref[...], columns_of(w_in, at)) + sec_fbias[:, at]
            value, rise = gelu_parts(u)
            act[:, at] = value.astype(LOW)
            slope[:, at] = rise.astype(LOW)

        tiles(low, high, tile)

    def ffn_down(rows=slice(None)):
        def tile(j):
            at = span_of(j, 256)
            norm_f[rows, at] = h[rows, at] + nn(act[rows, :], columns_of(w_out, at)) + sec_bias[4:5, at]

        tiles(0, 3, tile)

    def ffn_slope():
        def tile(j):
            at = span_of(j, width)
            block = w_out[pl.ds(2 * j, 2)].reshape(width, width)
            d_pre = (nt(d_ffn[...], block) * slope[:, at].astype(jnp.float32)).astype(LOW)
            slope[:, at] = d_pre
            b1_rows[j] = jnp.sum(d_pre.astype(jnp.float32), axis=0, keepdims=True)

        tiles(0, 4, tile)

    def ffn_hidden():
        def tile(j):
            at = span_of(j, width)
            grad[...] += nt(slope[:, at], columns_of(w_in, at))

        tiles(0, 4, tile)

    def grad_w_out(ref):
        def tile(c):
            block = tn(act[:, span_of(c, 384)], d_ffn[...])
            ref[c] = block.astype(LOW).reshape(2, 192, width)

        tiles(0, CHIPS, tile)

    def store(ref, at, value, rows=slice(None)):
        ref[:, :, rows, at] = value.astype(LOW).reshape(CHIPS, 2, 48, value.shape[1])

    def cross_weight(i, at=slice(None)):
        return columns_of(w_x, at, slice(48 * i, 48 * i + 48))

    def store_cross(i, value):
        store(w_x, slice(None), value, slice(48 * i, 48 * i + 48))

    def grad_w_in(low_ref):
        def tile(j):
            at = span_of(j, width)
            store(w_in, at, tn(low_ref[...], slope[:, at]))

        tiles(0, 4, tile)

    def set_small(row, value):
        small[row : row + 1, :] = value

    def set_b1(section):
        for j in range(4):
            set_small(24 + 4 * section + j, b1_rows[j])

    def self_back_a(section):
        gain, shift, branch = norm_undo(norm_a, rstd_a, sec_gain[0:1], grad, grad, d_branch)
        set_small(2 * section, gain)
        set_small(8 + 6 * section + 3, shift)
        set_small(8 + 6 * section + 2, branch)
        d_mixed[...] = nt(d_branch[...], columns_of(w_vo, slice(width, 2 * width))).astype(LOW)

    def self_back_b(section):
        set_small(8 + 6 * section, column_total(q))
        set_small(8 + 6 * section + 1, column_total(v))
        grad[...] += nt(q[...], columns_of(w_qk, slice(0, width)))
        grad[...] += nt(k[...], columns_of(w_qk, slice(width, 2 * width)))
        grad[...] += nt(v[...], columns_of(w_vo, slice(0, width)))
        pltpu.make_async_copy(grad, out_input.at[0, 0], out_sem.at[1]).start()

    def self_back_qk():
        store(w_qk, slice(0, width), tn(x[...], q[...]))
        store(w_qk, slice(width, 2 * width), tn(x[...], k[...]))

    def self_back_vo():
        store(w_vo, slice(0, width), tn(x[...], v[...]))
        store(w_vo, slice(width, 2 * width), tn(o[...], d_branch[...]))

    def result_at(p):
        holder = norm_f if p < 4 else norm_c
        return holder.at[96 * (p % 4) : 96 * (p % 4) + 96, :]

    def out_copies(p, half):
        source = result_at(p)
        low = width * half
        target = (
            out_qk.at[0, :, low : low + width],
            out_vo.at[0, :, low : low + width],
            out_in.at[0, :, low : low + width],
            out_in.at[0, :, 2 * width + low : 3 * width + low],
            out_out.at[0, 48 * half : 48 * half + 48, :],
            out_out.at[0, 96 + 48 * half : 144 + 48 * half, :],
            (out_cqk, out_cvo)[half].at[0],
            (out_cqk, out_cvo)[half].at[0],
        )[p]
        return pltpu.make_async_copy(
            source.at[48 * half : 48 * half + 48], target, out_sem.at[2 + 2 * min(p, 6) + half]
        )

    def finish_piece(scatter, word):
        p = int(word[1:])
        if word[0] == "f":
            fold_end(p)
            return
        total = scatter.last(p)
        target = result_at(p)
        if p >= 4:
            target[...] = total
        else:
            target[0:48] = total[:, :width]
            target[48:96] = total[:, width:]
        if p == 7:
            to_encoder.start()
        else:
            out_copies(p, 0).start()
            out_copies(p, 1).start()

    to_encoder = pltpu.make_async_remote_copy(
        result_at(7), result_at(7), peer_send.at[2], peer_recv.at[2], device_id=place.peer(), device_id_type=MESH
    )
    cross_copies = [
        pltpu.make_async_remote_copy(
            x_send.at[128 * c : 128 * c + 128], x_recv.at[128 * c : 128 * c + 128], peer_send.at[3 + c], peer_recv.at[3 + c],
            device_id=place.peer(), device_id_type=MESH,
        )
        for c in range(3)
    ]
    layer_copy = pltpu.make_async_copy(x_send, out_layer.at[0, 0], out_sem.at[0])

    def fold(i):
        return pltpu.make_async_remote_copy(
            small, small_land.at[i], fold_send.at[i], fold_recv.at[i], device_id=place.folds()[i], device_id_type=MESH
        )

    def fold_start(i):
        fold(i).start()

    def fold_end(i):
        fold(i).wait()
        small[...] = small[...] + small_land[i]
        if i < 4:
            fold(i + 1).start()

    @pl.when(encoder)
    def _():
        serve(plan(gather, None, "2.2", "3.2", "4.1", "5.1", "2.3", "3.3"))
        gather.side_arrivals(2)
        gather.side_arrivals(3)
        queue = plan(gather, None, "4.2", "5.2", "4.3", "5.3")
        for part in range(4):
            ffn_up(h_low, 3 * part, 3 * part + 3)
            serve(queue, 1)
        gather.side_arrivals(4)
        gather.side_arrivals(5)
        for c in range(3):
            ffn_down(slice(128 * c, 128 * c + 128))
            norm_pass(norm_f, rstd_f, gains[1:2], biases[5:6], None, x_send, 2 * c, 2 * c + 2)
            cross_copies[c].start()
        layer_copy.start()
        for copy in from_encoder:
            copy.wait_send()
        for p in range(6):
            gather.finish(p)
        layer_copy.wait()
        found = None
        for c in range(3):
            cross_copies[c].wait()
            found = norm_undo(norm_f, rstd_f, gains[1:2], x_recv, grad, d_ffn, 2 * c, 2 * c + 2, found)
        gain, shift, branch = found
        set_small(1, gain)
        set_small(8 + 5, shift)
        set_small(8 + 4, branch)
        scatter = Scatter(
            place, piece_list(w_qk, w_vo, w_in, w_x, None),
            side_c, side_r, land_c, land_r, near_c, near_r, rs2, rr2, ss2, sr2,
        )
        after = functools.partial(finish_piece, scatter)
        grad_w_out(w_x)
        scatter.hand_over(4)
        scatter.hand_over(5)
        ffn_slope()
        scatter.start(4)
        scatter.start(5)
        ffn_hidden()
        queue = plan(scatter, after, "4.0", "5.0", "+2", "+3", "4.1", "5.1", "2.0", "3.0", "4.2", "5.2", "2.1", "3.1", "=4", "=5")
        serve(queue, 1)
        grad_w_in(h_low)
        scatter.hand_over(2)
        scatter.hand_over(3)
        serve(queue, 1)
        set_b1(0)
        self_back_a(0)
        serve(queue, 3)
        for part in range(3):
            attend_back_pairs(q, k, v, score_bias, lse, None, d_mixed, 2 * part, 2 * part + 2)
            serve(queue, 1)
        self_back_b(0)
        fold_start(0)
        serve(queue, 2)
        self_back_qk()
        scatter.hand_over(0)
        serve(queue, 1)
        self_back_vo()
        scatter.hand_over(1)
        serve(queue, 1)
        scatter.start(0)
        serve(queue, 1)
        scatter.start(1)
        fold_end(0)
        serve(queue)
        serve(
            plan(
                scatter, after, "2.2", "3.2", "0.0", "f1", "1.0", "0.1", "1.1", "f2", "=2", "=3", "0.2", "1.2", "f3",
                "=0", "=1",
            )
        )
        to_encoder.wait_recv()
        out_copies(7, 0).start()
        out_copies(7, 1).start()
        for p in range(6):
            scatter.finish(p)

    @pl.when(decoder)
    def _():
        queue = plan(gather, None, "6.2", "+4", "7.2", "+5", "2.1", "3.1", "6.3", "7.3", "2.2", "3.2", "4.0", "5.0", "4.1", "5.1", "2.3", "3.3", "4.2", "5.2", "4.3", "5.3")
        serve(queue, 8)
        gather.side_arrivals(6)
        gather.side_arrivals(7)
        mask_scores(score_bias, segments[0], segments[1], False)

        def cross_query(j):
            at = span_of(j, 256)
            qc[:, at] = (nn(h_low[...], cross_weight(0, at)) + biases[12:13, at]).astype(LOW)

        tiles(0, 3, cross_query)
        serve(queue, 8)
        for c in range(3):
            rows = slice(128 * c, 128 * c + 128)
            cross_copies[c].wait_recv()

            def cross_keys(j):
                at = span_of(j, 256)
                kc[rows, at] = nn(x_recv[rows, :], cross_weight(2, at)).astype(LOW)
                vc[rows, at] = (nn(x_recv[rows, :], cross_weight(3, at)) + biases[13:14, at]).astype(LOW)

            tiles(0, 3, cross_keys)
        attend_pairs(qc, kc, vc, score_bias, oc, None, p_c, 0, 3)
        serve(queue, 2)
        attend_pairs(qc, kc, vc, score_bias, oc, None, p_c, 3, 6)
        serve(queue)
        gather.side_arrivals(2)
        gather.side_arrivals(3)

        def cross_out(j):
            at = span_of(j, 256)
            norm_c[:, at] = h[:, at] + nn(oc[...], cross_weight(1, at)) + biases[14:15, at]

        tiles(0, 3, cross_out)
        norm_pass(norm_c, rstd_c, gains[4:5], biases[15:16], h, h2_low)
        ffn_up(h2_low, 0, 12)
        gather.side_arrivals(4)
        gather.side_arrivals(5)
        ffn_down()
        norm_pass(norm_f, rstd_f, gains[3:4], biases[11:12], None, x_send)
        layer_copy.start()
        cot_load.wait()
        gain, shift, branch = norm_undo(norm_f, rstd_f, gains[3:4], d_mixed, grad, d_ffn)
        set_small(3, gain)
        set_small(8 + 11, shift)
        set_small(8 + 10, branch)
        for p in (4, 5):
            gather.finish(p)
        scatter = Scatter(
            place, pieces, side_c, side_r, land_c, land_r, near_c, near_r, rs2, rr2, ss2, sr2,
        )
        after = functools.partial(finish_piece, scatter)
        ffn_slope()
        grad_w_out(w_out)
        scatter.hand_over(4)
        scatter.hand_over(5)
        ffn_hidden()
        gain, shift, branch = norm_undo(norm_c, rstd_c, gains[4:5], grad, grad, d_branch)
        set_small(4, gain)
        set_small(8 + 15, shift)
        set_small(8 + 14, branch)
        scatter.start(4)
        scatter.start(5)
        d_mixed[...] = nt(d_branch[...], cross_weight(1)).astype(LOW)
        layer_copy.wait()
        queue = plan(scatter, after, "4.0", "5.0", "4.1", "5.1", "+2", "+3", "4.2", "5.2", "2.0", "3.0", "=4", "=5", "+7", "2.1", "3.1", "+6", "7.0", "2.2", "3.2")
        for c in range(3):
            rows = slice(128 * c, 128 * c + 128)
            attend_back_keys(qc, kc, vc, oc, p_c, d_mixed, norm_f, 128 * c, 128, c == 0)
            x_send[rows, :] = (nt(kc[rows, :], cross_weight(2)) + nt(vc[rows, :], cross_weight(3))).astype(LOW)
            cross_copies[c].start()
            serve(queue, 2 if c == 1 else 0)
        for p in (0, 1, 2, 3, 6, 7):
            gather.finish(p)
        qc[...] = norm_f[...].astype(LOW)
        grad_w_in(h2_low)
        scatter.hand_over(2)
        scatter.hand_over(3)
        serve(queue, 2)
        store_cross(2, tn(x_recv[...], kc[...]))
        store_cross(3, tn(x_recv[...], vc[...]))
        scatter.hand_over(7)
        serve(queue, 4)
        grad[...] += nt(qc[...], cross_weight(0))
        store_cross(0, tn(h_low[...], qc[...]))
        store_cross(1, tn(oc[...], d_branch[...]))
        scatter.hand_over(6)
        set_b1(1)
        set_small(8 + 12, column_total(qc))
        set_small(8 + 13, column_total(vc))
        serve(queue, 1)
        mask_scores(score_bias, segments[1], segments[1], True)
        self_back_a(1)
        serve(queue, 3)
        for part in range(3):
            attend_back_pairs(q, k, v, score_bias, lse, None, d_mixed, 2 * part, 2 * part + 2)
            serve(queue, 1)
        self_back_b(1)
        fold_start(0)
        serve(queue, 2)
        self_back_qk()
        scatter.hand_over(0)
        serve(queue, 1)
        self_back_vo()
        scatter.hand_over(1)
        serve(queue)
        scatter.start(0)
        fold_end(0)
        serve(
            plan(
                scatter, after, "6.0", "+1", "7.1", "6.1", "=2", "=3", "f1", "0.0", "1.0", "7.2", "6.2", "f2", "0.1",
                "1.1", "=7", "=6", "0.2", "1.2", "f3", "=0", "=1",
            )
        )
        for copy in cross_copies:
            copy.wait_send()
        to_encoder.wait_send()
        for p in range(8):
            scatter.finish(p)

    fold_end(4)
    out_small[...] = small[...]
    for p in range(7):
        for half in range(2):
            out_copies(p, half).wait()
    pltpu.make_async_copy(grad, out_input.at[0, 0], out_sem.at[1]).wait()


def layer_call(tokens, segments, cotangent, attn_qk, attn_vo, cross_qk, cross_vo, ffn_in, ffn_out, gains, biases, ffn_bias):
    length, width = tokens.shape[2:]
    hidden = ffn_in.shape[2]

    def result(like, kind):
        return jax.ShapeDtypeStruct(like.shape, kind)

    def low(*shape):
        return pltpu.VMEM(shape, LOW)

    def full(*shape):
        return pltpu.VMEM(shape, jnp.float32)

    any_space = pl.BlockSpec(memory_space=pl.ANY)
    in_vmem = pl.BlockSpec(memory_space=pltpu.VMEM)
    flat, wide, exact = low(length, width), low(length, hidden), full(length, width)
    dma = pltpu.SemaphoreType.DMA
    scratch = [
        low(CHIPS, 2, 48, 2 * width), low(CHIPS, 2, 48, 2 * width), low(CHIPS, 2, 48, hidden),
        low(CHIPS, 2, 192, width), low(CHIPS, 2, 192, width),
        low(4, CHIPS, 48, 2 * width), low(4, CHIPS, 96, width),
        low(4, 2, 3, 48, 2 * width), low(4, 2, 3, 96, width),
        low(4, 2, 48, width), low(4, 2, 48, width),
        full(32, width), full(5, 32, width),
        full(8, width), full(1, width), full(1, hidden), full(4, 1, width),
        flat, flat, flat, flat, flat, exact, exact, wide, wide, exact, flat, full(length, length), flat, flat,
        flat, flat, flat, low(HEADS, length, length), flat, flat, exact, flat, flat, exact,
        full(HEADS, 1, length), full(length, 128),
        dma((7,)), dma((6,)), dma((6,)),
        dma((8, 2, 4)), dma((8, 2, 4)), dma((8, 9)), dma((8, 9)),
        dma((8, 2, 4)), dma((8, 2, 4)), dma((8,)), dma((8,)),
        dma((5,)), dma((5,)), dma((16,)),
    ]
    return pl.pallas_call(
        layer_kernel,
        out_shape=(
            result(tokens, LOW), result(tokens, jnp.float32),
            result(attn_qk, jnp.float32), result(attn_vo, jnp.float32),
            result(cross_qk, jnp.float32), result(cross_vo, jnp.float32),
            result(ffn_in, jnp.float32), result(ffn_out, jnp.float32),
            jax.ShapeDtypeStruct((32, width), jnp.float32),
        ),
        in_specs=[in_vmem] * 5 + [any_space] * 7,
        out_specs=(any_space,) * 8 + (in_vmem,),
        scratch_shapes=scratch,
        compiler_params=pltpu.CompilerParams(
            collective_id=0, has_side_effects=True, vmem_limit_bytes=63 * 1024 * 1024
        ),
        name="layer_pair",
    )(
        tokens, segments, gains, biases, ffn_bias, cotangent[0],
        attn_qk, attn_vo, cross_qk, cross_vo, ffn_in, ffn_out,
    )


def hand_out_kernel(*refs):
    sources, small, rest = refs[:8], refs[8], refs[9:]
    targets, (gains, biases, ffn_bias), held, (take, give) = rest[:8], rest[8:11], rest[11:19], rest[19:]
    inward = [pltpu.make_async_copy(a, b, take.at[i]) for i, (a, b) in enumerate(zip(sources, held))]
    outward = [pltpu.make_async_copy(a, b, give.at[i]) for i, (a, b) in enumerate(zip(held, targets))]
    for copy in inward:
        copy.start()
    gains[...] = small[0:5]
    biases[...] = small[8:24]
    width = gains.shape[1]
    for row in range(8):
        ffn_bias[row // 4 : row // 4 + 1, width * (row % 4) : width * (row % 4 + 1)] = small[24 + row : 25 + row]
    for first, second in zip(inward, outward):
        first.wait()
        second.start()
    for copy in outward:
        copy.wait()


def hand_out(results, gains, biases, ffn_bias):
    any_space = pl.BlockSpec(memory_space=pl.ANY)
    in_vmem = pl.BlockSpec(memory_space=pltpu.VMEM)
    return pl.pallas_call(
        hand_out_kernel,
        out_shape=tuple(jax.ShapeDtypeStruct(r.shape, r.dtype) for r in tuple(results[:8]) + (gains, biases, ffn_bias)),
        in_specs=[any_space] * 8 + [in_vmem],
        out_specs=(any_space,) * 8 + (in_vmem,) * 3,
        scratch_shapes=[pltpu.VMEM(r.shape, r.dtype) for r in results[:8]] + [pltpu.SemaphoreType.DMA((8,))] * 2,
        compiler_params=pltpu.CompilerParams(vmem_limit_bytes=63 * 1024 * 1024),
        name="hand_out",
    )(*results)


def local_ring(
    tokens, segments, cotangent, attn_qk, attn_vo, cross_qk, cross_vo, ffn_in, ffn_out, gains, biases, ffn_bias
):
    results = layer_call(
        tokens, segments, cotangent, attn_qk, attn_vo, cross_qk, cross_vo, ffn_in, ffn_out, gains, biases, ffn_bias
    )
    return hand_out(results, gains, biases, ffn_bias)


def solution(mesh):
    any_size = mesh.shape["section"] != 2 or mesh.shape["dp"] != 2 * CHIPS
    placed = (
        P("section", "dp", None, None),
        P(None, "dp", None),
        P("dp", None, None),
        P("section", "dp", None),
        P("section", "dp", None),
        P("section", "dp", None),
        P("section", "dp", None),
        P("section", "dp", None),
        P("section", "dp", None),
        P(),
        P(),
        P(),
    )
    return jax.shard_map(
        local_any if any_size else local_ring,
        mesh=mesh,
        in_specs=placed,
        out_specs=(
            P("section", "dp", None, None),
            P("section", "dp", None, None),
            P("section", "dp", None),
            P("section", "dp", None),
            P("section", "dp", None),
            P("section", "dp", None),
            P("section", "dp", None),
            P("section", "dp", None),
            P(),
            P(),
            P(),
        ),
        check_vma=False,
    )
```

```python
import functools

import jax
import jax.numpy as jnp
from jax import lax
from jax.experimental import pallas as pl
from jax.experimental.pallas import tpu as pltpu
from jax.sharding import PartitionSpec as P

HEADS = 12


NORM_EPSILON = 1e-05


def from_behind(x, axis, by):
    devices = lax.axis_size(axis)
    pairs = [(i, i + by) for i in range(devices) if 0 <= i + by < devices]
    return lax.ppermute(x, axis, pairs)


def product(left, right):
    return jnp.einsum("rld,de->rle", left, right, preferred_element_type=jnp.float32)


def back_product(grad, right):
    return jnp.einsum("rle,de->rld", grad, right, preferred_element_type=jnp.float32)


def weight_grad(left, grad):
    return jnp.einsum("rld,rle->de", left, grad, preferred_element_type=jnp.float32)


def column_sum(values):
    return jnp.sum(values.astype(jnp.float32), axis=(0, 1))


def norm_rows(resid, gain, shift):
    center = resid - jnp.mean(resid, axis=-1, keepdims=True)
    spread = jnp.mean(center * center, axis=-1, keepdims=True)
    return center * lax.rsqrt(spread + NORM_EPSILON) * gain + shift


def norm_back(resid, gain, shift, grad):
    unused, pull = jax.vjp(norm_rows, resid, gain, shift)
    return pull(grad)


def split_heads(values, head_count):
    return values.reshape(
        values.shape[0], values.shape[1], head_count, values.shape[2] // head_count
    )


def masked_scores(query_heads, key_heads, allowed):
    scale = query_heads.shape[-1] ** (-0.5)
    scores = (
        jnp.einsum("rqhe,rkhe->rhqk", query_heads, key_heads, preferred_element_type=jnp.float32)
        * scale
    )
    return jnp.where(allowed[:, None], scores, -1e30)


def attend(query, key_rows, value_rows, allowed, head_count):
    query_heads = split_heads(query, head_count)
    scores = masked_scores(query_heads, split_heads(key_rows, head_count), allowed)
    peak = jnp.max(scores, axis=-1, keepdims=True)
    exponent = jnp.exp(scores - peak)
    summed = jnp.sum(exponent, axis=-1, keepdims=True)
    soft = (exponent / summed).astype(jnp.bfloat16)
    mixed = jnp.einsum(
        "rhqk,rkhe->rqhe",
        soft,
        split_heads(value_rows, head_count),
        preferred_element_type=jnp.float32,
    )
    return (mixed.reshape(query.shape), peak + jnp.log(summed))


def attend_back(query, key_rows, value_rows, allowed, log_total, grad_mixed, head_count):
    query_heads = split_heads(query, head_count)
    key_heads = split_heads(key_rows, head_count)
    value_heads = split_heads(value_rows, head_count)
    grad_heads = split_heads(grad_mixed, head_count)
    scale = query_heads.shape[-1] ** (-0.5)
    soft = jnp.exp(masked_scores(query_heads, key_heads, allowed) - log_total)
    grad_values = jnp.einsum(
        "rhqk,rqhe->rkhe", soft.astype(jnp.bfloat16), grad_heads, preferred_element_type=jnp.float32
    )
    grad_soft = jnp.einsum(
        "rqhe,rkhe->rhqk", grad_heads, value_heads, preferred_element_type=jnp.float32
    )
    inner_sum = jnp.sum(soft * grad_soft, axis=-1, keepdims=True)
    grad_scores = (soft * (grad_soft - inner_sum)).astype(jnp.bfloat16)
    grad_query = (
        jnp.einsum("rhqk,rkhe->rqhe", grad_scores, key_heads, preferred_element_type=jnp.float32)
        * scale
    )
    grad_keys = (
        jnp.einsum("rhqk,rqhe->rkhe", grad_scores, query_heads, preferred_element_type=jnp.float32)
        * scale
    )
    return (
        grad_query.reshape(query.shape),
        grad_keys.reshape(key_rows.shape),
        grad_values.reshape(key_rows.shape),
    )


def self_forward(inputs, w_qk, w_vo, section_bias, gain, allowed, head_count):
    model_width = inputs.shape[-1]
    query = (product(inputs, w_qk[:, :model_width]) + section_bias[0]).astype(jnp.bfloat16)
    key_rows = product(inputs, w_qk[:, model_width:]).astype(jnp.bfloat16)
    value_rows = (product(inputs, w_vo[:, :model_width]) + section_bias[1]).astype(jnp.bfloat16)
    mixed, log_total = attend(query, key_rows, value_rows, allowed, head_count)
    mixed = mixed.astype(jnp.bfloat16)
    resid = inputs.astype(jnp.float32) + product(mixed, w_vo[:, model_width:]) + section_bias[2]
    return (
        norm_rows(resid, gain, section_bias[3]),
        (query, key_rows, value_rows, log_total, mixed, resid),
    )


def self_backward(inputs, w_qk, w_vo, section_bias, gain, allowed, head_count, kept, grad_hidden):
    query, key_rows, value_rows, log_total, mixed, resid = kept
    model_width = inputs.shape[-1]
    grad_resid, grad_gain, grad_shift = norm_back(resid, gain, section_bias[3], grad_hidden)
    grad_branch = grad_resid.astype(jnp.bfloat16)
    grad_mixed = back_product(grad_branch, w_vo[:, model_width:]).astype(jnp.bfloat16)
    grad_query, grad_keys, grad_values = attend_back(
        query, key_rows, value_rows, allowed, log_total, grad_mixed, head_count
    )
    grad_query = grad_query.astype(jnp.bfloat16)
    grad_keys = grad_keys.astype(jnp.bfloat16)
    grad_values = grad_values.astype(jnp.bfloat16)
    grad_pair = jnp.concatenate([grad_query, grad_keys], axis=-1)
    grad_inputs = (
        grad_resid
        + back_product(grad_pair, w_qk)
        + back_product(grad_values, w_vo[:, :model_width])
    )
    grad_rows = jnp.stack(
        [column_sum(grad_query), column_sum(grad_values), column_sum(grad_branch), grad_shift]
    )
    return (grad_inputs, (inputs, grad_pair, grad_values, mixed, grad_branch), grad_rows, grad_gain)


def ffn_forward(hidden, w_in, w_out, b_in, b_out):
    hidden_low = hidden.astype(jnp.bfloat16)
    pre_act = product(hidden_low, w_in) + b_in
    activated = jax.nn.gelu(pre_act, approximate=False).astype(jnp.bfloat16)
    return (product(activated, w_out) + b_out, (hidden_low, pre_act, activated))


def gelu_exact(values):
    return jax.nn.gelu(values, approximate=False)


def ffn_backward(w_in, w_out, kept, grad_branch):
    hidden_low, pre_act, activated = kept
    grad_low = grad_branch.astype(jnp.bfloat16)
    grad_act = back_product(grad_low, w_out)
    unused, pull = jax.vjp(gelu_exact, pre_act)
    grad_pre = pull(grad_act)[0].astype(jnp.bfloat16)
    grad_hidden = back_product(grad_pre, w_in)
    return (
        grad_hidden,
        (hidden_low, grad_pre, activated, grad_low),
        column_sum(grad_pre),
        column_sum(grad_low),
    )


def encoder_forward(hidden, w_in, w_out, b_in, section_bias, gain_last, w_ck, w_cv, bias_cv):
    branch, kept = ffn_forward(hidden, w_in, w_out, b_in, section_bias[4])
    resid = hidden + branch
    memory = norm_rows(resid, gain_last, section_bias[5]).astype(jnp.bfloat16)
    key_rows = product(memory, w_ck).astype(jnp.bfloat16)
    value_rows = (product(memory, w_cv) + bias_cv).astype(jnp.bfloat16)
    return (memory, key_rows, value_rows, resid, kept)


def encoder_backward(
    w_in, w_out, section_bias, gain_last, w_ck, w_cv, memory, resid, kept, grad_keys, grad_values
):
    grad_memory = back_product(grad_keys, w_ck) + back_product(grad_values, w_cv)
    grad_last, grad_gain, grad_shift = norm_back(resid, gain_last, section_bias[5], grad_memory)
    grad_ffn, ffn_ops, grad_bin, grad_bout = ffn_backward(w_in, w_out, kept, grad_last)
    zero_line = jnp.zeros_like(grad_gain)
    cross_rows = jnp.stack([zero_line, column_sum(grad_values), zero_line, zero_line])
    operands = (memory, grad_keys, memory, grad_values) + ffn_ops
    return (
        grad_last + grad_ffn,
        operands,
        grad_bin,
        grad_bout,
        grad_gain,
        grad_shift,
        cross_rows,
        zero_line,
    )


def decoder_step(
    hidden,
    w_cq,
    w_co,
    w_in,
    w_out,
    b_in,
    section_bias,
    gain_last,
    gain_cross,
    cross_bias,
    key_rows,
    value_rows,
    allowed,
    cotangent,
    head_count,
):
    hidden_low = hidden.astype(jnp.bfloat16)
    query = (product(hidden_low, w_cq) + cross_bias[0]).astype(jnp.bfloat16)
    mixed, log_total = attend(query, key_rows, value_rows, allowed, head_count)
    mixed = mixed.astype(jnp.bfloat16)
    resid_mid = hidden + product(mixed, w_co) + cross_bias[2]
    middle = norm_rows(resid_mid, gain_cross, cross_bias[3])
    branch, kept = ffn_forward(middle, w_in, w_out, b_in, section_bias[4])
    resid_last = middle + branch
    result = norm_rows(resid_last, gain_last, section_bias[5])
    grad_last, grad_gain, grad_shift = norm_back(
        resid_last, gain_last, section_bias[5], cotangent.astype(jnp.float32)
    )
    grad_ffn, ffn_ops, grad_bin, grad_bout = ffn_backward(w_in, w_out, kept, grad_last)
    grad_mid, grad_gain_cross, grad_shift_cross = norm_back(
        resid_mid, gain_cross, cross_bias[3], grad_last + grad_ffn
    )
    grad_branch = grad_mid.astype(jnp.bfloat16)
    grad_mixed = back_product(grad_branch, w_co).astype(jnp.bfloat16)
    grad_query, grad_keys, grad_values = attend_back(
        query, key_rows, value_rows, allowed, log_total, grad_mixed, head_count
    )
    grad_query = grad_query.astype(jnp.bfloat16)
    grad_hidden = grad_mid + back_product(grad_query, w_cq)
    cross_rows = jnp.stack(
        [
            column_sum(grad_query),
            jnp.zeros_like(grad_gain),
            column_sum(grad_branch),
            grad_shift_cross,
        ]
    )
    operands = (hidden_low, grad_query, mixed, grad_branch) + ffn_ops
    tail_result = (
        grad_hidden,
        operands,
        grad_bin,
        grad_bout,
        grad_gain,
        grad_shift,
        cross_rows,
        grad_gain_cross,
    )
    return (
        result.astype(jnp.bfloat16),
        grad_keys.astype(jnp.bfloat16),
        grad_values.astype(jnp.bfloat16),
        tail_result,
    )


def zero_tail(hidden, w_in):
    model_width = hidden.shape[-1]
    ffn_width = w_in.shape[1]
    flat = jnp.zeros(hidden.shape, jnp.bfloat16)
    wide = jnp.zeros((hidden.shape[0], hidden.shape[1], ffn_width), jnp.bfloat16)
    zero_line = jnp.zeros((model_width,), jnp.float32)
    operands = (flat, flat, flat, flat, flat, wide, wide, flat)
    return (
        jnp.zeros_like(hidden),
        operands,
        jnp.zeros((ffn_width,), jnp.float32),
        zero_line,
        zero_line,
        zero_line,
        jnp.zeros((4, model_width), jnp.float32),
        zero_line,
    )


def tail_whole(operands):
    return (
        weight_grad(operands[0], operands[1]),
        weight_grad(operands[2], operands[3]),
        weight_grad(operands[4], operands[5]),
        weight_grad(operands[6], operands[7]),
    )


def self_whole(operands):
    grad_qk = weight_grad(operands[0], operands[1])
    grad_vo = jnp.concatenate(
        [weight_grad(operands[0], operands[2]), weight_grad(operands[3], operands[4])], axis=1
    )
    return (grad_qk, grad_vo)


def local_any(
    tokens,
    segments,
    cotangent,
    attn_qk,
    attn_vo,
    cross_qk,
    cross_vo,
    ffn_in,
    ffn_out,
    gains,
    biases,
    ffn_bias,
):
    head_count = HEADS
    section_index = lax.axis_index("section")
    is_enc = section_index == 0
    qk_whole, vo_whole = (
        lax.all_gather(attn_qk, "dp", axis=1, tiled=True),
        lax.all_gather(attn_vo, "dp", axis=1, tiled=True),
    )
    w_qk = qk_whole[0]
    w_vo = vo_whole[0]
    cqk_whole, cvo_whole, in_whole, out_whole = (
        lax.all_gather(cross_qk, "dp", axis=1, tiled=True),
        lax.all_gather(cross_vo, "dp", axis=1, tiled=True),
        lax.all_gather(ffn_in, "dp", axis=1, tiled=True),
        lax.all_gather(ffn_out, "dp", axis=1, tiled=True),
    )
    w_cqk = cqk_whole[0]
    w_cvo = cvo_whole[0]
    w_in = in_whole[0]
    w_out = out_whole[0]
    section_bias = lax.dynamic_slice_in_dim(biases, 6 * section_index, 6, 0)
    section_gain = lax.dynamic_slice_in_dim(gains, 2 * section_index, 2, 0)
    bias_in = lax.dynamic_index_in_dim(ffn_bias, section_index, 0, keepdims=False)
    section_seg = lax.dynamic_index_in_dim(segments, section_index, 0, keepdims=False)
    length = tokens.shape[2]
    position = jnp.arange(length)
    earlier = position[None, :] <= position[:, None]
    allowed_self = (section_seg[:, :, None] == section_seg[:, None, :]) & (earlier[None] | is_enc)
    allowed_cross = segments[1][:, :, None] == segments[0][:, None, :]
    source = tokens[0]
    hidden_one, kept_self = self_forward(
        source, w_qk, w_vo, section_bias, section_gain[0], allowed_self, head_count
    )

    def run_encoder():
        return encoder_forward(
            hidden_one,
            w_in,
            w_out,
            bias_in,
            section_bias,
            section_gain[1],
            w_cqk,
            w_cvo,
            biases[13],
        )

    def skip_encoder():
        flat = jnp.zeros(hidden_one.shape, jnp.bfloat16)
        wide_shape = (hidden_one.shape[0], hidden_one.shape[1], w_in.shape[1])
        return (
            flat,
            flat,
            flat,
            jnp.zeros_like(hidden_one),
            (flat, jnp.zeros(wide_shape, jnp.float32), jnp.zeros(wide_shape, jnp.bfloat16)),
        )

    memory, enc_keys, enc_values, enc_resid, enc_kept = lax.cond(is_enc, run_encoder, skip_encoder)
    got_keys, got_values = from_behind((enc_keys, enc_values), "section", 1)

    def run_decoder():
        return decoder_step(
            hidden_one,
            w_cqk,
            w_cvo,
            w_in,
            w_out,
            bias_in,
            section_bias,
            section_gain[1],
            gains[4],
            biases[12:16],
            got_keys,
            got_values,
            allowed_cross,
            cotangent,
            head_count,
        )

    def skip_decoder():
        flat = jnp.zeros(hidden_one.shape, jnp.bfloat16)
        return (flat, flat, flat, zero_tail(hidden_one, w_in))

    decoded, grad_keys, grad_values, dec_tail = lax.cond(is_enc, skip_decoder, run_decoder)
    back_keys, back_values = from_behind((grad_keys, grad_values), "section", -1)

    def run_encoder_back():
        return encoder_backward(
            w_in,
            w_out,
            section_bias,
            section_gain[1],
            w_cqk,
            w_cvo,
            memory,
            enc_resid,
            enc_kept,
            back_keys,
            back_values,
        )

    def keep_decoder():
        return dec_tail

    tail_result = lax.cond(is_enc, run_encoder_back, keep_decoder)
    (
        grad_hidden,
        tail_ops,
        grad_bin,
        grad_bout,
        grad_gain_last,
        grad_shift_last,
        cross_rows,
        grad_gain_cross,
    ) = tail_result
    layer_out = jnp.where(is_enc, memory, decoded)
    model_width = source.shape[-1]
    grad_ca, grad_cb, grad_in, grad_out = tail_whole(tail_ops)
    tail_parts = (
        lax.psum_scatter(grad_ca[None], "dp", scatter_dimension=1, tiled=True),
        lax.psum_scatter(grad_cb[None], "dp", scatter_dimension=1, tiled=True),
        lax.psum_scatter(grad_in[None], "dp", scatter_dimension=1, tiled=True),
        lax.psum_scatter(grad_out[None], "dp", scatter_dimension=1, tiled=True),
    )
    grad_source, self_ops, self_rows, grad_gain_first = self_backward(
        source,
        w_qk,
        w_vo,
        section_bias,
        section_gain[0],
        allowed_self,
        head_count,
        kept_self,
        grad_hidden,
    )
    grad_qk, grad_vo = self_whole(self_ops)
    attn_parts = (
        lax.psum_scatter(grad_qk[None], "dp", scatter_dimension=1, tiled=True),
        lax.psum_scatter(grad_vo[None], "dp", scatter_dimension=1, tiled=True),
    )
    large_parts = tuple(attn_parts) + tuple(tail_parts)
    section_rows = jnp.concatenate([self_rows, jnp.stack([grad_bout, grad_shift_last])], axis=0)
    bias_block = lax.dynamic_update_slice_in_dim(
        jnp.zeros((12, model_width), jnp.float32), section_rows, 6 * section_index, 0
    )
    grad_biases = jnp.concatenate([bias_block, cross_rows], axis=0)
    gain_block = lax.dynamic_update_slice_in_dim(
        jnp.zeros((4, model_width), jnp.float32),
        jnp.stack([grad_gain_first, grad_gain_last]),
        2 * section_index,
        0,
    )
    grad_gains = jnp.concatenate([gain_block, grad_gain_cross[None]], axis=0)
    grad_fbias = lax.dynamic_update_slice_in_dim(
        jnp.zeros_like(ffn_bias), grad_bin[None], section_index, 0
    )
    sum_gains, sum_biases, sum_fbias = lax.psum(
        (grad_gains, grad_biases, grad_fbias), ("section", "dp")
    )
    return (
        layer_out[None],
        grad_source[None],
        large_parts[0],
        large_parts[1],
        large_parts[2],
        large_parts[3],
        large_parts[4],
        large_parts[5],
        sum_gains,
        sum_biases,
        sum_fbias,
    )


MESH = pl.DeviceIdType.MESH
LOW = jnp.bfloat16
CHIPS = 8
FAR = 3
MASKED = -1e30


class Place:
    def __init__(self):
        self.section = lax.axis_index("section")
        shard = lax.axis_index("dp")
        self.core = shard % 2
        self.chip = shard // 2
        self.across = self.chip % 2
        self.along = self.chip // 2
        self.pos = self.along + self.across * (7 - 2 * self.along)

    def chip_at(self, step):
        spot = (self.pos + step + CHIPS) % CHIPS
        across = spot // 4
        along = spot + across * (7 - 2 * spot)
        return along * 2 + across

    def ring(self, step):
        return (self.section, self.chip_at(step) * 2 + self.core)

    def sibling(self):
        return (self.section, self.chip * 2 + 1 - self.core)

    def peer(self):
        return (1 - self.section, self.chip * 2 + self.core)

    def folds(self):
        near = self.along + 1 - 2 * (self.along % 2)
        far = (self.along + 2) % 4
        return (
            self.sibling(),
            (self.section, (self.along * 2 + 1 - self.across) * 2 + self.core),
            (self.section, (near * 2 + self.across) * 2 + self.core),
            (self.section, (far * 2 + self.across) * 2 + self.core),
            self.sibling(),
            self.peer(),
        )


def enter(place):
    barrier = pltpu.get_barrier_semaphore()
    others = (place.ring(1), place.ring(-1)) + place.folds()
    for other in others:
        pl.semaphore_signal(barrier, inc=1, device_id=other, device_id_type=MESH)
    pl.semaphore_wait(barrier, len(others))


class Piece:
    def __init__(self, ref, by_rows, low, span, slot):
        self.ref, self.by_rows, self.low, self.span, self.slot = ref, by_rows, low, span, slot

    def at(self, chip, core, half=None):
        low, span = self.low, self.span
        if half is not None:
            span = span // 2
            low = low + half * span
        if self.by_rows:
            return self.ref.at[chip, core, low : low + span, :]
        return self.ref.at[chip, core, :, low : low + span]


def piece_list(qk, vo, w_in, w_out, cross):
    return [
        Piece(qk, False, 0, 1536, 0),
        Piece(vo, False, 0, 1536, 1),
        Piece(w_in, False, 0, 1536, 2),
        Piece(w_in, False, 1536, 1536, 3),
        Piece(w_out, True, 0, 96, 0),
        Piece(w_out, True, 96, 96, 1),
        Piece(cross, True, 0, 96, 2),
        Piece(cross, True, 96, 96, 3),
    ]


class Gather:
    def __init__(self, place, pieces, own, ring_send, ring_recv, side_send, side_recv):
        self.place, self.pieces, self.own = place, pieces, own
        self.ring_send, self.ring_recv, self.side_send, self.side_recv = ring_send, ring_recv, side_send, side_recv

    def ring_copy(self, p, way, hop):
        sign = 1 - 2 * way
        ref = self.pieces[p].at(self.place.chip_at(-sign * hop), self.place.core, way if hop == FAR else None)
        return pltpu.make_async_remote_copy(
            self.own[p] if hop == 0 and p in self.own else ref, ref,
            self.ring_send.at[p, way, hop], self.ring_recv.at[p, way, hop],
            device_id=self.place.ring(sign), device_id_type=MESH,
        )

    def arrival(self, p, way, hop, core):
        sign = 1 - 2 * way
        return self.pieces[p].at(self.place.chip_at(-sign * (hop + 1)), core, way if hop == FAR else None)

    def side_copy(self, p, k, core):
        if k == 0:
            ref = self.pieces[p].at(self.place.chip, core)
        else:
            ref = self.arrival(p, (k - 1) // 4, (k - 1) % 4, core)
        return pltpu.make_async_remote_copy(
            self.own[p] if k == 0 and p in self.own else ref, ref, self.side_send.at[p, k], self.side_recv.at[p, k],
            device_id=self.place.sibling(), device_id_type=MESH,
        )

    def start(self, p):
        self.ring_copy(p, 0, 0).start()
        self.ring_copy(p, 1, 0).start()
        self.side_copy(p, 0, self.place.core).start()

    def event(self, p, way, hop):
        ref = self.arrival(p, way, hop, self.place.core)
        pltpu.make_async_remote_copy(
            ref, ref, self.ring_send.at[p, way, hop], self.ring_recv.at[p, way, hop],
            device_id=self.place.ring(1), device_id_type=MESH,
        ).wait_recv()
        if hop < FAR:
            self.ring_copy(p, way, hop + 1).start()
        self.side_copy(p, 1 + 4 * way + hop, self.place.core).start()

    def side_arrivals(self, p):
        for k in range(9):
            self.side_copy(p, k, 1 - self.place.core).wait_recv()

    def finish(self, p):
        for way in range(2):
            for hop in range(4):
                self.ring_copy(p, way, hop).wait_send()
        for k in range(9):
            self.side_copy(p, k, self.place.core).wait_send()


class Scatter:
    def __init__(self, place, pieces, side_c, side_r, land_c, land_r, near_c, near_r, ring_send, ring_recv, side_send, side_recv):
        self.place, self.pieces = place, pieces
        self.side_c, self.side_r, self.land_c, self.land_r = side_c, side_r, land_c, land_r
        self.near_c, self.near_r = near_c, near_r
        self.ring_send, self.ring_recv, self.side_send, self.side_recv = ring_send, ring_recv, side_send, side_recv

    def cut(self, p, ref, half):
        piece = self.pieces[p]
        if half is None:
            return ref
        span = piece.span // 2
        if piece.by_rows:
            return ref.at[half * span : (half + 1) * span, :]
        return ref.at[:, half * span : (half + 1) * span]

    def from_side(self, p, chip, half=None):
        piece = self.pieces[p]
        return self.cut(p, (self.side_r if piece.by_rows else self.side_c).at[piece.slot, chip], half)

    def landed(self, p, way, step, half=None):
        piece = self.pieces[p]
        if step == 0:
            return (self.near_r if piece.by_rows else self.near_c).at[piece.slot, way]
        return self.cut(p, (self.land_r if piece.by_rows else self.land_c).at[piece.slot, way, step - 1], half)

    def side_copy(self, p):
        piece = self.pieces[p]
        span = slice(piece.low, piece.low + piece.span)
        other = 1 - self.place.core
        src = piece.ref.at[:, other, span, :] if piece.by_rows else piece.ref.at[:, other, :, span]
        dst = (self.side_r if piece.by_rows else self.side_c).at[piece.slot]
        return pltpu.make_async_remote_copy(
            src, dst, self.side_send.at[p], self.side_recv.at[p],
            device_id=self.place.sibling(), device_id_type=MESH,
        )

    def chip_of(self, way, step):
        sign = 1 - 2 * way
        return self.place.chip_at(sign * (4 - step))

    def ring_copy(self, p, way, step):
        sign = 1 - 2 * way
        half = way if step == 0 else None
        return pltpu.make_async_remote_copy(
            self.pieces[p].at(self.chip_of(way, step), self.place.core, half), self.landed(p, way, step, half),
            self.ring_send.at[p, way, step], self.ring_recv.at[p, way, step],
            device_id=self.place.ring(sign), device_id_type=MESH,
        )

    def hand_over(self, p):
        self.side_copy(p).start()

    def start(self, p):
        self.side_copy(p).wait_recv()
        for way in range(2):
            chip = self.chip_of(way, 0)
            own = self.pieces[p].at(chip, self.place.core, way)
            total = own[...].astype(jnp.float32) + self.from_side(p, chip, way)[...].astype(jnp.float32)
            own[...] = total.astype(LOW)
            self.ring_copy(p, way, 0).start()

    def event(self, p, way, step):
        self.ring_copy(p, way, step).wait_recv()
        chip = self.chip_of(way, step + 1)
        for half in range(2):
            own = self.pieces[p].at(chip, self.place.core, half)
            total = own[...].astype(jnp.float32) + self.from_side(p, chip, half)[...].astype(jnp.float32)
            if step > 0 or half == way:
                total = total + self.landed(p, way, step, half)[...].astype(jnp.float32)
            own[...] = total.astype(LOW)
        self.ring_copy(p, way, step + 1).start()

    def last(self, p):
        chip = self.place.chip
        total = self.pieces[p].at(chip, self.place.core)[...].astype(jnp.float32)
        total = total + self.from_side(p, chip)[...].astype(jnp.float32)
        for way in range(2):
            self.ring_copy(p, way, 3).wait_recv()
            total = total + self.landed(p, way, 3)[...].astype(jnp.float32)
        return total

    def finish(self, p):
        self.side_copy(p).wait_send()
        for way in range(2):
            for step in range(4):
                self.ring_copy(p, way, step).wait_send()


def plan(ring, after, *words):
    found = []
    for word in words:
        if word[0] == "+":
            found.append([functools.partial(ring.start, int(word[1:]))])
        elif word[0] in "=f":
            found.append([functools.partial(after, word)])
        else:
            p, step = (int(part) for part in word.split("."))
            found.append([functools.partial(ring.event, p, way, step) for way in range(2)])
    return found


def serve(queue, count=None):
    for _ in range(len(queue) if count is None else min(count, len(queue))):
        for step in queue.pop(0):
            step()


def nn(left, right):
    return jnp.dot(left, right, preferred_element_type=jnp.float32)


def nt(left, right):
    return lax.dot_general(left, right, (((1,), (1,)), ((), ())), preferred_element_type=jnp.float32)


def tn(left, right):
    return lax.dot_general(left, right, (((0,), (0,)), ((), ())), preferred_element_type=jnp.float32)


def tiles(low, high, body):
    def step(j, carry):
        body(j)
        return carry

    lax.fori_loop(low, high, step, 0, unroll=min(6, high - low))


def span_of(j, width):
    return pl.ds(pl.multiple_of(j * width, width), width)


def columns_of(ref, at, rows=slice(None)):
    block = ref[:, :, rows, at]
    return block.reshape(block.shape[0] * block.shape[1] * block.shape[2], block.shape[3])


def head_masks(length, value):
    lane = lax.broadcasted_iota(jnp.int32, (length, 128), 1)
    first = jnp.where(lane < 64, value, 0.0).astype(LOW)
    second = jnp.where(lane < 64, 0.0, value).astype(LOW)
    return first, second


def mask_scores(bias_ref, key_row, query_row, causal):
    length = bias_ref.shape[0]
    keys = jnp.transpose(jnp.broadcast_to(key_row.astype(jnp.float32), (128, length)))
    keys = jnp.concatenate([keys] * (length // 128), axis=1)
    same = keys == jnp.broadcast_to(query_row.astype(jnp.float32), (length, length))
    if causal:
        key_at = lax.broadcasted_iota(jnp.int32, (length, length), 0)
        query_at = lax.broadcasted_iota(jnp.int32, (length, length), 1)
        same = same & (key_at <= query_at)
    bias_ref[...] = jnp.where(same, 0.0, MASKED)


def attend_pairs(q_ref, k_ref, v_ref, bias_ref, o_ref, lse_ref, p_ref, low, high):
    masks = head_masks(q_ref.shape[0], 0.125)

    def pair(i):
        at = span_of(i, 128)
        q2, k2 = q_ref[:, at], k_ref[:, at]
        v_turned = jnp.transpose(v_ref[:, at])
        parts = []
        for h in range(2):
            scores = nt(k2 * masks[h], q2) + bias_ref[...]
            peak = jnp.max(scores, axis=0, keepdims=True)
            exponent = jnp.exp(scores - peak)
            summed = jnp.sum(exponent, axis=0, keepdims=True)
            soft = (exponent * (1.0 / summed)).astype(LOW)
            if p_ref is not None:
                p_ref[2 * i + h] = soft
            if lse_ref is not None:
                lse_ref[2 * i + h] = peak + jnp.log(summed)
            parts.append(nn(v_turned[64 * h : 64 * h + 64], soft))
        o_ref[:, at] = jnp.transpose(jnp.concatenate(parts, axis=0)).astype(LOW)

    tiles(low, high, pair)


def attend_back_pairs(q_ref, k_ref, v_ref, bias_ref, lse_ref, p_ref, do_ref, low, high):
    masks = head_masks(q_ref.shape[0], 0.125)
    ones = head_masks(q_ref.shape[0], 1.0)

    def pair(i):
        at = span_of(i, 128)
        q2, k2, v2, do2 = q_ref[:, at], k_ref[:, at], v_ref[:, at], do_ref[:, at]
        k_turned = jnp.transpose(k2)
        parts = []
        dk = dv = None
        for h in range(2):
            if p_ref is not None:
                low_soft = p_ref[2 * i + h]
                soft = low_soft.astype(jnp.float32)
            else:
                soft = jnp.exp(nt(k2 * masks[h], q2) + bias_ref[...] - lse_ref[2 * i + h])
                low_soft = soft.astype(LOW)
            dv_h = nn(low_soft, do2 * ones[h])
            d_soft = nt(v2 * ones[h], do2)
            inner = jnp.sum(soft * d_soft, axis=0, keepdims=True)
            d_scores = (soft * (d_soft - inner)).astype(LOW)
            dk_h = nn(d_scores, q2 * masks[h])
            parts.append(nn(k_turned[64 * h : 64 * h + 64], d_scores))
            dk = dk_h if dk is None else dk + dk_h
            dv = dv_h if dv is None else dv + dv_h
        q_ref[:, at] = (jnp.transpose(jnp.concatenate(parts, axis=0)) * 0.125).astype(LOW)
        k_ref[:, at] = dk.astype(LOW)
        v_ref[:, at] = dv.astype(LOW)

    tiles(low, high, pair)


def attend_back_keys(q_ref, k_ref, v_ref, o_ref, p_ref, do_ref, dq_ref, low, span, first):
    masks = head_masks(q_ref.shape[0], 0.125)
    ones = head_masks(q_ref.shape[0], 1.0)
    short = head_masks(span, 1.0)
    rows = slice(low, low + span)

    def pair(i):
        at = span_of(i, 128)
        q2, k2, v2, do2 = q_ref[:, at], k_ref[rows, at], v_ref[rows, at], do_ref[:, at]
        k_turned = jnp.transpose(k2)
        inner = jnp.transpose(do2.astype(jnp.float32) * o_ref[:, at].astype(jnp.float32))
        parts = []
        dk = dv = None
        for h in range(2):
            low_soft = p_ref[2 * i + h, rows, :]
            soft = low_soft.astype(jnp.float32)
            dv_h = nn(low_soft, do2 * ones[h])
            d_soft = nt(v2 * short[h], do2)
            total = jnp.sum(inner[64 * h : 64 * h + 64], axis=0, keepdims=True)
            d_scores = (soft * (d_soft - total)).astype(LOW)
            dk_h = nn(d_scores, q2 * masks[h])
            parts.append(nn(k_turned[64 * h : 64 * h + 64], d_scores))
            dk = dk_h if dk is None else dk + dk_h
            dv = dv_h if dv is None else dv + dv_h
        dq = jnp.transpose(jnp.concatenate(parts, axis=0)) * 0.125
        dq_ref[:, at] = dq if first else dq_ref[:, at] + dq
        k_ref[rows, at] = dk.astype(LOW)
        v_ref[rows, at] = dv.astype(LOW)

    tiles(0, q_ref.shape[1] // 128, pair)


def gelu_parts(u):
    size = jnp.abs(u)
    bell = jnp.exp(-0.5 * u * u)
    t = 1.0 / (1.0 + 0.2316419 * size)
    tail = t * (0.127414796 + t * (-0.142248368 + t * (0.710706870 + t * (-0.726576013 + t * 0.530702714)))) * bell
    upper = jnp.where(u < 0, tail, 1.0 - tail)
    return u * upper, upper + u * bell * 0.3989422804014327


def norm_pass(norm_ref, rstd_ref, gain, shift, hidden_ref, low_ref, first=0, last=6):
    def rows(j):
        at = span_of(j, 64)
        resid = norm_ref[at, :]
        center = resid - jnp.mean(resid, axis=-1, keepdims=True)
        rstd = lax.rsqrt(jnp.mean(center * center, axis=-1, keepdims=True) + NORM_EPSILON)
        normal = center * rstd
        norm_ref[at, :] = normal
        rstd_ref[0][at, rstd_ref[1]] = rstd
        result = normal * gain + shift
        if hidden_ref is not None:
            hidden_ref[at, :] = result
        low_ref[at, :] = result.astype(LOW)

    tiles(first, last, rows)


def norm_undo(norm_ref, rstd_ref, gain, source_ref, grad_ref, low_ref, first=0, last=6, carry=None):
    width = norm_ref.shape[1]

    def rows(j, carry):
        d_gain, d_shift, d_low = carry
        at = span_of(j, 64)
        dy = source_ref[at, :].astype(jnp.float32)
        normal = norm_ref[at, :]
        scaled = dy * gain
        mean = jnp.mean(scaled, axis=-1, keepdims=True)
        along = jnp.mean(scaled * normal, axis=-1, keepdims=True)
        d_resid = rstd_ref[0][at, rstd_ref[1]] * (scaled - mean - normal * along)
        grad_ref[at, :] = d_resid
        low = d_resid.astype(LOW)
        low_ref[at, :] = low
        return (
            d_gain + jnp.sum(dy * normal, axis=0, keepdims=True),
            d_shift + jnp.sum(dy, axis=0, keepdims=True),
            d_low + jnp.sum(low.astype(jnp.float32), axis=0, keepdims=True),
        )

    zero = jnp.zeros((1, width), jnp.float32)
    return lax.fori_loop(first, last, rows, (zero, zero, zero) if carry is None else carry)


def column_total(ref):
    return jnp.sum(ref[...].astype(jnp.float32), axis=0, keepdims=True)


def layer_kernel(
    tokens, segments, gains, biases, ffn_bias, cotangent, s_qk, s_vo, s_cqk, s_cvo, s_in, s_out,
    out_layer, out_input, out_qk, out_vo, out_cqk, out_cvo, out_in, out_out, out_small,
    w_qk, w_vo, w_in, w_out, w_x,
    side_c, side_r, land_c, land_r, near_c, near_r, small, small_land, small_whole,
    sec_bias, sec_gain,
    q, k, v, o, h_low, norm_a, h, act, slope, norm_f, d_ffn, score_bias, x_send, x_recv,
    qc, kc, vc, p_c, oc, h2_low, norm_c, d_branch, d_mixed, grad, lse, rstd,
    load_sem, peer_send, peer_recv, rs, rr, ss, sr, rs2, rr2, ss2, sr2, fold_send, fold_recv, out_sem,
):
    place = Place()
    chip, core = place.chip, place.core
    width = tokens.shape[-1]
    encoder, decoder = place.section == 0, place.section == 1
    x = tokens.at[0, 0]
    rstd_a, rstd_f, rstd_c = ((rstd, slice(i, i + 1)) for i in range(3))
    loads = [
        pltpu.make_async_copy(src.at[0], dst.at[chip, core], load_sem.at[i])
        for i, (src, dst) in enumerate([(s_qk, w_qk), (s_vo, w_vo), (s_in, w_in), (s_out, w_out)])
    ]
    for copy in loads:
        copy.start()
    enter(place)
    own_cross = [
        pltpu.make_async_copy(src.at[0], w_x.at[chip, core, 48 * i : 48 * i + 48, :], load_sem.at[4 + i])
        for i, src in enumerate([s_cqk, s_cvo])
    ]
    from_encoder = [
        pltpu.make_async_remote_copy(
            src.at[0], w_x.at[chip, core, 96 + 48 * i : 144 + 48 * i, :], peer_send.at[i], peer_recv.at[i],
            device_id=place.peer(), device_id_type=MESH,
        )
        for i, src in enumerate([s_cqk, s_cvo])
    ]
    pieces = piece_list(w_qk, w_vo, w_in, w_out, w_x)
    own = {
        0: s_qk.at[0],
        1: s_vo.at[0],
        2: s_in.at[0, :, 0 : 2 * width],
        3: s_in.at[0, :, 2 * width : 4 * width],
        4: s_out.at[0, 0:96, :],
        5: s_out.at[0, 96:192, :],
    }
    gather = Gather(place, pieces, own, rs, rr, ss, sr)
    gather.start(0)
    gather.start(1)
    cot_load = pltpu.make_async_copy(cotangent, d_mixed, load_sem.at[6])

    @pl.when(encoder)
    def _():
        for copy in from_encoder:
            copy.start()
        sec_bias[0:6] = biases[0:6]
        sec_gain[0:1] = gains[0:1]
        mask_scores(score_bias, segments[0], segments[0], False)

    @pl.when(decoder)
    def _():
        for copy in own_cross:
            copy.start()
        cot_load.start()
        sec_bias[0:6] = biases[6:12]
        sec_gain[0:1] = gains[2:3]
        mask_scores(score_bias, segments[1], segments[1], True)

    small[...] = jnp.zeros_like(small)
    serve(plan(gather, None, "0.0", "1.0", "0.1", "1.1"))

    def next_pieces(first, second):
        serve(plan(gather, None, "0.2", f"+{first}", "1.2", f"+{second}", "0.3", "1.3"))

    @pl.when(encoder)
    def _():
        next_pieces(2, 3)

    @pl.when(decoder)
    def _():
        for copy in own_cross:
            copy.wait()
        for copy in from_encoder:
            copy.wait_recv()
        next_pieces(6, 7)

    for copy in loads:
        copy.wait()
    gather.side_arrivals(0)
    gather.side_arrivals(1)

    def early(count):
        @pl.when(encoder)
        def _():
            serve(first_steps, count)

        @pl.when(decoder)
        def _():
            serve(other_steps, count)

    first_steps = plan(gather, None, "2.0", "+4", "3.0", "+5", "2.1", "3.1", "4.0", "5.0")
    other_steps = plan(gather, None, "6.0", "+2", "7.0", "+3", "6.1", "7.1", "2.0", "3.0")

    def project(j):
        at = span_of(j, 256)
        past = pl.ds(pl.multiple_of(width + j * 256, 256), 256)
        q[:, at] = (nn(x[...], columns_of(w_qk, at)) + sec_bias[0:1, at]).astype(LOW)
        k[:, at] = nn(x[...], columns_of(w_qk, past)).astype(LOW)
        v[:, at] = (nn(x[...], columns_of(w_vo, at)) + sec_bias[1:2, at]).astype(LOW)

    tiles(0, 3, project)
    early(2)
    attend_pairs(q, k, v, score_bias, o, lse, None, 0, 2)
    early(2)
    attend_pairs(q, k, v, score_bias, o, lse, None, 2, 4)
    early(2)
    attend_pairs(q, k, v, score_bias, o, lse, None, 4, 6)
    early(1)

    def self_out(j):
        at = span_of(j, 256)
        past = pl.ds(pl.multiple_of(width + j * 256, 256), 256)
        norm_a[:, at] = x[:, at].astype(jnp.float32) + nn(o[...], columns_of(w_vo, past)) + sec_bias[2:3, at]

    tiles(0, 3, self_out)
    norm_pass(norm_a, rstd_a, sec_gain[0:1], sec_bias[3:4], h, h_low)
    early(None)

    def ffn_up(section, low_ref, low, high):
        def tile(j):
            at = span_of(j, 256)
            u = nn(low_ref[...], columns_of(w_in, at)) + ffn_bias[section : section + 1, at]
            value, rise = gelu_parts(u)
            act[:, at] = value.astype(LOW)
            slope[:, at] = rise.astype(LOW)

        tiles(low, high, tile)

    def ffn_down(rows=slice(None)):
        def tile(j):
            at = span_of(j, 256)
            norm_f[rows, at] = h[rows, at] + nn(act[rows, :], columns_of(w_out, at)) + sec_bias[4:5, at]

        tiles(0, 3, tile)

    def ffn_slope(section):
        for j in range(4):
            at = slice(j * width, (j + 1) * width)
            block = w_out[2 * j : 2 * j + 2].reshape(width, width)
            d_pre = (nt(d_ffn[...], block) * slope[:, at].astype(jnp.float32)).astype(LOW)
            slope[:, at] = d_pre
            set_small(24 + 4 * section + j, jnp.sum(d_pre.astype(jnp.float32), axis=0, keepdims=True))

    def ffn_hidden():
        def tile(j):
            at = span_of(j, width)
            grad[...] += nt(slope[:, at], columns_of(w_in, at))

        tiles(0, 4, tile)

    def grad_w_out(ref, low=0, high=CHIPS):
        def tile(c):
            block = tn(act[:, span_of(c, 384)], d_ffn[...])
            ref[c] = block.astype(LOW).reshape(2, 192, width)

        tiles(low, high, tile)

    def store(ref, at, value, rows=slice(None)):
        ref[:, :, rows, at] = value.astype(LOW).reshape(CHIPS, 2, 48, value.shape[1])

    def cross_weight(i, at=slice(None)):
        return columns_of(w_x, at, slice(48 * i, 48 * i + 48))

    def store_cross(i, value):
        store(w_x, slice(None), value, slice(48 * i, 48 * i + 48))

    def grad_w_in(low_ref):
        def tile(j):
            at = span_of(j, width)
            store(w_in, at, tn(low_ref[...], slope[:, at]))

        tiles(0, 4, tile)

    def set_small(row, value):
        small[row // 16, row % 16 : row % 16 + 1, :] = value

    def self_back_a(section):
        gain, shift, branch = norm_undo(norm_a, rstd_a, sec_gain[0:1], grad, grad, d_branch)
        set_small(2 * section, gain)
        set_small(8 + 6 * section + 3, shift)
        set_small(8 + 6 * section + 2, branch)
        d_mixed[...] = nt(d_branch[...], columns_of(w_vo, slice(width, 2 * width))).astype(LOW)

    def self_back_b(section):
        set_small(8 + 6 * section, column_total(q))
        set_small(8 + 6 * section + 1, column_total(v))
        grad[...] += nt(q[...], columns_of(w_qk, slice(0, width)))
        grad[...] += nt(k[...], columns_of(w_qk, slice(width, 2 * width)))
        grad[...] += nt(v[...], columns_of(w_vo, slice(0, width)))
        pltpu.make_async_copy(grad, out_input.at[0, 0], out_sem.at[1]).start()

    def self_back_qk():
        store(w_qk, slice(0, width), tn(x[...], q[...]))
        store(w_qk, slice(width, 2 * width), tn(x[...], k[...]))

    def self_back_vo():
        store(w_vo, slice(0, width), tn(x[...], v[...]))
        store(w_vo, slice(width, 2 * width), tn(o[...], d_branch[...]))

    def result_at(p):
        holder = norm_f if p < 4 else norm_c
        return holder.at[96 * (p % 4) : 96 * (p % 4) + 96, :]

    def out_copies(p, half):
        source = result_at(p)
        low = width * half
        target = (
            out_qk.at[0, :, low : low + width],
            out_vo.at[0, :, low : low + width],
            out_in.at[0, :, low : low + width],
            out_in.at[0, :, 2 * width + low : 3 * width + low],
            out_out.at[0, 48 * half : 48 * half + 48, :],
            out_out.at[0, 96 + 48 * half : 144 + 48 * half, :],
            (out_cqk, out_cvo)[half].at[0],
            (out_cqk, out_cvo)[half].at[0],
        )[p]
        return pltpu.make_async_copy(
            source.at[48 * half : 48 * half + 48], target, out_sem.at[2 + 2 * min(p, 6) + half]
        )

    def finish_piece(scatter, word):
        p = int(word[1:])
        if word[0] == "f":
            fold_end(p)
            return
        total = scatter.last(p)
        target = result_at(p)
        if p >= 4:
            target[...] = total
        else:
            target[0:48] = total[:, :width]
            target[48:96] = total[:, width:]
        if p == 7:
            to_encoder.start()
        else:
            out_copies(p, 0).start()
            out_copies(p, 1).start()

    to_encoder = pltpu.make_async_remote_copy(
        result_at(7), result_at(7), peer_send.at[2], peer_recv.at[2], device_id=place.peer(), device_id_type=MESH
    )
    cross_copies = [
        pltpu.make_async_remote_copy(
            x_send.at[128 * c : 128 * c + 128], x_recv.at[128 * c : 128 * c + 128], peer_send.at[3 + c], peer_recv.at[3 + c],
            device_id=place.peer(), device_id_type=MESH,
        )
        for c in range(3)
    ]
    layer_copy = pltpu.make_async_copy(x_send, out_layer.at[0, 0], out_sem.at[0])

    def fold(i):
        if i == 5:
            source, target = small, small_whole
        else:
            source, target = small.at[1 - core if i == 0 else core], small_land.at[i]
        return pltpu.make_async_remote_copy(
            source, target, fold_send.at[i], fold_recv.at[i], device_id=place.folds()[i], device_id_type=MESH
        )

    def fold_start(i):
        fold(i).start()

    def fold_end(i):
        fold(i).wait()
        if i < 4:
            small[core] = small[core] + small_land[i]
        elif i == 4:
            small[1 - core] = small_land[i]
        if i < 5:
            fold(i + 1).start()

    @pl.when(encoder)
    def _():
        serve(plan(gather, None, "2.2", "3.2", "4.1", "5.1", "2.3", "3.3"))
        gather.side_arrivals(2)
        gather.side_arrivals(3)
        queue = plan(gather, None, "4.2", "5.2", "4.3", "5.3")
        for part in range(4):
            ffn_up(0, h_low, 3 * part, 3 * part + 3)
            serve(queue, 1)
        gather.side_arrivals(4)
        gather.side_arrivals(5)
        for c in range(3):
            ffn_down(slice(128 * c, 128 * c + 128))
            norm_pass(norm_f, rstd_f, gains[1:2], biases[5:6], None, x_send, 2 * c, 2 * c + 2)
            cross_copies[c].start()
        layer_copy.start()
        for copy in from_encoder:
            copy.wait_send()
        for p in range(6):
            gather.finish(p)
        layer_copy.wait()
        found = None
        for c in range(3):
            cross_copies[c].wait()
            found = norm_undo(norm_f, rstd_f, gains[1:2], x_recv, grad, d_ffn, 2 * c, 2 * c + 2, found)
        gain, shift, branch = found
        set_small(1, gain)
        set_small(8 + 5, shift)
        set_small(8 + 4, branch)
        scatter = Scatter(
            place, piece_list(w_qk, w_vo, w_in, w_x, None),
            side_c, side_r, land_c, land_r, near_c, near_r, rs2, rr2, ss2, sr2,
        )
        after = functools.partial(finish_piece, scatter)
        grad_w_out(w_x)
        scatter.hand_over(4)
        scatter.hand_over(5)
        ffn_slope(0)
        scatter.start(4)
        scatter.start(5)
        ffn_hidden()
        queue = plan(scatter, after, "4.0", "5.0", "+2", "+3", "4.1", "5.1", "2.0", "3.0", "4.2", "5.2", "2.1", "3.1", "=4", "=5")
        serve(queue, 1)
        grad_w_in(h_low)
        scatter.hand_over(2)
        scatter.hand_over(3)
        serve(queue, 1)
        self_back_a(0)
        serve(queue, 3)
        for part in range(3):
            attend_back_pairs(q, k, v, score_bias, lse, None, d_mixed, 2 * part, 2 * part + 2)
            serve(queue, 1)
        self_back_b(0)
        fold_start(0)
        serve(queue, 2)
        self_back_qk()
        scatter.hand_over(0)
        serve(queue, 1)
        self_back_vo()
        scatter.hand_over(1)
        serve(queue, 1)
        scatter.start(0)
        serve(queue, 1)
        scatter.start(1)
        fold_end(0)
        serve(queue)
        serve(
            plan(
                scatter, after, "2.2", "3.2", "0.0", "f1", "1.0", "0.1", "1.1", "f2", "=2", "=3", "0.2", "f3",
                "1.2", "f4", "=0", "=1",
            )
        )
        to_encoder.wait_recv()
        out_copies(7, 0).start()
        out_copies(7, 1).start()
        for p in range(6):
            scatter.finish(p)

    @pl.when(decoder)
    def _():
        queue = plan(gather, None, "6.2", "+4", "7.2", "+5", "2.1", "3.1", "6.3", "7.3", "2.2", "3.2", "4.0", "5.0", "4.1", "5.1", "2.3", "3.3", "4.2", "5.2", "4.3", "5.3")
        serve(queue, 8)
        gather.side_arrivals(6)
        gather.side_arrivals(7)
        mask_scores(score_bias, segments[0], segments[1], False)

        def cross_query(j):
            at = span_of(j, 256)
            qc[:, at] = (nn(h_low[...], cross_weight(0, at)) + biases[12:13, at]).astype(LOW)

        tiles(0, 3, cross_query)
        serve(queue, 8)
        for c in range(3):
            rows = slice(128 * c, 128 * c + 128)
            cross_copies[c].wait_recv()

            def cross_keys(j):
                at = span_of(j, 256)
                kc[rows, at] = nn(x_recv[rows, :], cross_weight(2, at)).astype(LOW)
                vc[rows, at] = (nn(x_recv[rows, :], cross_weight(3, at)) + biases[13:14, at]).astype(LOW)

            tiles(0, 3, cross_keys)
        attend_pairs(qc, kc, vc, score_bias, oc, None, p_c, 0, 3)
        serve(queue, 2)
        attend_pairs(qc, kc, vc, score_bias, oc, None, p_c, 3, 6)
        serve(queue)
        gather.side_arrivals(2)
        gather.side_arrivals(3)

        def cross_out(j):
            at = span_of(j, 256)
            norm_c[:, at] = h[:, at] + nn(oc[...], cross_weight(1, at)) + biases[14:15, at]

        tiles(0, 3, cross_out)
        norm_pass(norm_c, rstd_c, gains[4:5], biases[15:16], h, h2_low)
        ffn_up(1, h2_low, 0, 12)
        gather.side_arrivals(4)
        gather.side_arrivals(5)
        ffn_down()
        norm_pass(norm_f, rstd_f, gains[3:4], biases[11:12], None, x_send)
        layer_copy.start()
        cot_load.wait()
        gain, shift, branch = norm_undo(norm_f, rstd_f, gains[3:4], d_mixed, grad, d_ffn)
        set_small(3, gain)
        set_small(8 + 11, shift)
        set_small(8 + 10, branch)
        scatter = Scatter(
            place, pieces, side_c, side_r, land_c, land_r, near_c, near_r, rs2, rr2, ss2, sr2,
        )
        after = functools.partial(finish_piece, scatter)
        ffn_slope(1)
        ffn_hidden()
        gain, shift, branch = norm_undo(norm_c, rstd_c, gains[4:5], grad, grad, d_branch)
        set_small(4, gain)
        set_small(8 + 15, shift)
        set_small(8 + 14, branch)
        d_mixed[...] = nt(d_branch[...], cross_weight(1)).astype(LOW)
        layer_copy.wait()
        queue = plan(scatter, after, "4.0", "5.0", "4.1", "5.1", "+2", "+3", "4.2", "5.2", "2.0", "3.0", "=4", "=5", "+7", "2.1", "3.1", "+6", "7.0", "2.2", "3.2")
        for c in range(3):
            rows = slice(128 * c, 128 * c + 128)
            attend_back_keys(qc, kc, vc, oc, p_c, d_mixed, norm_f, 128 * c, 128, c == 0)
            x_send[rows, :] = (nt(kc[rows, :], cross_weight(2)) + nt(vc[rows, :], cross_weight(3))).astype(LOW)
            cross_copies[c].start()
            if c == 0:
                for p in (4, 5):
                    gather.finish(p)
                grad_w_out(w_out, 0, 4)
            elif c == 1:
                grad_w_out(w_out, 4, 8)
                scatter.hand_over(4)
                scatter.hand_over(5)
        scatter.start(4)
        scatter.start(5)
        for p in (0, 1, 2, 3, 6, 7):
            gather.finish(p)
        qc[...] = norm_f[...].astype(LOW)
        grad_w_in(h2_low)
        scatter.hand_over(2)
        scatter.hand_over(3)
        serve(queue, 2)
        store_cross(2, tn(x_recv[...], kc[...]))
        store_cross(3, tn(x_recv[...], vc[...]))
        scatter.hand_over(7)
        serve(queue, 4)
        grad[...] += nt(qc[...], cross_weight(0))
        store_cross(0, tn(h_low[...], qc[...]))
        store_cross(1, tn(oc[...], d_branch[...]))
        scatter.hand_over(6)
        set_small(8 + 12, column_total(qc))
        set_small(8 + 13, column_total(vc))
        serve(queue, 1)
        mask_scores(score_bias, segments[1], segments[1], True)
        self_back_a(1)
        serve(queue, 3)
        for part in range(3):
            attend_back_pairs(q, k, v, score_bias, lse, None, d_mixed, 2 * part, 2 * part + 2)
            serve(queue, 1)
        self_back_b(1)
        fold_start(0)
        serve(queue, 2)
        self_back_qk()
        scatter.hand_over(0)
        serve(queue, 1)
        self_back_vo()
        scatter.hand_over(1)
        serve(queue)
        scatter.start(0)
        fold_end(0)
        serve(
            plan(
                scatter, after, "6.0", "+1", "7.1", "6.1", "=2", "=3", "f1", "0.0", "1.0", "7.2", "6.2", "f2", "0.1",
                "1.1", "=7", "=6", "0.2", "f3", "1.2", "f4", "=0", "=1",
            )
        )
        for copy in cross_copies:
            copy.wait_send()
        to_encoder.wait_send()
        for p in range(8):
            scatter.finish(p)

    fold_end(5)
    for half in range(2):
        out_small[16 * half : 16 * half + 16] = small[half] + small_whole[half]
    for p in range(7):
        for half in range(2):
            out_copies(p, half).wait()
    pltpu.make_async_copy(grad, out_input.at[0, 0], out_sem.at[1]).wait()


def layer_call(tokens, segments, cotangent, attn_qk, attn_vo, cross_qk, cross_vo, ffn_in, ffn_out, gains, biases, ffn_bias):
    length, width = tokens.shape[2:]
    hidden = ffn_in.shape[2]

    def result(like, kind):
        return jax.ShapeDtypeStruct(like.shape, kind)

    def low(*shape):
        return pltpu.VMEM(shape, LOW)

    def full(*shape):
        return pltpu.VMEM(shape, jnp.float32)

    any_space = pl.BlockSpec(memory_space=pl.ANY)
    in_vmem = pl.BlockSpec(memory_space=pltpu.VMEM)
    flat, wide, exact = low(length, width), low(length, hidden), full(length, width)
    dma = pltpu.SemaphoreType.DMA
    scratch = [
        low(CHIPS, 2, 48, 2 * width), low(CHIPS, 2, 48, 2 * width), low(CHIPS, 2, 48, hidden),
        low(CHIPS, 2, 192, width), low(CHIPS, 2, 192, width),
        low(4, CHIPS, 48, 2 * width), low(4, CHIPS, 96, width),
        low(4, 2, 3, 48, 2 * width), low(4, 2, 3, 96, width),
        low(4, 2, 48, width), low(4, 2, 48, width),
        full(2, 16, width), full(5, 16, width), full(2, 16, width),
        full(8, width), full(1, width),
        flat, flat, flat, flat, flat, exact, exact, wide, wide, exact, flat, full(length, length), flat, flat,
        flat, flat, flat, low(HEADS, length, length), flat, flat, exact, flat, flat, exact,
        full(HEADS, 1, length), full(length, 128),
        dma((7,)), dma((6,)), dma((6,)),
        dma((8, 2, 4)), dma((8, 2, 4)), dma((8, 9)), dma((8, 9)),
        dma((8, 2, 4)), dma((8, 2, 4)), dma((8,)), dma((8,)),
        dma((6,)), dma((6,)), dma((16,)),
    ]
    return pl.pallas_call(
        layer_kernel,
        out_shape=(
            result(tokens, LOW), result(tokens, jnp.float32),
            result(attn_qk, jnp.float32), result(attn_vo, jnp.float32),
            result(cross_qk, jnp.float32), result(cross_vo, jnp.float32),
            result(ffn_in, jnp.float32), result(ffn_out, jnp.float32),
            jax.ShapeDtypeStruct((32, width), jnp.float32),
        ),
        in_specs=[in_vmem] * 5 + [any_space] * 7,
        out_specs=(any_space,) * 8 + (in_vmem,),
        scratch_shapes=scratch,
        compiler_params=pltpu.CompilerParams(
            collective_id=0, has_side_effects=True, vmem_limit_bytes=63 * 1024 * 1024 + 524288
        ),
        name="layer_pair",
    )(
        tokens, segments, gains, biases, ffn_bias, cotangent[0],
        attn_qk, attn_vo, cross_qk, cross_vo, ffn_in, ffn_out,
    )


def hand_out_kernel(*refs):
    sources, small, rest = refs[:8], refs[8], refs[9:]
    targets, (gains, biases, ffn_bias), held, (take, give) = rest[:8], rest[8:11], rest[11:19], rest[19:]
    inward = [pltpu.make_async_copy(a, b, take.at[i]) for i, (a, b) in enumerate(zip(sources, held))]
    outward = [pltpu.make_async_copy(a, b, give.at[i]) for i, (a, b) in enumerate(zip(held, targets))]
    for copy in inward:
        copy.start()
    gains[...] = small[0:5]
    biases[...] = small[8:24]
    width = gains.shape[1]
    for row in range(8):
        ffn_bias[row // 4 : row // 4 + 1, width * (row % 4) : width * (row % 4 + 1)] = small[24 + row : 25 + row]
    for first, second in zip(inward, outward):
        first.wait()
        second.start()
    for copy in outward:
        copy.wait()


def hand_out(results, gains, biases, ffn_bias):
    any_space = pl.BlockSpec(memory_space=pl.ANY)
    in_vmem = pl.BlockSpec(memory_space=pltpu.VMEM)
    return pl.pallas_call(
        hand_out_kernel,
        out_shape=tuple(jax.ShapeDtypeStruct(r.shape, r.dtype) for r in tuple(results[:8]) + (gains, biases, ffn_bias)),
        in_specs=[any_space] * 8 + [in_vmem],
        out_specs=(any_space,) * 8 + (in_vmem,) * 3,
        scratch_shapes=[pltpu.VMEM(r.shape, r.dtype) for r in results[:8]] + [pltpu.SemaphoreType.DMA((8,))] * 2,
        compiler_params=pltpu.CompilerParams(vmem_limit_bytes=63 * 1024 * 1024),
        name="hand_out",
    )(*results)


def local_ring(
    tokens, segments, cotangent, attn_qk, attn_vo, cross_qk, cross_vo, ffn_in, ffn_out, gains, biases, ffn_bias
):
    results = layer_call(
        tokens, segments, cotangent, attn_qk, attn_vo, cross_qk, cross_vo, ffn_in, ffn_out, gains, biases, ffn_bias
    )
    return hand_out(results, gains, biases, ffn_bias)


def solution(mesh):
    any_size = mesh.shape["section"] != 2 or mesh.shape["dp"] != 2 * CHIPS
    placed = (
        P("section", "dp", None, None),
        P(None, "dp", None),
        P("dp", None, None),
        P("section", "dp", None),
        P("section", "dp", None),
        P("section", "dp", None),
        P("section", "dp", None),
        P("section", "dp", None),
        P("section", "dp", None),
        P(),
        P(),
        P(),
    )
    return jax.shard_map(
        local_any if any_size else local_ring,
        mesh=mesh,
        in_specs=placed,
        out_specs=(
            P("section", "dp", None, None),
            P("section", "dp", None, None),
            P("section", "dp", None),
            P("section", "dp", None),
            P("section", "dp", None),
            P("section", "dp", None),
            P("section", "dp", None),
            P("section", "dp", None),
            P(),
            P(),
            P(),
        ),
        check_vma=False,
    )
```

```python
import functools

import jax
import jax.numpy as jnp
from jax import lax
from jax.experimental import pallas as pl
from jax.experimental.pallas import tpu as pltpu
from jax.sharding import PartitionSpec as P

HEADS = 12


NORM_EPSILON = 1e-05


def from_behind(x, axis, by):
    devices = lax.axis_size(axis)
    pairs = [(i, i + by) for i in range(devices) if 0 <= i + by < devices]
    return lax.ppermute(x, axis, pairs)


def product(left, right):
    return jnp.einsum("rld,de->rle", left, right, preferred_element_type=jnp.float32)


def back_product(grad, right):
    return jnp.einsum("rle,de->rld", grad, right, preferred_element_type=jnp.float32)


def weight_grad(left, grad):
    return jnp.einsum("rld,rle->de", left, grad, preferred_element_type=jnp.float32)


def column_sum(values):
    return jnp.sum(values.astype(jnp.float32), axis=(0, 1))


def norm_rows(resid, gain, shift):
    center = resid - jnp.mean(resid, axis=-1, keepdims=True)
    spread = jnp.mean(center * center, axis=-1, keepdims=True)
    return center * lax.rsqrt(spread + NORM_EPSILON) * gain + shift


def norm_back(resid, gain, shift, grad):
    unused, pull = jax.vjp(norm_rows, resid, gain, shift)
    return pull(grad)


def split_heads(values, head_count):
    return values.reshape(
        values.shape[0], values.shape[1], head_count, values.shape[2] // head_count
    )


def masked_scores(query_heads, key_heads, allowed):
    scale = query_heads.shape[-1] ** (-0.5)
    scores = (
        jnp.einsum("rqhe,rkhe->rhqk", query_heads, key_heads, preferred_element_type=jnp.float32)
        * scale
    )
    return jnp.where(allowed[:, None], scores, -1e30)


def attend(query, key_rows, value_rows, allowed, head_count):
    query_heads = split_heads(query, head_count)
    scores = masked_scores(query_heads, split_heads(key_rows, head_count), allowed)
    peak = jnp.max(scores, axis=-1, keepdims=True)
    exponent = jnp.exp(scores - peak)
    summed = jnp.sum(exponent, axis=-1, keepdims=True)
    soft = (exponent / summed).astype(jnp.bfloat16)
    mixed = jnp.einsum(
        "rhqk,rkhe->rqhe",
        soft,
        split_heads(value_rows, head_count),
        preferred_element_type=jnp.float32,
    )
    return (mixed.reshape(query.shape), peak + jnp.log(summed))


def attend_back(query, key_rows, value_rows, allowed, log_total, grad_mixed, head_count):
    query_heads = split_heads(query, head_count)
    key_heads = split_heads(key_rows, head_count)
    value_heads = split_heads(value_rows, head_count)
    grad_heads = split_heads(grad_mixed, head_count)
    scale = query_heads.shape[-1] ** (-0.5)
    soft = jnp.exp(masked_scores(query_heads, key_heads, allowed) - log_total)
    grad_values = jnp.einsum(
        "rhqk,rqhe->rkhe", soft.astype(jnp.bfloat16), grad_heads, preferred_element_type=jnp.float32
    )
    grad_soft = jnp.einsum(
        "rqhe,rkhe->rhqk", grad_heads, value_heads, preferred_element_type=jnp.float32
    )
    inner_sum = jnp.sum(soft * grad_soft, axis=-1, keepdims=True)
    grad_scores = (soft * (grad_soft - inner_sum)).astype(jnp.bfloat16)
    grad_query = (
        jnp.einsum("rhqk,rkhe->rqhe", grad_scores, key_heads, preferred_element_type=jnp.float32)
        * scale
    )
    grad_keys = (
        jnp.einsum("rhqk,rqhe->rkhe", grad_scores, query_heads, preferred_element_type=jnp.float32)
        * scale
    )
    return (
        grad_query.reshape(query.shape),
        grad_keys.reshape(key_rows.shape),
        grad_values.reshape(key_rows.shape),
    )


def self_forward(inputs, w_qk, w_vo, section_bias, gain, allowed, head_count):
    model_width = inputs.shape[-1]
    query = (product(inputs, w_qk[:, :model_width]) + section_bias[0]).astype(jnp.bfloat16)
    key_rows = product(inputs, w_qk[:, model_width:]).astype(jnp.bfloat16)
    value_rows = (product(inputs, w_vo[:, :model_width]) + section_bias[1]).astype(jnp.bfloat16)
    mixed, log_total = attend(query, key_rows, value_rows, allowed, head_count)
    mixed = mixed.astype(jnp.bfloat16)
    resid = inputs.astype(jnp.float32) + product(mixed, w_vo[:, model_width:]) + section_bias[2]
    return (
        norm_rows(resid, gain, section_bias[3]),
        (query, key_rows, value_rows, log_total, mixed, resid),
    )


def self_backward(inputs, w_qk, w_vo, section_bias, gain, allowed, head_count, kept, grad_hidden):
    query, key_rows, value_rows, log_total, mixed, resid = kept
    model_width = inputs.shape[-1]
    grad_resid, grad_gain, grad_shift = norm_back(resid, gain, section_bias[3], grad_hidden)
    grad_branch = grad_resid.astype(jnp.bfloat16)
    grad_mixed = back_product(grad_branch, w_vo[:, model_width:]).astype(jnp.bfloat16)
    grad_query, grad_keys, grad_values = attend_back(
        query, key_rows, value_rows, allowed, log_total, grad_mixed, head_count
    )
    grad_query = grad_query.astype(jnp.bfloat16)
    grad_keys = grad_keys.astype(jnp.bfloat16)
    grad_values = grad_values.astype(jnp.bfloat16)
    grad_pair = jnp.concatenate([grad_query, grad_keys], axis=-1)
    grad_inputs = (
        grad_resid
        + back_product(grad_pair, w_qk)
        + back_product(grad_values, w_vo[:, :model_width])
    )
    grad_rows = jnp.stack(
        [column_sum(grad_query), column_sum(grad_values), column_sum(grad_branch), grad_shift]
    )
    return (grad_inputs, (inputs, grad_pair, grad_values, mixed, grad_branch), grad_rows, grad_gain)


def ffn_forward(hidden, w_in, w_out, b_in, b_out):
    hidden_low = hidden.astype(jnp.bfloat16)
    pre_act = product(hidden_low, w_in) + b_in
    activated = jax.nn.gelu(pre_act, approximate=False).astype(jnp.bfloat16)
    return (product(activated, w_out) + b_out, (hidden_low, pre_act, activated))


def gelu_exact(values):
    return jax.nn.gelu(values, approximate=False)


def ffn_backward(w_in, w_out, kept, grad_branch):
    hidden_low, pre_act, activated = kept
    grad_low = grad_branch.astype(jnp.bfloat16)
    grad_act = back_product(grad_low, w_out)
    unused, pull = jax.vjp(gelu_exact, pre_act)
    grad_pre = pull(grad_act)[0].astype(jnp.bfloat16)
    grad_hidden = back_product(grad_pre, w_in)
    return (
        grad_hidden,
        (hidden_low, grad_pre, activated, grad_low),
        column_sum(grad_pre),
        column_sum(grad_low),
    )


def encoder_forward(hidden, w_in, w_out, b_in, section_bias, gain_last, w_ck, w_cv, bias_cv):
    branch, kept = ffn_forward(hidden, w_in, w_out, b_in, section_bias[4])
    resid = hidden + branch
    memory = norm_rows(resid, gain_last, section_bias[5]).astype(jnp.bfloat16)
    key_rows = product(memory, w_ck).astype(jnp.bfloat16)
    value_rows = (product(memory, w_cv) + bias_cv).astype(jnp.bfloat16)
    return (memory, key_rows, value_rows, resid, kept)


def encoder_backward(
    w_in, w_out, section_bias, gain_last, w_ck, w_cv, memory, resid, kept, grad_keys, grad_values
):
    grad_memory = back_product(grad_keys, w_ck) + back_product(grad_values, w_cv)
    grad_last, grad_gain, grad_shift = norm_back(resid, gain_last, section_bias[5], grad_memory)
    grad_ffn, ffn_ops, grad_bin, grad_bout = ffn_backward(w_in, w_out, kept, grad_last)
    zero_line = jnp.zeros_like(grad_gain)
    cross_rows = jnp.stack([zero_line, column_sum(grad_values), zero_line, zero_line])
    operands = (memory, grad_keys, memory, grad_values) + ffn_ops
    return (
        grad_last + grad_ffn,
        operands,
        grad_bin,
        grad_bout,
        grad_gain,
        grad_shift,
        cross_rows,
        zero_line,
    )


def decoder_step(
    hidden,
    w_cq,
    w_co,
    w_in,
    w_out,
    b_in,
    section_bias,
    gain_last,
    gain_cross,
    cross_bias,
    key_rows,
    value_rows,
    allowed,
    cotangent,
    head_count,
):
    hidden_low = hidden.astype(jnp.bfloat16)
    query = (product(hidden_low, w_cq) + cross_bias[0]).astype(jnp.bfloat16)
    mixed, log_total = attend(query, key_rows, value_rows, allowed, head_count)
    mixed = mixed.astype(jnp.bfloat16)
    resid_mid = hidden + product(mixed, w_co) + cross_bias[2]
    middle = norm_rows(resid_mid, gain_cross, cross_bias[3])
    branch, kept = ffn_forward(middle, w_in, w_out, b_in, section_bias[4])
    resid_last = middle + branch
    result = norm_rows(resid_last, gain_last, section_bias[5])
    grad_last, grad_gain, grad_shift = norm_back(
        resid_last, gain_last, section_bias[5], cotangent.astype(jnp.float32)
    )
    grad_ffn, ffn_ops, grad_bin, grad_bout = ffn_backward(w_in, w_out, kept, grad_last)
    grad_mid, grad_gain_cross, grad_shift_cross = norm_back(
        resid_mid, gain_cross, cross_bias[3], grad_last + grad_ffn
    )
    grad_branch = grad_mid.astype(jnp.bfloat16)
    grad_mixed = back_product(grad_branch, w_co).astype(jnp.bfloat16)
    grad_query, grad_keys, grad_values = attend_back(
        query, key_rows, value_rows, allowed, log_total, grad_mixed, head_count
    )
    grad_query = grad_query.astype(jnp.bfloat16)
    grad_hidden = grad_mid + back_product(grad_query, w_cq)
    cross_rows = jnp.stack(
        [
            column_sum(grad_query),
            jnp.zeros_like(grad_gain),
            column_sum(grad_branch),
            grad_shift_cross,
        ]
    )
    operands = (hidden_low, grad_query, mixed, grad_branch) + ffn_ops
    tail_result = (
        grad_hidden,
        operands,
        grad_bin,
        grad_bout,
        grad_gain,
        grad_shift,
        cross_rows,
        grad_gain_cross,
    )
    return (
        result.astype(jnp.bfloat16),
        grad_keys.astype(jnp.bfloat16),
        grad_values.astype(jnp.bfloat16),
        tail_result,
    )


def zero_tail(hidden, w_in):
    model_width = hidden.shape[-1]
    ffn_width = w_in.shape[1]
    flat = jnp.zeros(hidden.shape, jnp.bfloat16)
    wide = jnp.zeros((hidden.shape[0], hidden.shape[1], ffn_width), jnp.bfloat16)
    zero_line = jnp.zeros((model_width,), jnp.float32)
    operands = (flat, flat, flat, flat, flat, wide, wide, flat)
    return (
        jnp.zeros_like(hidden),
        operands,
        jnp.zeros((ffn_width,), jnp.float32),
        zero_line,
        zero_line,
        zero_line,
        jnp.zeros((4, model_width), jnp.float32),
        zero_line,
    )


def tail_whole(operands):
    return (
        weight_grad(operands[0], operands[1]),
        weight_grad(operands[2], operands[3]),
        weight_grad(operands[4], operands[5]),
        weight_grad(operands[6], operands[7]),
    )


def self_whole(operands):
    grad_qk = weight_grad(operands[0], operands[1])
    grad_vo = jnp.concatenate(
        [weight_grad(operands[0], operands[2]), weight_grad(operands[3], operands[4])], axis=1
    )
    return (grad_qk, grad_vo)


def local_any(
    tokens,
    segments,
    cotangent,
    attn_qk,
    attn_vo,
    cross_qk,
    cross_vo,
    ffn_in,
    ffn_out,
    gains,
    biases,
    ffn_bias,
):
    head_count = HEADS
    section_index = lax.axis_index("section")
    is_enc = section_index == 0
    qk_whole, vo_whole = (
        lax.all_gather(attn_qk, "dp", axis=1, tiled=True),
        lax.all_gather(attn_vo, "dp", axis=1, tiled=True),
    )
    w_qk = qk_whole[0]
    w_vo = vo_whole[0]
    cqk_whole, cvo_whole, in_whole, out_whole = (
        lax.all_gather(cross_qk, "dp", axis=1, tiled=True),
        lax.all_gather(cross_vo, "dp", axis=1, tiled=True),
        lax.all_gather(ffn_in, "dp", axis=1, tiled=True),
        lax.all_gather(ffn_out, "dp", axis=1, tiled=True),
    )
    w_cqk = cqk_whole[0]
    w_cvo = cvo_whole[0]
    w_in = in_whole[0]
    w_out = out_whole[0]
    section_bias = lax.dynamic_slice_in_dim(biases, 6 * section_index, 6, 0)
    section_gain = lax.dynamic_slice_in_dim(gains, 2 * section_index, 2, 0)
    bias_in = lax.dynamic_index_in_dim(ffn_bias, section_index, 0, keepdims=False)
    section_seg = lax.dynamic_index_in_dim(segments, section_index, 0, keepdims=False)
    length = tokens.shape[2]
    position = jnp.arange(length)
    earlier = position[None, :] <= position[:, None]
    allowed_self = (section_seg[:, :, None] == section_seg[:, None, :]) & (earlier[None] | is_enc)
    allowed_cross = segments[1][:, :, None] == segments[0][:, None, :]
    source = tokens[0]
    hidden_one, kept_self = self_forward(
        source, w_qk, w_vo, section_bias, section_gain[0], allowed_self, head_count
    )

    def run_encoder():
        return encoder_forward(
            hidden_one,
            w_in,
            w_out,
            bias_in,
            section_bias,
            section_gain[1],
            w_cqk,
            w_cvo,
            biases[13],
        )

    def skip_encoder():
        flat = jnp.zeros(hidden_one.shape, jnp.bfloat16)
        wide_shape = (hidden_one.shape[0], hidden_one.shape[1], w_in.shape[1])
        return (
            flat,
            flat,
            flat,
            jnp.zeros_like(hidden_one),
            (flat, jnp.zeros(wide_shape, jnp.float32), jnp.zeros(wide_shape, jnp.bfloat16)),
        )

    memory, enc_keys, enc_values, enc_resid, enc_kept = lax.cond(is_enc, run_encoder, skip_encoder)
    got_keys, got_values = from_behind((enc_keys, enc_values), "section", 1)

    def run_decoder():
        return decoder_step(
            hidden_one,
            w_cqk,
            w_cvo,
            w_in,
            w_out,
            bias_in,
            section_bias,
            section_gain[1],
            gains[4],
            biases[12:16],
            got_keys,
            got_values,
            allowed_cross,
            cotangent,
            head_count,
        )

    def skip_decoder():
        flat = jnp.zeros(hidden_one.shape, jnp.bfloat16)
        return (flat, flat, flat, zero_tail(hidden_one, w_in))

    decoded, grad_keys, grad_values, dec_tail = lax.cond(is_enc, skip_decoder, run_decoder)
    back_keys, back_values = from_behind((grad_keys, grad_values), "section", -1)

    def run_encoder_back():
        return encoder_backward(
            w_in,
            w_out,
            section_bias,
            section_gain[1],
            w_cqk,
            w_cvo,
            memory,
            enc_resid,
            enc_kept,
            back_keys,
            back_values,
        )

    def keep_decoder():
        return dec_tail

    tail_result = lax.cond(is_enc, run_encoder_back, keep_decoder)
    (
        grad_hidden,
        tail_ops,
        grad_bin,
        grad_bout,
        grad_gain_last,
        grad_shift_last,
        cross_rows,
        grad_gain_cross,
    ) = tail_result
    layer_out = jnp.where(is_enc, memory, decoded)
    model_width = source.shape[-1]
    grad_ca, grad_cb, grad_in, grad_out = tail_whole(tail_ops)
    tail_parts = (
        lax.psum_scatter(grad_ca[None], "dp", scatter_dimension=1, tiled=True),
        lax.psum_scatter(grad_cb[None], "dp", scatter_dimension=1, tiled=True),
        lax.psum_scatter(grad_in[None], "dp", scatter_dimension=1, tiled=True),
        lax.psum_scatter(grad_out[None], "dp", scatter_dimension=1, tiled=True),
    )
    grad_source, self_ops, self_rows, grad_gain_first = self_backward(
        source,
        w_qk,
        w_vo,
        section_bias,
        section_gain[0],
        allowed_self,
        head_count,
        kept_self,
        grad_hidden,
    )
    grad_qk, grad_vo = self_whole(self_ops)
    attn_parts = (
        lax.psum_scatter(grad_qk[None], "dp", scatter_dimension=1, tiled=True),
        lax.psum_scatter(grad_vo[None], "dp", scatter_dimension=1, tiled=True),
    )
    large_parts = tuple(attn_parts) + tuple(tail_parts)
    section_rows = jnp.concatenate([self_rows, jnp.stack([grad_bout, grad_shift_last])], axis=0)
    bias_block = lax.dynamic_update_slice_in_dim(
        jnp.zeros((12, model_width), jnp.float32), section_rows, 6 * section_index, 0
    )
    grad_biases = jnp.concatenate([bias_block, cross_rows], axis=0)
    gain_block = lax.dynamic_update_slice_in_dim(
        jnp.zeros((4, model_width), jnp.float32),
        jnp.stack([grad_gain_first, grad_gain_last]),
        2 * section_index,
        0,
    )
    grad_gains = jnp.concatenate([gain_block, grad_gain_cross[None]], axis=0)
    grad_fbias = lax.dynamic_update_slice_in_dim(
        jnp.zeros_like(ffn_bias), grad_bin[None], section_index, 0
    )
    sum_gains, sum_biases, sum_fbias = lax.psum(
        (grad_gains, grad_biases, grad_fbias), ("section", "dp")
    )
    return (
        layer_out[None],
        grad_source[None],
        large_parts[0],
        large_parts[1],
        large_parts[2],
        large_parts[3],
        large_parts[4],
        large_parts[5],
        sum_gains,
        sum_biases,
        sum_fbias,
    )


MESH = pl.DeviceIdType.MESH
LOW = jnp.bfloat16
CHIPS = 8
FAR = 3
MASKED = -1e30


class Place:
    def __init__(self):
        self.section = lax.axis_index("section")
        shard = lax.axis_index("dp")
        self.core = shard % 2
        self.chip = shard // 2
        self.across = self.chip % 2
        self.along = self.chip // 2
        self.pos = self.along + self.across * (7 - 2 * self.along)

    def chip_at(self, step):
        spot = (self.pos + step + CHIPS) % CHIPS
        across = spot // 4
        along = spot + across * (7 - 2 * spot)
        return along * 2 + across

    def ring(self, step):
        return (self.section, self.chip_at(step) * 2 + self.core)

    def sibling(self):
        return (self.section, self.chip * 2 + 1 - self.core)

    def peer(self):
        return (1 - self.section, self.chip * 2 + self.core)

    def folds(self):
        near = self.along + 1 - 2 * (self.along % 2)
        far = (self.along + 2) % 4
        return (
            self.sibling(),
            (self.section, (self.along * 2 + 1 - self.across) * 2 + self.core),
            (self.section, (near * 2 + self.across) * 2 + self.core),
            (self.section, (far * 2 + self.across) * 2 + self.core),
            self.sibling(),
            self.peer(),
        )


def enter(place):
    barrier = pltpu.get_barrier_semaphore()
    others = (place.ring(1), place.ring(-1)) + place.folds()
    for other in others:
        pl.semaphore_signal(barrier, inc=1, device_id=other, device_id_type=MESH)
    pl.semaphore_wait(barrier, len(others))


class Piece:
    def __init__(self, ref, by_rows, low, span, slot):
        self.ref, self.by_rows, self.low, self.span, self.slot = ref, by_rows, low, span, slot

    def at(self, chip, core, half=None):
        low, span = self.low, self.span
        if half is not None:
            span = span // 2
            low = low + half * span
        if self.by_rows:
            return self.ref.at[chip, core, low : low + span, :]
        return self.ref.at[chip, core, :, low : low + span]


def piece_list(qk, vo, w_in, w_out, cross):
    return [
        Piece(qk, False, 0, 1536, 0),
        Piece(vo, False, 0, 1536, 1),
        Piece(w_in, False, 0, 1536, 2),
        Piece(w_in, False, 1536, 1536, 3),
        Piece(w_out, True, 0, 96, 0),
        Piece(w_out, True, 96, 96, 1),
        Piece(cross, True, 0, 96, 2),
        Piece(cross, True, 96, 96, 3),
    ]


class Gather:
    def __init__(self, place, pieces, own, ring_send, ring_recv, side_send, side_recv):
        self.place, self.pieces, self.own = place, pieces, own
        self.ring_send, self.ring_recv, self.side_send, self.side_recv = ring_send, ring_recv, side_send, side_recv

    def ring_copy(self, p, way, hop):
        sign = 1 - 2 * way
        ref = self.pieces[p].at(self.place.chip_at(-sign * hop), self.place.core, way if hop == FAR else None)
        return pltpu.make_async_remote_copy(
            self.own[p] if hop == 0 and p in self.own else ref, ref,
            self.ring_send.at[p, way, hop], self.ring_recv.at[p, way, hop],
            device_id=self.place.ring(sign), device_id_type=MESH,
        )

    def arrival(self, p, way, hop, core):
        sign = 1 - 2 * way
        return self.pieces[p].at(self.place.chip_at(-sign * (hop + 1)), core, way if hop == FAR else None)

    def side_copy(self, p, k, core):
        if k == 0:
            ref = self.pieces[p].at(self.place.chip, core)
        else:
            ref = self.arrival(p, (k - 1) // 4, (k - 1) % 4, core)
        return pltpu.make_async_remote_copy(
            self.own[p] if k == 0 and p in self.own else ref, ref, self.side_send.at[p, k], self.side_recv.at[p, k],
            device_id=self.place.sibling(), device_id_type=MESH,
        )

    def start(self, p):
        self.ring_copy(p, 0, 0).start()
        self.ring_copy(p, 1, 0).start()
        self.side_copy(p, 0, self.place.core).start()

    def event(self, p, way, hop):
        ref = self.arrival(p, way, hop, self.place.core)
        pltpu.make_async_remote_copy(
            ref, ref, self.ring_send.at[p, way, hop], self.ring_recv.at[p, way, hop],
            device_id=self.place.ring(1), device_id_type=MESH,
        ).wait_recv()
        if hop < FAR:
            self.ring_copy(p, way, hop + 1).start()
        self.side_copy(p, 1 + 4 * way + hop, self.place.core).start()

    def side_arrivals(self, p):
        for k in range(9):
            self.side_copy(p, k, 1 - self.place.core).wait_recv()

    def finish(self, p):
        for way in range(2):
            for hop in range(4):
                self.ring_copy(p, way, hop).wait_send()
        for k in range(9):
            self.side_copy(p, k, self.place.core).wait_send()


class Scatter:
    def __init__(self, place, pieces, side_c, side_r, land_c, land_r, near_c, near_r, ring_send, ring_recv, side_send, side_recv):
        self.place, self.pieces = place, pieces
        self.side_c, self.side_r, self.land_c, self.land_r = side_c, side_r, land_c, land_r
        self.near_c, self.near_r = near_c, near_r
        self.ring_send, self.ring_recv, self.side_send, self.side_recv = ring_send, ring_recv, side_send, side_recv

    def cut(self, p, ref, half):
        piece = self.pieces[p]
        if half is None:
            return ref
        span = piece.span // 2
        if piece.by_rows:
            return ref.at[half * span : (half + 1) * span, :]
        return ref.at[:, half * span : (half + 1) * span]

    def from_side(self, p, chip, half=None):
        piece = self.pieces[p]
        return self.cut(p, (self.side_r if piece.by_rows else self.side_c).at[piece.slot, chip], half)

    def landed(self, p, way, step, half=None):
        piece = self.pieces[p]
        if step == 0:
            return (self.near_r if piece.by_rows else self.near_c).at[piece.slot, way]
        return self.cut(p, (self.land_r if piece.by_rows else self.land_c).at[piece.slot, way, step - 1], half)

    def side_copy(self, p, step):
        piece = self.pieces[p]
        chip = self.place.chip_at(step)
        return pltpu.make_async_remote_copy(
            piece.at(chip, 1 - self.place.core), self.from_side(p, chip),
            self.side_send.at[p, step], self.side_recv.at[p, step],
            device_id=self.place.sibling(), device_id_type=MESH,
        )

    def chip_of(self, way, step):
        sign = 1 - 2 * way
        return self.place.chip_at(sign * (4 - step))

    def ring_copy(self, p, way, step):
        sign = 1 - 2 * way
        half = way if step == 0 else None
        return pltpu.make_async_remote_copy(
            self.pieces[p].at(self.chip_of(way, step), self.place.core, half), self.landed(p, way, step, half),
            self.ring_send.at[p, way, step], self.ring_recv.at[p, way, step],
            device_id=self.place.ring(sign), device_id_type=MESH,
        )

    def hand_over(self, p):
        for step in (4, 3, 5, 2, 6, 1, 7, 0):
            self.side_copy(p, step).start()

    def start(self, p):
        self.side_copy(p, 4).wait_recv()
        for way in range(2):
            chip = self.chip_of(way, 0)
            own = self.pieces[p].at(chip, self.place.core, way)
            total = own[...].astype(jnp.float32) + self.from_side(p, chip, way)[...].astype(jnp.float32)
            own[...] = total.astype(LOW)
            self.ring_copy(p, way, 0).start()

    def event(self, p, way, step):
        self.side_copy(p, (3 - step, 5 + step)[way]).wait_recv()
        self.ring_copy(p, way, step).wait_recv()
        chip = self.chip_of(way, step + 1)
        for half in range(2):
            own = self.pieces[p].at(chip, self.place.core, half)
            total = own[...].astype(jnp.float32) + self.from_side(p, chip, half)[...].astype(jnp.float32)
            if step > 0 or half == way:
                total = total + self.landed(p, way, step, half)[...].astype(jnp.float32)
            own[...] = total.astype(LOW)
        self.ring_copy(p, way, step + 1).start()

    def last(self, p):
        chip = self.place.chip
        self.side_copy(p, 0).wait_recv()
        total = self.pieces[p].at(chip, self.place.core)[...].astype(jnp.float32)
        total = total + self.from_side(p, chip)[...].astype(jnp.float32)
        for way in range(2):
            self.ring_copy(p, way, 3).wait_recv()
            total = total + self.landed(p, way, 3)[...].astype(jnp.float32)
        return total

    def finish(self, p):
        for step in range(CHIPS):
            self.side_copy(p, step).wait_send()
        for way in range(2):
            for step in range(4):
                self.ring_copy(p, way, step).wait_send()


def plan(ring, after, *words):
    found = []
    for word in words:
        if word[0] == "+":
            found.append([functools.partial(ring.start, int(word[1:]))])
        elif word[0] in "=f":
            found.append([functools.partial(after, word)])
        else:
            p, step = (int(part) for part in word.split("."))
            found.append([functools.partial(ring.event, p, way, step) for way in range(2)])
    return found


def serve(queue, count=None):
    for _ in range(len(queue) if count is None else min(count, len(queue))):
        for step in queue.pop(0):
            step()


def nn(left, right):
    return jnp.dot(left, right, preferred_element_type=jnp.float32)


def nt(left, right):
    return lax.dot_general(left, right, (((1,), (1,)), ((), ())), preferred_element_type=jnp.float32)


def tn(left, right):
    return lax.dot_general(left, right, (((0,), (0,)), ((), ())), preferred_element_type=jnp.float32)


def tiles(low, high, body):
    def step(j, carry):
        body(j)
        return carry

    lax.fori_loop(low, high, step, 0, unroll=min(6, high - low))


def span_of(j, width):
    return pl.ds(pl.multiple_of(j * width, width), width)


def columns_of(ref, at, rows=slice(None)):
    block = ref[:, :, rows, at]
    return block.reshape(block.shape[0] * block.shape[1] * block.shape[2], block.shape[3])


def head_masks(length, value):
    lane = lax.broadcasted_iota(jnp.int32, (length, 128), 1)
    first = jnp.where(lane < 64, value, 0.0).astype(LOW)
    second = jnp.where(lane < 64, 0.0, value).astype(LOW)
    return first, second


def mask_scores(bias_ref, key_row, query_row, causal):
    length = bias_ref.shape[0]
    keys = jnp.transpose(jnp.broadcast_to(key_row.astype(jnp.float32), (128, length)))
    keys = jnp.concatenate([keys] * (length // 128), axis=1)
    same = keys == jnp.broadcast_to(query_row.astype(jnp.float32), (length, length))
    if causal:
        key_at = lax.broadcasted_iota(jnp.int32, (length, length), 0)
        query_at = lax.broadcasted_iota(jnp.int32, (length, length), 1)
        same = same & (key_at <= query_at)
    bias_ref[...] = jnp.where(same, 0.0, MASKED)


def attend_pairs(q_ref, k_ref, v_ref, bias_ref, o_ref, lse_ref, p_ref, low, high):
    masks = head_masks(q_ref.shape[0], 0.125)

    def pair(i):
        at = span_of(i, 128)
        q2, k2 = q_ref[:, at], k_ref[:, at]
        v_turned = jnp.transpose(v_ref[:, at])
        parts = []
        for h in range(2):
            scores = nt(k2 * masks[h], q2) + bias_ref[...]
            peak = jnp.max(scores, axis=0, keepdims=True)
            exponent = jnp.exp(scores - peak)
            summed = jnp.sum(exponent, axis=0, keepdims=True)
            soft = (exponent * (1.0 / summed)).astype(LOW)
            if p_ref is not None:
                p_ref[2 * i + h] = soft
            if lse_ref is not None:
                lse_ref[2 * i + h] = peak + jnp.log(summed)
            parts.append(nn(v_turned[64 * h : 64 * h + 64], soft))
        o_ref[:, at] = jnp.transpose(jnp.concatenate(parts, axis=0)).astype(LOW)

    tiles(low, high, pair)


def attend_back_pairs(q_ref, k_ref, v_ref, bias_ref, lse_ref, p_ref, do_ref, low, high):
    masks = head_masks(q_ref.shape[0], 0.125)
    ones = head_masks(q_ref.shape[0], 1.0)

    def pair(i):
        at = span_of(i, 128)
        q2, k2, v2, do2 = q_ref[:, at], k_ref[:, at], v_ref[:, at], do_ref[:, at]
        k_turned = jnp.transpose(k2)
        parts = []
        dk = dv = None
        for h in range(2):
            if p_ref is not None:
                low_soft = p_ref[2 * i + h]
                soft = low_soft.astype(jnp.float32)
            else:
                soft = jnp.exp(nt(k2 * masks[h], q2) + bias_ref[...] - lse_ref[2 * i + h])
                low_soft = soft.astype(LOW)
            dv_h = nn(low_soft, do2 * ones[h])
            d_soft = nt(v2 * ones[h], do2)
            inner = jnp.sum(soft * d_soft, axis=0, keepdims=True)
            d_scores = (soft * (d_soft - inner)).astype(LOW)
            dk_h = nn(d_scores, q2 * masks[h])
            parts.append(nn(k_turned[64 * h : 64 * h + 64], d_scores))
            dk = dk_h if dk is None else dk + dk_h
            dv = dv_h if dv is None else dv + dv_h
        q_ref[:, at] = (jnp.transpose(jnp.concatenate(parts, axis=0)) * 0.125).astype(LOW)
        k_ref[:, at] = dk.astype(LOW)
        v_ref[:, at] = dv.astype(LOW)

    tiles(low, high, pair)


def attend_back_keys(q_ref, k_ref, v_ref, o_ref, p_ref, do_ref, dq_ref, low, span, first):
    masks = head_masks(q_ref.shape[0], 0.125)
    ones = head_masks(q_ref.shape[0], 1.0)
    short = head_masks(span, 1.0)
    rows = slice(low, low + span)

    def pair(i):
        at = span_of(i, 128)
        q2, k2, v2, do2 = q_ref[:, at], k_ref[rows, at], v_ref[rows, at], do_ref[:, at]
        k_turned = jnp.transpose(k2)
        inner = jnp.transpose(do2.astype(jnp.float32) * o_ref[:, at].astype(jnp.float32))
        parts = []
        dk = dv = None
        for h in range(2):
            low_soft = p_ref[2 * i + h, rows, :]
            soft = low_soft.astype(jnp.float32)
            dv_h = nn(low_soft, do2 * ones[h])
            d_soft = nt(v2 * short[h], do2)
            total = jnp.sum(inner[64 * h : 64 * h + 64], axis=0, keepdims=True)
            d_scores = (soft * (d_soft - total)).astype(LOW)
            dk_h = nn(d_scores, q2 * masks[h])
            parts.append(nn(k_turned[64 * h : 64 * h + 64], d_scores))
            dk = dk_h if dk is None else dk + dk_h
            dv = dv_h if dv is None else dv + dv_h
        dq = jnp.transpose(jnp.concatenate(parts, axis=0)) * 0.125
        dq_ref[:, at] = dq if first else dq_ref[:, at] + dq
        k_ref[rows, at] = dk.astype(LOW)
        v_ref[rows, at] = dv.astype(LOW)

    tiles(0, q_ref.shape[1] // 128, pair)


def gelu_parts(u):
    size = jnp.abs(u)
    bell = jnp.exp(-0.5 * u * u)
    t = 1.0 / (1.0 + 0.2316419 * size)
    tail = t * (0.127414796 + t * (-0.142248368 + t * (0.710706870 + t * (-0.726576013 + t * 0.530702714)))) * bell
    upper = jnp.where(u < 0, tail, 1.0 - tail)
    return u * upper, upper + u * bell * 0.3989422804014327


def norm_pass(norm_ref, rstd_ref, gain, shift, hidden_ref, low_ref, first=0, last=6):
    def rows(j):
        at = span_of(j, 64)
        resid = norm_ref[at, :]
        center = resid - jnp.mean(resid, axis=-1, keepdims=True)
        rstd = lax.rsqrt(jnp.mean(center * center, axis=-1, keepdims=True) + NORM_EPSILON)
        normal = center * rstd
        norm_ref[at, :] = normal
        rstd_ref[0][at, rstd_ref[1]] = rstd
        result = normal * gain + shift
        if hidden_ref is not None:
            hidden_ref[at, :] = result
        low_ref[at, :] = result.astype(LOW)

    tiles(first, last, rows)


def norm_undo(norm_ref, rstd_ref, gain, source_ref, grad_ref, low_ref, first=0, last=6, carry=None):
    width = norm_ref.shape[1]

    def rows(j, carry):
        d_gain, d_shift, d_low = carry
        at = span_of(j, 64)
        dy = source_ref[at, :].astype(jnp.float32)
        normal = norm_ref[at, :]
        scaled = dy * gain
        mean = jnp.mean(scaled, axis=-1, keepdims=True)
        along = jnp.mean(scaled * normal, axis=-1, keepdims=True)
        d_resid = rstd_ref[0][at, rstd_ref[1]] * (scaled - mean - normal * along)
        grad_ref[at, :] = d_resid
        low = d_resid.astype(LOW)
        low_ref[at, :] = low
        return (
            d_gain + jnp.sum(dy * normal, axis=0, keepdims=True),
            d_shift + jnp.sum(dy, axis=0, keepdims=True),
            d_low + jnp.sum(low.astype(jnp.float32), axis=0, keepdims=True),
        )

    zero = jnp.zeros((1, width), jnp.float32)
    return lax.fori_loop(first, last, rows, (zero, zero, zero) if carry is None else carry)


def column_total(ref):
    return jnp.sum(ref[...].astype(jnp.float32), axis=0, keepdims=True)


def layer_kernel(
    i_tokens, i_segments, i_gains, i_biases, i_ffn_bias, cotangent, s_qk, s_vo, s_cqk, s_cvo, s_in, s_out,
    out_layer, out_input, out_qk, out_vo, out_cqk, out_cvo, out_in, out_out, out_small,
    w_qk, w_vo, w_in, w_out, w_x,
    side_c, side_r, land_c, land_r, near_c, near_r, small, small_land, small_whole,
    sec_bias, sec_gain,
    q, k, v, o, h_low, norm_a, h, act, slope, norm_f, d_ffn, score_bias, x_send, x_recv,
    qc, kc, vc, p_c, oc, h2_low, norm_c, d_branch, d_mixed, grad, lse, rstd,
    x, segments, gains, biases, ffn_bias, load_sem, peer_send, peer_recv, rs, rr, ss, sr, rs2, rr2, ss2, sr2, fold_send, fold_recv, out_sem,
):
    place = Place()
    chip, core = place.chip, place.core
    width = x.shape[-1]
    encoder, decoder = place.section == 0, place.section == 1
    rstd_a, rstd_f, rstd_c = ((rstd, slice(i, i + 1)) for i in range(3))
    loads = [
        pltpu.make_async_copy(src.at[0], dst.at[chip, core], load_sem.at[i])
        for i, (src, dst) in enumerate([(s_qk, w_qk), (s_vo, w_vo), (s_in, w_in), (s_out, w_out)])
    ]
    small_loads = [
        pltpu.make_async_copy(src, dst, load_sem.at[7 + i])
        for i, (src, dst) in enumerate(
            [(i_tokens.at[0, 0], x), (i_segments, segments), (i_gains, gains), (i_biases, biases), (i_ffn_bias, ffn_bias)]
        )
    ]
    for copy in loads + small_loads:
        copy.start()
    enter(place)
    own_cross = [
        pltpu.make_async_copy(src.at[0], w_x.at[chip, core, 48 * i : 48 * i + 48, :], load_sem.at[4 + i])
        for i, src in enumerate([s_cqk, s_cvo])
    ]
    from_encoder = [
        pltpu.make_async_remote_copy(
            src.at[0], w_x.at[chip, core, 96 + 48 * i : 144 + 48 * i, :], peer_send.at[i], peer_recv.at[i],
            device_id=place.peer(), device_id_type=MESH,
        )
        for i, src in enumerate([s_cqk, s_cvo])
    ]
    pieces = piece_list(w_qk, w_vo, w_in, w_out, w_x)
    own = {
        0: s_qk.at[0],
        1: s_vo.at[0],
        2: s_in.at[0, :, 0 : 2 * width],
        3: s_in.at[0, :, 2 * width : 4 * width],
        4: s_out.at[0, 0:96, :],
        5: s_out.at[0, 96:192, :],
    }
    gather = Gather(place, pieces, own, rs, rr, ss, sr)
    gather.start(0)
    gather.start(1)
    cot_load = pltpu.make_async_copy(cotangent, d_mixed, load_sem.at[6])
    for copy in small_loads:
        copy.wait()

    @pl.when(encoder)
    def _():
        for copy in from_encoder:
            copy.start()
        sec_bias[0:6] = biases[0:6]
        sec_gain[0:1] = gains[0:1]
        mask_scores(score_bias, segments[0], segments[0], False)

    @pl.when(decoder)
    def _():
        for copy in own_cross:
            copy.start()
        cot_load.start()
        sec_bias[0:6] = biases[6:12]
        sec_gain[0:1] = gains[2:3]
        mask_scores(score_bias, segments[1], segments[1], True)

    small[...] = jnp.zeros_like(small)
    serve(plan(gather, None, "0.0", "1.0", "0.1", "1.1"))

    def next_pieces(first, second):
        serve(plan(gather, None, "0.2", f"+{first}", "1.2", f"+{second}", "0.3", "1.3"))

    @pl.when(encoder)
    def _():
        next_pieces(2, 3)

    @pl.when(decoder)
    def _():
        for copy in own_cross:
            copy.wait()
        for copy in from_encoder:
            copy.wait_recv()
        next_pieces(6, 7)

    for copy in loads:
        copy.wait()
    gather.side_arrivals(0)
    gather.side_arrivals(1)

    def early(count):
        @pl.when(encoder)
        def _():
            serve(first_steps, count)

        @pl.when(decoder)
        def _():
            serve(other_steps, count)

    first_steps = plan(gather, None, "2.0", "+4", "3.0", "+5", "2.1", "3.1", "4.0", "5.0")
    other_steps = plan(gather, None, "6.0", "+2", "7.0", "+3", "6.1", "7.1", "2.0", "3.0")

    def project(j):
        at = span_of(j, 256)
        past = pl.ds(pl.multiple_of(width + j * 256, 256), 256)
        q[:, at] = (nn(x[...], columns_of(w_qk, at)) + sec_bias[0:1, at]).astype(LOW)
        k[:, at] = nn(x[...], columns_of(w_qk, past)).astype(LOW)
        v[:, at] = (nn(x[...], columns_of(w_vo, at)) + sec_bias[1:2, at]).astype(LOW)

    tiles(0, 3, project)
    early(2)
    attend_pairs(q, k, v, score_bias, o, lse, None, 0, 2)
    early(2)
    attend_pairs(q, k, v, score_bias, o, lse, None, 2, 4)
    early(2)
    attend_pairs(q, k, v, score_bias, o, lse, None, 4, 6)
    early(1)

    def self_out(j):
        at = span_of(j, 256)
        past = pl.ds(pl.multiple_of(width + j * 256, 256), 256)
        norm_a[:, at] = x[:, at].astype(jnp.float32) + nn(o[...], columns_of(w_vo, past)) + sec_bias[2:3, at]

    tiles(0, 3, self_out)
    norm_pass(norm_a, rstd_a, sec_gain[0:1], sec_bias[3:4], h, h_low)
    early(None)

    def ffn_up(section, low_ref, low, high):
        def tile(j):
            at = span_of(j, 256)
            u = nn(low_ref[...], columns_of(w_in, at)) + ffn_bias[section : section + 1, at]
            value, rise = gelu_parts(u)
            act[:, at] = value.astype(LOW)
            slope[:, at] = rise.astype(LOW)

        tiles(low, high, tile)

    def ffn_down(rows=slice(None)):
        def tile(j):
            at = span_of(j, 256)
            norm_f[rows, at] = h[rows, at] + nn(act[rows, :], columns_of(w_out, at)) + sec_bias[4:5, at]

        tiles(0, 3, tile)

    def ffn_slope(section):
        for j in range(4):
            at = slice(j * width, (j + 1) * width)
            block = w_out[2 * j : 2 * j + 2].reshape(width, width)
            d_pre = (nt(d_ffn[...], block) * slope[:, at].astype(jnp.float32)).astype(LOW)
            slope[:, at] = d_pre
            set_small(24 + 4 * section + j, jnp.sum(d_pre.astype(jnp.float32), axis=0, keepdims=True))

    def ffn_hidden():
        def tile(j):
            at = span_of(j, width)
            grad[...] += nt(slope[:, at], columns_of(w_in, at))

        tiles(0, 4, tile)

    def grad_w_out(ref):
        def tile(c):
            block = tn(act[:, span_of(c, 384)], d_ffn[...])
            ref[c] = block.astype(LOW).reshape(2, 192, width)

        tiles(0, CHIPS, tile)

    def store(ref, at, value, rows=slice(None)):
        ref[:, :, rows, at] = value.astype(LOW).reshape(CHIPS, 2, 48, value.shape[1])

    def cross_weight(i, at=slice(None)):
        return columns_of(w_x, at, slice(48 * i, 48 * i + 48))

    def store_cross(i, value):
        store(w_x, slice(None), value, slice(48 * i, 48 * i + 48))

    def grad_w_in(low_ref):
        def tile(j):
            at = span_of(j, width)
            store(w_in, at, tn(low_ref[...], slope[:, at]))

        tiles(0, 4, tile)

    def set_small(row, value):
        small[row // 16, row % 16 : row % 16 + 1, :] = value

    def self_back_a(section):
        gain, shift, branch = norm_undo(norm_a, rstd_a, sec_gain[0:1], grad, grad, d_branch)
        set_small(2 * section, gain)
        set_small(8 + 6 * section + 3, shift)
        set_small(8 + 6 * section + 2, branch)
        d_mixed[...] = nt(d_branch[...], columns_of(w_vo, slice(width, 2 * width))).astype(LOW)

    def self_back_b(section):
        set_small(8 + 6 * section, column_total(q))
        set_small(8 + 6 * section + 1, column_total(v))
        grad[...] += nt(q[...], columns_of(w_qk, slice(0, width)))
        grad[...] += nt(k[...], columns_of(w_qk, slice(width, 2 * width)))
        grad[...] += nt(v[...], columns_of(w_vo, slice(0, width)))
        pltpu.make_async_copy(grad, out_input.at[0, 0], out_sem.at[1]).start()

    def self_back_qk():
        store(w_qk, slice(0, width), tn(x[...], q[...]))
        store(w_qk, slice(width, 2 * width), tn(x[...], k[...]))

    def self_back_vo():
        store(w_vo, slice(0, width), tn(x[...], v[...]))
        store(w_vo, slice(width, 2 * width), tn(o[...], d_branch[...]))

    def result_at(p):
        holder = norm_f if p < 4 else norm_c
        return holder.at[96 * (p % 4) : 96 * (p % 4) + 96, :]

    def out_copies(p, half):
        source = result_at(p)
        low = width * half
        target = (
            out_qk.at[0, :, low : low + width],
            out_vo.at[0, :, low : low + width],
            out_in.at[0, :, low : low + width],
            out_in.at[0, :, 2 * width + low : 3 * width + low],
            out_out.at[0, 48 * half : 48 * half + 48, :],
            out_out.at[0, 96 + 48 * half : 144 + 48 * half, :],
            (out_cqk, out_cvo)[half].at[0],
            (out_cqk, out_cvo)[half].at[0],
        )[p]
        return pltpu.make_async_copy(
            source.at[48 * half : 48 * half + 48], target, out_sem.at[2 + 2 * min(p, 6) + half]
        )

    def finish_piece(scatter, word):
        p = int(word[1:])
        if word[0] == "f":
            fold_end(p)
            return
        total = scatter.last(p)
        target = result_at(p)
        if p >= 4:
            target[...] = total
        else:
            target[0:48] = total[:, :width]
            target[48:96] = total[:, width:]
        if p == 7:
            to_encoder.start()
        else:
            out_copies(p, 0).start()
            out_copies(p, 1).start()

    to_encoder = pltpu.make_async_remote_copy(
        result_at(7), result_at(7), peer_send.at[2], peer_recv.at[2], device_id=place.peer(), device_id_type=MESH
    )
    cross_copies = [
        pltpu.make_async_remote_copy(
            x_send.at[128 * c : 128 * c + 128], x_recv.at[128 * c : 128 * c + 128], peer_send.at[3 + c], peer_recv.at[3 + c],
            device_id=place.peer(), device_id_type=MESH,
        )
        for c in range(3)
    ]
    layer_copy = pltpu.make_async_copy(x_send, out_layer.at[0, 0], out_sem.at[0])

    def fold(i):
        if i == 5:
            source, target = small, small_whole
        else:
            source, target = small.at[1 - core if i == 0 else core], small_land.at[i]
        return pltpu.make_async_remote_copy(
            source, target, fold_send.at[i], fold_recv.at[i], device_id=place.folds()[i], device_id_type=MESH
        )

    def fold_start(i):
        fold(i).start()

    def fold_end(i):
        fold(i).wait()
        if i < 4:
            small[core] = small[core] + small_land[i]
        elif i == 4:
            small[1 - core] = small_land[i]
        if i < 5:
            fold(i + 1).start()

    @pl.when(encoder)
    def _():
        serve(plan(gather, None, "2.2", "3.2", "4.1", "5.1", "2.3", "3.3"))
        gather.side_arrivals(2)
        gather.side_arrivals(3)
        queue = plan(gather, None, "4.2", "5.2", "4.3", "5.3")
        for part in range(4):
            ffn_up(0, h_low, 3 * part, 3 * part + 3)
            serve(queue, 1)
        gather.side_arrivals(4)
        gather.side_arrivals(5)
        for c in range(3):
            ffn_down(slice(128 * c, 128 * c + 128))
            norm_pass(norm_f, rstd_f, gains[1:2], biases[5:6], None, x_send, 2 * c, 2 * c + 2)
            cross_copies[c].start()
        layer_copy.start()
        for copy in from_encoder:
            copy.wait_send()
        for p in range(6):
            gather.finish(p)
        layer_copy.wait()
        found = None
        for c in range(3):
            cross_copies[c].wait()
            found = norm_undo(norm_f, rstd_f, gains[1:2], x_recv, grad, d_ffn, 2 * c, 2 * c + 2, found)
        gain, shift, branch = found
        set_small(1, gain)
        set_small(8 + 5, shift)
        set_small(8 + 4, branch)
        scatter = Scatter(
            place, piece_list(w_qk, w_vo, w_in, w_x, None),
            side_c, side_r, land_c, land_r, near_c, near_r, rs2, rr2, ss2, sr2,
        )
        after = functools.partial(finish_piece, scatter)
        grad_w_out(w_x)
        scatter.hand_over(4)
        scatter.hand_over(5)
        ffn_slope(0)
        scatter.start(4)
        scatter.start(5)
        ffn_hidden()
        queue = plan(scatter, after, "4.0", "5.0", "+2", "+3", "4.1", "5.1", "2.0", "3.0", "4.2", "5.2", "2.1", "3.1", "=4", "=5")
        serve(queue, 1)
        grad_w_in(h_low)
        scatter.hand_over(2)
        scatter.hand_over(3)
        serve(queue, 1)
        self_back_a(0)
        serve(queue, 3)
        for part in range(3):
            attend_back_pairs(q, k, v, score_bias, lse, None, d_mixed, 2 * part, 2 * part + 2)
            serve(queue, 1)
        self_back_b(0)
        fold_start(0)
        serve(queue, 2)
        self_back_qk()
        scatter.hand_over(0)
        serve(queue, 1)
        self_back_vo()
        scatter.hand_over(1)
        serve(queue, 1)
        scatter.start(0)
        serve(queue, 1)
        scatter.start(1)
        fold_end(0)
        serve(queue)
        serve(
            plan(
                scatter, after, "2.2", "3.2", "0.0", "f1", "1.0", "0.1", "1.1", "f2", "=2", "=3", "0.2", "f3",
                "1.2", "f4", "=0", "=1",
            )
        )
        to_encoder.wait_recv()
        out_copies(7, 0).start()
        out_copies(7, 1).start()
        for p in range(6):
            scatter.finish(p)

    @pl.when(decoder)
    def _():
        queue = plan(gather, None, "6.2", "+4", "7.2", "+5", "2.1", "3.1", "6.3", "7.3", "2.2", "3.2", "4.0", "5.0", "4.1", "5.1", "2.3", "3.3", "4.2", "5.2", "4.3", "5.3")
        serve(queue, 8)
        gather.side_arrivals(6)
        gather.side_arrivals(7)
        mask_scores(score_bias, segments[0], segments[1], False)

        def cross_query(j):
            at = span_of(j, 256)
            qc[:, at] = (nn(h_low[...], cross_weight(0, at)) + biases[12:13, at]).astype(LOW)

        tiles(0, 3, cross_query)
        serve(queue, 8)
        for c in range(3):
            rows = slice(128 * c, 128 * c + 128)
            cross_copies[c].wait_recv()

            def cross_keys(j):
                at = span_of(j, 256)
                kc[rows, at] = nn(x_recv[rows, :], cross_weight(2, at)).astype(LOW)
                vc[rows, at] = (nn(x_recv[rows, :], cross_weight(3, at)) + biases[13:14, at]).astype(LOW)

            tiles(0, 3, cross_keys)
        attend_pairs(qc, kc, vc, score_bias, oc, None, p_c, 0, 3)
        serve(queue, 2)
        attend_pairs(qc, kc, vc, score_bias, oc, None, p_c, 3, 6)
        serve(queue)
        gather.side_arrivals(2)
        gather.side_arrivals(3)

        def cross_out(j):
            at = span_of(j, 256)
            norm_c[:, at] = h[:, at] + nn(oc[...], cross_weight(1, at)) + biases[14:15, at]

        tiles(0, 3, cross_out)
        norm_pass(norm_c, rstd_c, gains[4:5], biases[15:16], h, h2_low)
        ffn_up(1, h2_low, 0, 12)
        gather.side_arrivals(4)
        gather.side_arrivals(5)
        ffn_down()
        norm_pass(norm_f, rstd_f, gains[3:4], biases[11:12], None, x_send)
        layer_copy.start()
        cot_load.wait()
        gain, shift, branch = norm_undo(norm_f, rstd_f, gains[3:4], d_mixed, grad, d_ffn)
        set_small(3, gain)
        set_small(8 + 11, shift)
        set_small(8 + 10, branch)
        scatter = Scatter(
            place, pieces, side_c, side_r, land_c, land_r, near_c, near_r, rs2, rr2, ss2, sr2,
        )
        after = functools.partial(finish_piece, scatter)
        ffn_slope(1)
        ffn_hidden()
        gain, shift, branch = norm_undo(norm_c, rstd_c, gains[4:5], grad, grad, d_branch)
        set_small(4, gain)
        set_small(8 + 15, shift)
        set_small(8 + 14, branch)
        d_mixed[...] = nt(d_branch[...], cross_weight(1)).astype(LOW)
        layer_copy.wait()
        queue = plan(scatter, after, "4.0", "5.0", "+2", "+3", "4.1", "5.1", "+7", "2.0", "3.0", "4.2", "5.2", "+6", "2.1", "3.1", "=4", "=5", "7.0", "2.2", "3.2")
        for c in range(3):
            rows = slice(128 * c, 128 * c + 128)
            attend_back_keys(qc, kc, vc, oc, p_c, d_mixed, norm_f, 128 * c, 128, c == 0)
            x_send[rows, :] = (nt(kc[rows, :], cross_weight(2)) + nt(vc[rows, :], cross_weight(3))).astype(LOW)
            cross_copies[c].start()
            if c == 1:
                for p in (4, 5):
                    gather.finish(p)
                grad_w_out(w_out)
                scatter.hand_over(4)
                scatter.hand_over(5)
        scatter.start(4)
        scatter.start(5)
        for p in (0, 1, 2, 3, 6, 7):
            gather.finish(p)
        qc[...] = norm_f[...].astype(LOW)
        grad_w_in(h2_low)
        scatter.hand_over(2)
        scatter.hand_over(3)
        serve(queue, 4)
        store_cross(2, tn(x_recv[...], kc[...]))
        store_cross(3, tn(x_recv[...], vc[...]))
        scatter.hand_over(7)
        serve(queue, 3)
        grad[...] += nt(qc[...], cross_weight(0))
        store_cross(0, tn(h_low[...], qc[...]))
        store_cross(1, tn(oc[...], d_branch[...]))
        scatter.hand_over(6)
        set_small(8 + 12, column_total(qc))
        set_small(8 + 13, column_total(vc))
        serve(queue, 1)
        mask_scores(score_bias, segments[1], segments[1], True)
        self_back_a(1)
        serve(queue, 2)
        for part in range(3):
            attend_back_pairs(q, k, v, score_bias, lse, None, d_mixed, 2 * part, 2 * part + 2)
            serve(queue, 2 if part == 1 else 1)
        self_back_b(1)
        fold_start(0)
        serve(queue, 2)
        self_back_qk()
        scatter.hand_over(0)
        serve(queue, 1)
        self_back_vo()
        scatter.hand_over(1)
        serve(queue)
        scatter.start(0)
        fold_end(0)
        serve(
            plan(
                scatter, after, "6.0", "+1", "7.1", "6.1", "=2", "=3", "f1", "0.0", "1.0", "7.2", "6.2", "f2", "0.1",
                "1.1", "=7", "=6", "0.2", "f3", "1.2", "f4", "=0", "=1",
            )
        )
        for copy in cross_copies:
            copy.wait_send()
        to_encoder.wait_send()
        for p in range(8):
            scatter.finish(p)

    fold_end(5)
    for half in range(2):
        out_small[16 * half : 16 * half + 16] = small[half] + small_whole[half]
    for p in range(7):
        for half in range(2):
            out_copies(p, half).wait()
    pltpu.make_async_copy(grad, out_input.at[0, 0], out_sem.at[1]).wait()


def layer_call(tokens, segments, cotangent, attn_qk, attn_vo, cross_qk, cross_vo, ffn_in, ffn_out, gains, biases, ffn_bias):
    length, width = tokens.shape[2:]
    hidden = ffn_in.shape[2]

    def result(like, kind):
        return jax.ShapeDtypeStruct(like.shape, kind)

    def low(*shape):
        return pltpu.VMEM(shape, LOW)

    def full(*shape):
        return pltpu.VMEM(shape, jnp.float32)

    any_space = pl.BlockSpec(memory_space=pl.ANY)
    in_vmem = pl.BlockSpec(memory_space=pltpu.VMEM)
    flat, wide, exact = low(length, width), low(length, hidden), full(length, width)
    dma = pltpu.SemaphoreType.DMA
    scratch = [
        low(CHIPS, 2, 48, 2 * width), low(CHIPS, 2, 48, 2 * width), low(CHIPS, 2, 48, hidden),
        low(CHIPS, 2, 192, width), low(CHIPS, 2, 192, width),
        low(4, CHIPS, 48, 2 * width), low(4, CHIPS, 96, width),
        low(4, 2, 3, 48, 2 * width), low(4, 2, 3, 96, width),
        low(4, 2, 48, width), low(4, 2, 48, width),
        full(2, 16, width), full(5, 16, width), full(2, 16, width),
        full(8, width), full(1, width),
        flat, flat, flat, flat, flat, exact, exact, wide, wide, exact, flat, full(length, length), flat, flat,
        flat, flat, flat, low(HEADS, length, length), flat, flat, exact, flat, flat, exact,
        full(HEADS, 1, length), full(length, 128),
        flat, pltpu.VMEM(segments.shape, segments.dtype), full(*gains.shape), full(*biases.shape), full(*ffn_bias.shape),
        dma((12,)), dma((6,)), dma((6,)),
        dma((8, 2, 4)), dma((8, 2, 4)), dma((8, 9)), dma((8, 9)),
        dma((8, 2, 4)), dma((8, 2, 4)), dma((8, 8)), dma((8, 8)),
        dma((6,)), dma((6,)), dma((16,)),
    ]
    return pl.pallas_call(
        layer_kernel,
        out_shape=(
            result(tokens, LOW), result(tokens, jnp.float32),
            result(attn_qk, jnp.float32), result(attn_vo, jnp.float32),
            result(cross_qk, jnp.float32), result(cross_vo, jnp.float32),
            result(ffn_in, jnp.float32), result(ffn_out, jnp.float32),
            jax.ShapeDtypeStruct((32, width), jnp.float32),
        ),
        in_specs=[any_space] * 12,
        out_specs=(any_space,) * 8 + (in_vmem,),
        scratch_shapes=scratch,
        compiler_params=pltpu.CompilerParams(
            collective_id=0, has_side_effects=True, vmem_limit_bytes=63 * 1024 * 1024 + 524288
        ),
        name="layer_pair",
    )(
        tokens, segments, gains, biases, ffn_bias, cotangent[0],
        attn_qk, attn_vo, cross_qk, cross_vo, ffn_in, ffn_out,
    )


def hand_out_kernel(*refs):
    sources, small, rest = refs[:8], refs[8], refs[9:]
    targets, (gains, biases, ffn_bias), held, (take, give) = rest[:8], rest[8:11], rest[11:19], rest[19:]
    inward = [pltpu.make_async_copy(a, b, take.at[i]) for i, (a, b) in enumerate(zip(sources, held))]
    outward = [pltpu.make_async_copy(a, b, give.at[i]) for i, (a, b) in enumerate(zip(held, targets))]
    for copy in inward:
        copy.start()
    gains[...] = small[0:5]
    biases[...] = small[8:24]
    width = gains.shape[1]
    for row in range(8):
        ffn_bias[row // 4 : row // 4 + 1, width * (row % 4) : width * (row % 4 + 1)] = small[24 + row : 25 + row]
    for first, second in zip(inward, outward):
        first.wait()
        second.start()
    for copy in outward:
        copy.wait()


def hand_out(results, gains, biases, ffn_bias):
    any_space = pl.BlockSpec(memory_space=pl.ANY)
    in_vmem = pl.BlockSpec(memory_space=pltpu.VMEM)
    return pl.pallas_call(
        hand_out_kernel,
        out_shape=tuple(jax.ShapeDtypeStruct(r.shape, r.dtype) for r in tuple(results[:8]) + (gains, biases, ffn_bias)),
        in_specs=[any_space] * 8 + [in_vmem],
        out_specs=(any_space,) * 8 + (in_vmem,) * 3,
        scratch_shapes=[pltpu.VMEM(r.shape, r.dtype) for r in results[:8]] + [pltpu.SemaphoreType.DMA((8,))] * 2,
        compiler_params=pltpu.CompilerParams(vmem_limit_bytes=63 * 1024 * 1024),
        name="hand_out",
    )(*results)


def local_ring(
    tokens, segments, cotangent, attn_qk, attn_vo, cross_qk, cross_vo, ffn_in, ffn_out, gains, biases, ffn_bias
):
    results = layer_call(
        tokens, segments, cotangent, attn_qk, attn_vo, cross_qk, cross_vo, ffn_in, ffn_out, gains, biases, ffn_bias
    )
    return hand_out(results, gains, biases, ffn_bias)


def solution(mesh):
    any_size = mesh.shape["section"] != 2 or mesh.shape["dp"] != 2 * CHIPS
    placed = (
        P("section", "dp", None, None),
        P(None, "dp", None),
        P("dp", None, None),
        P("section", "dp", None),
        P("section", "dp", None),
        P("section", "dp", None),
        P("section", "dp", None),
        P("section", "dp", None),
        P("section", "dp", None),
        P(),
        P(),
        P(),
    )
    return jax.shard_map(
        local_any if any_size else local_ring,
        mesh=mesh,
        in_specs=placed,
        out_specs=(
            P("section", "dp", None, None),
            P("section", "dp", None, None),
            P("section", "dp", None),
            P("section", "dp", None),
            P("section", "dp", None),
            P("section", "dp", None),
            P("section", "dp", None),
            P("section", "dp", None),
            P(),
            P(),
            P(),
        ),
        check_vma=False,
    )
```
